128 devices in a mesh: dp: 16 (over z_hi, x, core), ctx: 8 (over y, z_lo).
Axes of the slice: x: 4, y: 4, z: 4 (z_hi: 2, z_lo: 2; z = z_hi * 2 + z_lo), core: 2. Of those that a mesh axis runs over, the one named last changes fastest.
Arguments:
- inputs: bfloat16 [16, 1024, 768], P('dp', 'ctx'), may hold values from -6 to 6
- positions: int32 [16, 1024], P('dp', 'ctx'), may hold values from 0 to 1023, as said below
- output_grad: bfloat16 [16, 1024, 768], P('dp', 'ctx'), may hold values from -8 to 8
- qkv_weight: float32 [768, 2304], P(('dp', 'ctx')), may hold values from -0.21875 to 0.21875
- qkv_first: float32 [768, 2304], P(('dp', 'ctx')), may hold values from -40 to 40
- qkv_second: float32 [768, 2304], P(('dp', 'ctx')), may hold values from 106.496 to 1720.32
- out_weight: float32 [768, 768], P(('dp', 'ctx')), may hold values from -1.25 to 1.25
- out_first: float32 [768, 768], P(('dp', 'ctx')), may hold values from -8 to 8
- out_second: float32 [768, 768], P(('dp', 'ctx')), may hold values from 4.25984 to 68.8128
- gate_up_weight: float32 [768, 6144], P(('dp', 'ctx')), may hold values from -0.21875 to 0.21875
- gate_up_first: float32 [768, 6144], P(('dp', 'ctx')), may hold values from -24 to 24
- gate_up_second: float32 [768, 6144], P(('dp', 'ctx')), may hold values from 38.33856 to 619.3152
- down_weight: float32 [3072, 768], P(None, ('dp', 'ctx')), may hold values from -0.109375 to 0.109375
- down_first: float32 [3072, 768], P(None, ('dp', 'ctx')), may hold values from -40 to 40
- down_second: float32 [3072, 768], P(None, ('dp', 'ctx')), may hold values from 106.496 to 1720.32
- norm_gains: float32 [2, 768], P(None, ('dp', 'ctx')), may hold values from 0.5 to 1.5
- gains_first: float32 [2, 768], P(None, ('dp', 'ctx')), may hold values from -48 to 48
- gains_second: float32 [2, 768], P(None, ('dp', 'ctx')), may hold values from 153.35423 to 2473.984
Outputs:
- outputs: bfloat16 [16, 1024, 768], P('dp', 'ctx')
- input_grad: float32 [16, 1024, 768], P('dp', 'ctx')
- new_qkv_first: float32 [768, 2304], P(('dp', 'ctx'))
- new_qkv_second: float32 [768, 2304], P(('dp', 'ctx'))
- new_qkv_weight: float32 [768, 2304], P(('dp', 'ctx'))
- new_out_first: float32 [768, 768], P(('dp', 'ctx'))
- new_out_second: float32 [768, 768], P(('dp', 'ctx'))
- new_out_weight: float32 [768, 768], P(('dp', 'ctx'))
- new_gate_up_first: float32 [768, 6144], P(('dp', 'ctx'))
- new_gate_up_second: float32 [768, 6144], P(('dp', 'ctx'))
- new_gate_up_weight: float32 [768, 6144], P(('dp', 'ctx'))
- new_down_first: float32 [3072, 768], P(None, ('dp', 'ctx'))
- new_down_second: float32 [3072, 768], P(None, ('dp', 'ctx'))
- new_down_weight: float32 [3072, 768], P(None, ('dp', 'ctx'))
- new_gains_first: float32 [2, 768], P(None, ('dp', 'ctx'))
- new_gains_second: float32 [2, 768], P(None, ('dp', 'ctx'))
- new_gains: float32 [2, 768], P(None, ('dp', 'ctx'))
The draws below stay inside these ranges and needn't reach their ends.
Inputs may be any that keep to these rules, and one draw needn't show every extreme that they name: Each row of positions is a permutation of the positions of one sequence in which every aligned block of 64 slots holds 64 consecutive positions starting at a multiple of 64.
All inputs are finite; a program needn't handle non-finite values.
Results may differ from the reference program's by a relative error of at most 0.03.
Values may be sent and summed in bfloat16 or wider, within the bound.
A program may use at most 192 MiB of HBM per device.

```python
import math
import jax
import jax.numpy as jnp
from jax import lax

D = 768
H = 12
KV = 12
HD = 64
FF = 3072
LEN = 1024
STEP = 10
SEQS = 16
SPAN = 64


def draw_positions(key, part):
    key = jax.random.fold_in(key, 7)
    blocks = LEN // SPAN
    row_keys = jax.random.split(key, SEQS)
    orders = jax.vmap(jax.random.permutation, in_axes=(0, None))(row_keys, blocks)
    slot_index = jnp.arange(LEN, dtype=jnp.int32)
    starts = jnp.take(orders, slot_index // SPAN, axis=1).astype(jnp.int32)
    return (starts * SPAN + slot_index % SPAN).astype(jnp.int32)


def with_spikes(array, stream_key, source, target, parts, factor):
    owner, partner = [(jnp.arange(array.shape[position]) // (array.shape[position] // parts)).reshape([-1 if axis == position else 1 for axis in range(array.ndim)]) for position in (source, target)]
    chosen = jax.random.permutation(stream_key, parts)[partner]
    strong = (owner == chosen) | (owner == (partner + parts // 2) % parts)
    return jnp.where(strong, factor * array, array)


def block_scale(own_key, shape, pieces, smallest, high):
    gain, own = 1.0, jax.random.fold_in(own_key, 6)
    for axis_at, parts in pieces:
        heights = jnp.exp(jax.random.uniform(jax.random.fold_in(own, axis_at), (parts,), jnp.float32, smallest / len(pieces), high / len(pieces)))
        gain = gain * jnp.repeat(heights, shape[axis_at] // parts).reshape([-1 if axis == axis_at else 1 for axis in range(len(shape))])
    return gain


def scatter_about(stream_key, extent, spread, limit, cuts=(), held_as=jnp.bfloat16):
    entries = jax.random.normal(stream_key, extent, jnp.float32) * spread
    if len(cuts) > 0:
        entries = block_scale(stream_key, extent, cuts, -0.22, 0.18) * entries
    return jnp.clip(entries, min=-limit, max=limit).astype(held_as)


def gaussian_with(own_key, shape, scale, most, shards, heavy, kind=jnp.bfloat16):
    drawn = scale * jax.random.normal(own_key, shape, jnp.float32)
    if shards:
        drawn = drawn * block_scale(own_key, shape, shards, -0.22, 0.18)
    return jnp.clip(with_spikes(drawn, jax.random.fold_in(own_key, 3), *heavy), -most, most).astype(kind)


def setup_inputs(seed: int = 0) -> dict:
    seeds = jax.random.split(jax.random.key(seed), 19)
    inputs = scatter_about(seeds[0], (SEQS, LEN, D), 1.0, 6.0, ((0, 16), (1, 8)))
    positions = draw_positions(jax.random.fold_in(seeds[18], 71), 0)
    output_grad = gaussian_with(seeds[2], (SEQS, LEN, D), 1.0, 8.0, ((0, 16), (1, 8)), (1, 2, 8, 2.0))
    qkv_weight = scatter_about(seeds[3], (D, H * HD + 2 * KV * HD), D ** -0.5, 0.21875, ((0, 128),), jnp.float32)
    qkv_first = scatter_about(seeds[4], (D, H * HD + 2 * KV * HD), (0.0555 * (SEQS * LEN) ** 0.5), 40.0, ((0, 128),), jnp.float32)
    qkv_second = jnp.clip(jnp.exp(math.log(1720.32) - 2.7821581 * jax.random.uniform(seeds[5], (D, H * HD + 2 * KV * HD), jnp.float32) ** block_scale(seeds[5], (D, H * HD + 2 * KV * HD), ((0, 128),), -0.2, 0.2)), 106.496, 1720.32)
    out_weight = scatter_about(seeds[6], (H * HD, D), (H * HD * 32 // LEN) ** -0.5, 1.25, ((0, 128),), jnp.float32)
    out_first = scatter_about(seeds[7], (H * HD, D), (0.0111 * (SEQS * LEN) ** 0.5), 8.0, ((0, 128),), jnp.float32)
    out_second = jnp.clip(jnp.exp(math.log(68.8128) - 2.7821581 * jax.random.uniform(seeds[8], (H * HD, D), jnp.float32) ** block_scale(seeds[8], (H * HD, D), ((0, 128),), -0.2, 0.2)), 4.25984, 68.8128)
    gate_up_weight = scatter_about(seeds[9], (D, 2 * FF), D ** -0.5, 0.21875, ((0, 128),), jnp.float32)
    gate_up_first = scatter_about(seeds[10], (D, 2 * FF), (0.0333 * (SEQS * LEN) ** 0.5), 24.0, ((0, 128),), jnp.float32)
    gate_up_second = jnp.clip(jnp.exp(math.log(619.3152) - 2.7821582 * jax.random.uniform(seeds[11], (D, 2 * FF), jnp.float32) ** block_scale(seeds[11], (D, 2 * FF), ((0, 128),), -0.2, 0.2)), 38.33856, 619.3152)
    down_weight = scatter_about(seeds[12], (FF, D), FF ** -0.5, 0.109375, ((1, 128),), jnp.float32)
    down_first = scatter_about(seeds[13], (FF, D), (0.0555 * (SEQS * LEN) ** 0.5), 40.0, ((1, 128),), jnp.float32)
    down_second = jnp.clip(jnp.exp(math.log(1720.32) - 2.7821581 * jax.random.uniform(seeds[14], (FF, D), jnp.float32) ** block_scale(seeds[14], (FF, D), ((1, 128),), -0.2, 0.2)), 106.496, 1720.32)
    norm_gains = jnp.clip(1.0 + 0.1 * jax.random.normal(seeds[15], (2, D), jnp.float32), 0.5, 1.5)
    gains_first = scatter_about(seeds[16], (2, D), (0.0666 * (SEQS * LEN) ** 0.5), 48.0, ((1, 128),), jnp.float32)
    gains_second = jnp.clip(jnp.exp(math.log(2473.984) - 2.7808345 * jax.random.uniform(seeds[17], (2, D), jnp.float32) ** block_scale(seeds[17], (2, D), ((1, 128),), -0.2, 0.2)), 153.35423, 2473.984)
    return {"inputs": inputs, "positions": positions, "output_grad": output_grad, "qkv_weight": qkv_weight, "qkv_first": qkv_first, "qkv_second": qkv_second, "out_weight": out_weight, "out_first": out_first, "out_second": out_second, "gate_up_weight": gate_up_weight, "gate_up_first": gate_up_first, "gate_up_second": gate_up_second, "down_weight": down_weight, "down_first": down_first, "down_second": down_second, "norm_gains": norm_gains, "gains_first": gains_first, "gains_second": gains_second}


@jax.custom_vjp
def low(v):
    return lax.optimization_barrier(v.astype(jnp.bfloat16)).astype(jnp.float32)

@jax.custom_vjp
def low_back(v):
    return v

def low_keep(v):
    return (low(v), None)

def low_pass(kept, grad):
    return (grad,)

def back_keep(v):
    return (v, None)

def back_low(kept, grad):
    return (low(grad),)
low.defvjp(low_keep, low_pass)
low_back.defvjp(back_keep, back_low)
NORM_EPS = 1e-05
ROPE_BASE = 10000.0
BETA_FIRST = 0.9
BETA_SECOND = 0.95
ADAM_EPS = 1e-08
WEIGHT_DECAY = 0.1
GAIN_RATE = 1.2
MASKED = -1e+30

def matmul(left, right):
    return jnp.dot(left, right, precision=lax.Precision.HIGHEST, preferred_element_type=jnp.float32)

def rms_norm(values, gain_row):
    inverse = lax.rsqrt(lax.optimization_barrier(jnp.mean(values * values, axis=-1, keepdims=True)) + NORM_EPS)
    return values * inverse * gain_row

def rotate(values, positions):
    half_width = values.shape[-1] // 2
    frequency = ROPE_BASE ** (-2.0 * jnp.arange(half_width, dtype=jnp.float32) / values.shape[-1])
    angles = positions.astype(jnp.float32)[:, None] * frequency[None, :]
    cosine_table = jnp.cos(angles)[:, None, :]
    sine_table = jnp.sin(angles)[:, None, :]
    front_half = values[..., :half_width]
    back_half = values[..., half_width:]
    return jnp.concatenate([front_half * cosine_table - back_half * sine_table, back_half * cosine_table + front_half * sine_table], axis=-1)

def layer_sequence(params, inputs, positions):
    qkv_weight, out_weight, gate_up_weight, down_weight, norm_gains = params
    length = inputs.shape[0]
    q_width = H * HD
    k_width = KV * HD
    groups = H // KV
    score_scale = HD ** (-0.5)
    normed = low(rms_norm(inputs, norm_gains[0]))
    projected = low_back(matmul(normed, qkv_weight))
    queries = low(rotate(projected[:, :q_width].reshape(length, H, HD), positions))
    key_heads = low(rotate(projected[:, q_width:q_width + k_width].reshape(length, KV, HD), positions))
    value_heads = low(projected[:, q_width + k_width:].reshape(length, KV, HD))
    grouped = queries.reshape(length, KV, groups, HD)
    scores = low_back(jnp.einsum('qgrd,kgd->grqk', grouped, key_heads, precision=lax.Precision.HIGHEST) * score_scale)
    allowed = positions[None, :] <= positions[:, None]
    scores = jnp.where(allowed, scores, MASKED)
    exponent = jnp.exp(scores - lax.optimization_barrier(jnp.max(scores, axis=-1, keepdims=True)))
    attn_probs = low(exponent / lax.optimization_barrier(jnp.sum(exponent, axis=-1, keepdims=True)))
    mixed_heads = jnp.einsum('grqk,kgd->qgrd', attn_probs, value_heads, precision=lax.Precision.HIGHEST)
    mixed_heads = low(low_back(mixed_heads.reshape(length, q_width)))
    attended = low_back(matmul(mixed_heads, out_weight))
    middle = inputs + attended
    normed_two = low(rms_norm(middle, norm_gains[1]))
    gate_up = low_back(matmul(normed_two, gate_up_weight))
    hidden = low(jax.nn.silu(gate_up[:, :FF]) * gate_up[:, FF:])
    return middle + matmul(hidden, down_weight)

def adam_step(master, gradient, moment_one, moment_two, rate_value, decay_value):
    moment_one = BETA_FIRST * moment_one + (1.0 - BETA_FIRST) * gradient
    moment_two = BETA_SECOND * moment_two + (1.0 - BETA_SECOND) * gradient * gradient
    first_hat = moment_one / (1.0 - BETA_FIRST ** STEP)
    second_hat = moment_two / (1.0 - BETA_SECOND ** STEP)
    updated = master - rate_value * (first_hat / (jnp.sqrt(second_hat) + ADAM_EPS) + decay_value * master)
    return (moment_one, moment_two, updated)

def reference(inputs, positions, output_grad, qkv_weight, qkv_first, qkv_second, out_weight, out_first, out_second, gate_up_weight, gate_up_first, gate_up_second, down_weight, down_first, down_second, norm_gains, gains_first, gains_second):
    params = (qkv_weight, out_weight, gate_up_weight, down_weight, norm_gains)

    def forward(values, weights):
        rounded = tuple((low(member) for member in weights))

        def sequence(element):
            return layer_sequence(rounded, element[0], element[1])
        return lax.map(jax.checkpoint(sequence), (values, positions))
    outputs, pullback = jax.vjp(forward, inputs.astype(jnp.float32), params)
    input_grad, weight_grads = pullback(output_grad.astype(jnp.float32))
    step_rates = (D ** (-0.5), (H * HD * 32 // LEN) ** (-0.5), D ** (-0.5), FF ** (-0.5), GAIN_RATE)
    decays = (WEIGHT_DECAY, WEIGHT_DECAY, WEIGHT_DECAY, WEIGHT_DECAY, 0.0)
    qkv_new = adam_step(qkv_weight, weight_grads[0], qkv_first, qkv_second, step_rates[0], decays[0])
    out_new = adam_step(out_weight, weight_grads[1], out_first, out_second, step_rates[1], decays[1])
    gate_up_new = adam_step(gate_up_weight, weight_grads[2], gate_up_first, gate_up_second, step_rates[2], decays[2])
    down_new = adam_step(down_weight, weight_grads[3], down_first, down_second, step_rates[3], decays[3])
    gains_new = adam_step(norm_gains, weight_grads[4], gains_first, gains_second, step_rates[4], decays[4])
    return (outputs.astype(jnp.bfloat16), input_grad, qkv_new[0], qkv_new[1], qkv_new[2], out_new[0], out_new[1], out_new[2], gate_up_new[0], gate_up_new[1], gate_up_new[2], down_new[0], down_new[1], down_new[2], gains_new[0], gains_new[1], gains_new[2])
```

```python
import functools

import jax
import jax.numpy as jnp
from jax import lax
from jax.experimental import pallas as pl
from jax.experimental.pallas import tpu as pltpu
from jax.sharding import PartitionSpec as P

D = 768
H = 12
HD = 64
FF = 3072
LEN = 1024
STEP = 10

NORM_EPS = 1e-05
ROPE_BASE = 10000.0
BETA_FIRST = 0.9
BETA_SECOND = 0.95
ADAM_EPS = 1e-08
WEIGHT_DECAY = 0.1
GAIN_RATE = 1.2
MASKED = -1e30

MESH = pl.DeviceIdType.MESH
bf16, f32 = jnp.bfloat16, jnp.float32

ORDERS = (("x", "y", "z"), ("y", "z", "x"), ("z", "x", "y"))
JOB_ROWS = 80


def here():
    dp, ctx = lax.axis_index("dp"), lax.axis_index("ctx")
    return dict(x=(dp // 2) % 4, y=ctx // 2, z=(dp // 8) * 2 + ctx % 2, c=dp % 2)


def low_z(at):
    return at["z"] % 2


def device(at, zl=None, **moved):
    at = dict(at, **moved)
    if zl is not None:
        at["z"] = (at["z"] // 2) * 2 + zl
    return ((at["z"] // 2) * 8 + at["x"] * 2 + at["c"], at["y"] * 2 + at["z"] % 2)


def moved(at, axis, step):
    return dict(at, **{axis: (at[axis] + step + 4) % 4})


def row_block(at):
    return (at["z"] // 2) * 8 + at["x"] * 2 + at["z"] % 2


def group_of(at):
    out = []
    me = at["c"] * 8 + at["y"] * 2 + low_z(at)
    for k in range(1, 16):
        other = (me + k) % 16
        out.append(device(at, c=other // 8, y=(other // 2) % 4, zl=other % 2))
    for k in range(4):
        for j in range(4):
            if k == 0 and j in (0, 1):
                continue
            out.append(device(moved_zlow(at, j), x=(at["x"] + k) % 4))
    return out


def moved_zlow(at, j):
    zh, zl = at["z"] // 2, at["z"] % 2
    zh = (zh + j // 2) % 2
    zl = (zl + j % 2) % 2
    return dict(at, z=zh * 2 + zl)


def signal_all(peers):
    barrier = pltpu.get_barrier_semaphore()
    for p in peers:
        pl.semaphore_signal(barrier, inc=1, device_id=p, device_id_type=MESH)


def wait_all(peers):
    pl.semaphore_wait(pltpu.get_barrier_semaphore(), len(peers))


class Net:
    def __init__(self, at, send_sem, recv_sem):
        self.at, self.send_sem, self.recv_sem = at, send_sem, recv_sem
        self.used = 0
        self.sent = []

    def take(self, count):
        base = self.used
        self.used += count
        return base

    def copy(self, src, dst, s, r, to):
        return pltpu.make_async_remote_copy(
            src_ref=src, dst_ref=dst, send_sem=self.send_sem.at[s], recv_sem=self.recv_sem.at[r],
            device_id=to, device_id_type=MESH,
        )

    def send(self, src, dst, s, r, to):
        c = self.copy(src, dst, s, r, to)
        c.start()
        self.sent.append((c, None))

    def send_or_keep(self, src, dst, s, r, to, mine):
        c = self.copy(src, dst, s, r, to)
        away = jnp.logical_not(mine)

        @pl.when(away)
        def _():
            c.start()

        @pl.when(mine)
        def _():
            pltpu.make_async_copy(src, dst, self.recv_sem.at[r]).start()

        self.sent.append((c, away))

    def arrive(self, dst, r):
        pltpu.make_async_copy(dst, dst, self.recv_sem.at[r]).wait()

    def drain(self):
        for c, away in self.sent:
            if away is None:
                c.wait_send()
            else:
                pl.when(away)(c.wait_send)
        self.sent = []


class Gather:
    def __init__(self, net, ref, job):
        self.net, self.at, self.ref, self.job = net, net.at, ref, job
        self.base = net.take(27)

    def view(self, part, at, phase):
        a1, a2, a3 = ORDERS[part]
        return self.ref.at[(self.job, part, at[a3], at[a2], at[a1])[: 5 - phase]]

    def sem(self, part, phase, kind):
        return self.base + (part * 3 + phase) * 3 + kind

    def send(self, part, phase, kind, at, axis, step):
        v, i = self.view(part, at, phase), self.sem(part, phase, kind)
        self.net.send(v, v, i, i, device(moved(self.at, axis, step)))

    def arrive(self, part, phase, kind, at):
        self.net.arrive(self.view(part, at, phase), self.sem(part, phase, kind))

    def start(self, phase):
        for part in range(3):
            axis = ORDERS[part][phase]
            self.send(part, phase, 0, self.at, axis, 1)
            self.send(part, phase, 1, self.at, axis, 3)

    def forward(self, phase):
        d = 1 - 2 * self.at["c"]
        for part in range(3):
            axis = ORDERS[part][phase]
            self.arrive(part, phase, 0, moved(self.at, axis, 3))
            self.arrive(part, phase, 1, moved(self.at, axis, 1))
            self.send(part, phase, 2, moved(self.at, axis, -d), axis, d)

    def finish(self, phase):
        for part in range(3):
            self.arrive(part, phase, 2, moved(self.at, ORDERS[part][phase], 2))


class Scatter:
    def __init__(self, net, levels, got, turned, job):
        self.net, self.at, self.job = net, net.at, job
        self.levels, self.got, self.turned = levels, got, turned
        self.base = net.take(27)

    def sem(self, part, phase, kind):
        return self.base + (part * 3 + phase) * 3 + kind

    def level(self, part, phase, i):
        return self.levels[2 - phase].at[self.job, part, i]

    def slot(self, part, phase, kind):
        return self.got[2 - phase].at[self.job, part, kind]

    def pass_on(self, part, phase):
        return self.turned[2 - phase].at[self.job, part]

    def go(self, src, part, phase, kind, axis, step):
        i = self.sem(part, phase, kind)
        self.net.send(src, self.slot(part, phase, kind), i, i, device(moved(self.at, axis, step)))

    def come(self, part, phase, kind):
        self.net.arrive(self.slot(part, phase, kind), self.sem(part, phase, kind))

    def add(self, to, refs, phase):
        blocks = 4**phase

        def one(b, carry):
            index = ()
            for k in reversed(range(phase)):
                index += ((b // 4**k) % 4,)
            total = refs[0][index].astype(f32)
            for r in refs[1:]:
                total = total + r[index].astype(f32)
            to[index] = total.astype(to.dtype)
            return carry

        if blocks == 1:
            one(0, 0)
        else:
            lax.fori_loop(0, blocks, one, 0)

    def start(self, phase):
        d = 1 - 2 * self.at["c"]
        for part in range(3):
            axis = ORDERS[part][phase]
            me = self.at[axis]
            self.go(self.level(part, phase, (me + 2) % 4), part, phase, 2, axis, 4 - d)
            self.go(self.level(part, phase, (me + d + 4) % 4), part, phase, 0, axis, d)

    def forward(self, phase):
        d = 1 - 2 * self.at["c"]
        for part in range(3):
            axis = ORDERS[part][phase]
            me = self.at[axis]
            self.come(part, phase, 2)
            to = self.pass_on(part, phase)
            self.add(to, [self.level(part, phase, (me - d + 4) % 4), self.slot(part, phase, 2)], phase)
            self.go(to, part, phase, 1, axis, 4 - d)

    def finish(self, phase):
        for part in range(3):
            axis = ORDERS[part][phase]
            me = self.at[axis]
            self.come(part, phase, 0)
            self.come(part, phase, 1)
            to = self.levels[3 - phase].at[self.job, part]
            self.add(
                to,
                [self.level(part, phase, me), self.slot(part, phase, 0), self.slot(part, phase, 1)],
                phase,
            )


def dot(a, b):
    return jnp.dot(a, b, preferred_element_type=f32)


def dot_nt(a, b):
    return lax.dot_general(a, b, (((1,), (1,)), ((), ())), preferred_element_type=f32)


def dot_tn(a, b):
    return lax.dot_general(a, b, (((0,), (0,)), ((), ())), preferred_element_type=f32)


def inverse_rms(v):
    return lax.rsqrt(jnp.mean(v * v, axis=-1, keepdims=True) + NORM_EPS)


def tables(t):
    lane = lax.broadcasted_iota(jnp.int32, t.shape, 1)
    quarter = lane // 32
    r32, r64, r96 = (pltpu.roll(t, s, 1) for s in (32, 64, 96))
    cosine = jnp.where(quarter == 0, t, jnp.where(quarter == 1, r32, jnp.where(quarter == 2, r64, r96)))
    sine = jnp.where(quarter == 0, -r96, jnp.where(quarter == 1, t, jnp.where(quarter == 2, -r32, r64)))
    return cosine, sine


def turn(v, cosine, sine):
    lane = lax.broadcasted_iota(jnp.int32, v.shape, 1)
    swapped = jnp.where(lane % 64 < 32, pltpu.roll(v, 96, 1), pltpu.roll(v, 32, 1))
    return v * cosine + swapped * sine


def turn_first_half(v, cosine, sine):
    lane = lax.broadcasted_iota(jnp.int32, v.shape, 1)
    return jnp.where(lane < 64, turn(v, cosine, sine), v)


def every_lane_position(t):
    lane = lax.broadcasted_iota(jnp.int32, t.shape, 1)
    return jnp.where(lane < 64, pltpu.roll(t, 64, 1), t)


def ffn_index(part, y, x, z):
    place = dict(x=x, y=y, z=z)
    a1, a2, a3 = ORDERS[part]
    return (part, place[a3], place[a2], place[a1])


ROWS = (
    ((0, 0, 0, 48),),
    ((0, 0, 48, 32), (32, 1, 0, 16)),
    ((0, 1, 16, 48),),
    ((0, 1, 64, 16),),
)


def put_rows(ref, place, matrix, value):
    for own, job, first, count in ROWS[matrix]:
        ref[(job,) + place + (pl.ds(first, count), slice(None))] = value[own : own + count, :]


def get_rows(ref, place, matrix):
    return [ref[(job,) + place + (pl.ds(first, count), slice(None))] for _, job, first, count in ROWS[matrix]]


def ffn_panel(wf, matrix, y):
    return jnp.concatenate(
        [
            jnp.concatenate(
                [
                    rows
                    for zh in range(2) for x in range(4) for zl in range(2)
                    for rows in get_rows(wf, ffn_index(p, y, x, zh * 2 + zl), matrix)
                ],
                axis=0,
            )
            for p in range(3)
        ],
        axis=1,
    )


def store_ffn_panel(g, matrix, y, value):
    for p in range(3):
        for zh in range(2):
            for x in range(4):
                for zl in range(2):
                    r = (zh * 8 + x * 2 + zl) * 48
                    put_rows(
                        g, ffn_index(p, y, x, zh * 2 + zl), matrix, value[r : r + 48, p * 128 : (p + 1) * 128]
                    )


def first_body(
    qkv, out, gu, dt, gains, x, t,
    wf, watt, wo, xn, tb, kv, q, lse, mixed,
    stage, pieces, recv, wide, tall, xg, kpos, mixed_t, mixed_s, send_sem, recv_sem,
):
    at = here()
    c, y, zl = at["c"], at["y"], low_z(at)
    net = Net(at, send_sem, recv_sem)
    peers = group_of(at)
    partner = device(at, c=1 - c)
    signal_all(peers)

    eye = lax.broadcasted_iota(jnp.int32, (6, 6), 0) == lax.broadcasted_iota(jnp.int32, (6, 6), 1)
    g_low = gains[...].astype(bf16).astype(f32)
    g_one = jnp.sum(jnp.where(eye, g_low[0:1, :], 0.0), axis=1, keepdims=True)
    g_two = jnp.sum(jnp.where(eye, g_low[1:2, :], 0.0), axis=1, keepdims=True)

    def put(slot, unit, v):
        stage[slot, pl.ds(unit * 6, 6), :] = v

    zero = jnp.zeros((6, 64), f32)
    for yy in range(4):
        o = yy * 192
        q_y = qkv[:, o : o + 192].astype(bf16).astype(f32) * g_one
        k_y = qkv[:, 768 + o : 768 + o + 192].astype(bf16).astype(f32) * g_one
        v_y = qkv[:, 1536 + o : 1536 + o + 192].astype(bf16).astype(f32) * g_one
        put(yy, 0, k_y[:, :128])
        put(yy, 1, jnp.concatenate([k_y[:, 128:], v_y[:, :64]], axis=1))
        put(yy, 2, v_y[:, 64:])
        put(4 + yy, 0, q_y[:, :128])
        put(4 + yy, 1, jnp.concatenate([q_y[:, 128:], zero], axis=1))
        put(4 + yy, 2, jnp.zeros((6, 128), f32))
        for cc in range(2):
            slot = cc * 4 + yy
            for cb in range(3):
                f = cc * 1536 + yy * 384 + cb * 128
                put(slot, 3 + cb, gu[:, f : f + 128].astype(bf16).astype(f32) * g_two)
                put(slot, 6 + cb, gu[:, 3072 + f : 3072 + f + 128].astype(bf16).astype(f32) * g_two)
                put(slot, 9 + cb, dt[:, f : f + 128])
            if yy < 3:
                put(slot, 12, out[:, cc * 384 + yy * 128 : cc * 384 + (yy + 1) * 128])
            else:
                put(slot, 12, jnp.zeros((6, 128), f32))
            stage[slot, pl.ds(78, 2), :] = jnp.zeros((2, 128), f32)
    pieces[...] = stage[...].astype(bf16)
    wait_all(peers)

    a_s, a_r = net.take(8), None
    a_r = a_s
    source = y * 2 + zl
    for cc in range(2):
        for yy in range(4):
            mine = jnp.logical_and(zl == c, jnp.logical_and(y == yy, c == cc))
            net.send_or_keep(
                pieces.at[cc * 4 + yy], recv.at[source], a_s + cc * 4 + yy, a_r + source,
                device(at, y=yy, zl=c, c=cc), mine,
            )
    x_s, t_s = net.take(4), net.take(4)
    for yy in range(4):
        mine = jnp.logical_and(zl == c, y == yy)
        to = device(at, y=yy, zl=c, c=zl)
        net.send_or_keep(x, xg.at[y], x_s + yy, x_s + y, to, mine)
        net.send_or_keep(t, tb.at[zl, y], t_s + yy, t_s + y, to, mine)

    for s in range(8):
        net.arrive(recv.at[s], a_r + s)
    wide[...] = recv[...].astype(f32)
    for unit in range(13):
        for s in range(8):
            tall[unit, pl.ds(s * 6, 6), :] = wide[s, pl.ds(unit * 6, 6), :]
    rb = row_block(at)
    for cb in range(3):
        watt[c, rb, :, pl.ds(cb * 128, 128)] = tall[cb].astype(bf16)
        block = ffn_index(cb, y, at["x"], at["z"])
        for m in range(3):
            put_rows(wf, block, m, tall[3 + m * 3 + cb].astype(bf16))
        put_rows(wf, block, 3, tall[12, pl.ds(cb * 16, 16), :].astype(bf16))

    w_s = net.take(16)
    w_r = net.take(16)
    others = []
    for k in range(4):
        for j in range(4):
            if k == 0 and j == 0:
                continue
            place = dict(moved_zlow(at, j), x=(at["x"] + k) % 4)
            others.append((k * 4 + j, place))
    for i, place in others:
        net.send(watt.at[c, rb], watt.at[c, rb], w_s + i, w_r + rb, device(place))
    jobs = [Gather(net, wf, job) for job in range(2)]
    for g in jobs:
        g.start(0)

    for yy in range(4):
        net.arrive(xg.at[yy], x_s + yy)
        net.arrive(tb.at[c, yy], t_s + yy)
    e_t = net.take(1)
    net.send(tb.at[c], tb.at[c], e_t, e_t, partner)
    for yy in range(4):
        v = xg[yy].astype(f32)
        xn[yy] = (v * inverse_rms(v)).astype(bf16)

    for g in jobs:
        g.forward(0)
    for _, place in others:
        r = row_block(place)
        net.arrive(watt.at[c, r], w_r + r)
    e_w = net.take(2)
    net.send(watt.at[c], watt.at[c], e_w, e_w + c, partner)
    for g in jobs:
        g.finish(0)
        g.start(1)
    net.arrive(watt.at[1 - c], e_w + 1 - c)

    w_kv = watt[0].reshape(768, 384)
    w_q = watt[1, :, :, :256].reshape(768, 256)
    for yy in range(4):
        cosine, sine = tables(tb[c, yy])
        n = xn[yy]
        kv_y = dot(n, w_kv)
        kv[c, pl.ds(yy * 128, 128), :128] = turn(kv_y[:, :128], cosine, sine).astype(bf16)
        kv[c, pl.ds(yy * 128, 128), 128:256] = turn_first_half(kv_y[:, 128:256], cosine, sine).astype(bf16)
        kv[c, pl.ds(yy * 128, 128), 256:] = kv_y[:, 256:].astype(bf16)
        q_y = dot(n, w_q)
        q[pl.ds(yy * 128, 128), :128] = (turn(q_y[:, :128], cosine, sine).astype(bf16) * 0.125).astype(bf16)
        q[pl.ds(yy * 128, 128), 128:] = (turn(q_y[:, 128:], cosine, sine).astype(bf16) * 0.125).astype(bf16)
    e_k = net.take(1)
    net.send(kv.at[c], kv.at[c], e_k, e_k, partner)
    for g in jobs:
        g.forward(1)
    net.arrive(tb.at[1 - c], e_t)
    for cc in range(2):
        for yy in range(4):
            kpos[pl.ds(cc * 512 + yy * 128, 128), :] = every_lane_position(tb[cc, yy])
    net.arrive(kv.at[1 - c], e_k)
    for g in jobs:
        g.finish(1)
        g.start(2)

    for h in range(3):
        forward_head(h, c, q, kv, tb, kpos, lse, mixed_t)
        if h == 1:
            jobs[0].forward(2)
    mix = mixed_t[...].T.astype(bf16)
    for yy in range(4):
        mixed_s[yy] = mix[yy * 128 : (yy + 1) * 128, :]
    m_s = net.take(4)
    for yy in range(4):
        mine = jnp.logical_and(y == yy, jnp.logical_and(zl == c, y // 2 == c))
        net.send_or_keep(
            mixed_s.at[yy], mixed.at[zl, y % 2], m_s + yy, m_s + zl * 2 + y % 2,
            device(at, y=yy, zl=c, c=y // 2), mine,
        )
    jobs[1].forward(2)
    for s in range(2):
        for y2 in range(2):
            net.arrive(mixed.at[s, y2], m_s + s * 2 + y2)
    for g in jobs:
        g.finish(2)
    for p in range(3):
        for yy in range(3):
            for z in range(4):
                for xx in range(4):
                    r = (xx * 2 + z % 2) * 48 + p * 16
                    wo[c, z // 2, pl.ds(r, 16), pl.ds(yy * 128, 128)] = get_rows(wf, ffn_index(p, yy, xx, z), 3)[0]
    e_o = net.take(2)
    net.send(wo.at[c], wo.at[c], e_o, e_o + c, partner)
    net.arrive(wo.at[1 - c], e_o + 1 - c)
    net.drain()


def head_parts(h, c_rows, kv):
    k = jnp.concatenate([kv[0, :, h * 64 : (h + 1) * 64], kv[1, :, h * 64 : (h + 1) * 64]], axis=0)
    o = 192 + h * 64
    v = jnp.concatenate([kv[0, :, o : o + 64], kv[1, :, o : o + 64]], axis=0)
    return k, v


def query_positions(tb, c, half):
    rows = [every_lane_position(tb[c, half * 2 + j]).T[0:1, :] for j in range(2)]
    return jnp.concatenate(rows, axis=1)


def masked_scores(k, q_part, kpos, q_row):
    s = dot_nt(k, q_part)
    kp = kpos[...]
    allowed = jnp.concatenate([kp, kp], axis=1) <= q_row
    return jnp.where(allowed, s, MASKED)


def forward_head(h, c, q, kv, tb, kpos, lse, mixed_t):
    k, v = head_parts(h, c, kv)
    for half in range(2):
        q_part = q[pl.ds(half * 256, 256), h * 64 : (h + 1) * 64]
        s = masked_scores(k, q_part, kpos, query_positions(tb, c, half))
        highest = jnp.max(s, axis=0, keepdims=True)
        e = jnp.exp(s - highest)
        total = jnp.sum(e, axis=0, keepdims=True)
        p = (e * (1.0 / total)).astype(bf16)
        mixed_t[pl.ds(h * 64, 64), pl.ds(half * 256, 256)] = dot_tn(v, p)
        lse[pl.ds(h, 1), pl.ds(half * 256, 256)] = highest + jnp.log(total)


VM = pl.BlockSpec(memory_space=pltpu.VMEM)
SEMS = 200


def call(body, collective, outs, scratch, *args, sems=SEMS):
    return pl.pallas_call(
        body,
        out_shape=tuple(jax.ShapeDtypeStruct(s, t) for s, t in outs),
        in_specs=[VM] * len(args),
        out_specs=(VM,) * len(outs),
        scratch_shapes=[pltpu.VMEM(s, t) for s, t in scratch]
        + [pltpu.SemaphoreType.DMA((sems,)), pltpu.SemaphoreType.DMA((sems,))],
        compiler_params=pltpu.CompilerParams(
            collective_id=collective, has_side_effects=True, vmem_limit_bytes=56 << 20
        ),
    )(*args)


def second_body(
    mixed, wo, wf, x, og,
    outputs, grad_middle, gm, g,
    xb, ogb, po, por, mid, n2t, ogt, acc, accr, outp, outr, gb, dwo, dwr, send_sem, recv_sem,
):
    at = here()
    c = at["c"]
    net = Net(at, send_sem, recv_sem)
    partner = device(at, c=1 - c)
    signal_all([partner])
    xb[c] = x[...]
    ogb[c] = og[...]
    wait_all([partner])

    def swap(src, dst):
        i = net.take(2)
        net.send(src, dst, i, i + 1, partner)
        return i + 1

    def swap_half(ref):
        i = net.take(1)
        net.send(ref.at[c], ref.at[c], i, i, partner)
        return i

    s_x = swap_half(xb)
    s_o = swap_half(ogb)
    mix = [mixed[:, y2].reshape(256, 192) for y2 in range(2)]
    for ch in range(2):
        po[:, pl.ds(ch * 384, 384)] = dot(mix[0], wo[ch, c, :192, :]) + dot(mix[1], wo[ch, c, 192:, :])
    s_po = swap(po, por)
    net.arrive(xb.at[1 - c], s_x)
    net.arrive(ogb.at[1 - c], s_o)
    net.arrive(por, s_po)
    middle = xb[...].reshape(256, 768).astype(f32) + (po[...] + por[...])
    r2 = inverse_rms(middle)
    mid[...] = middle
    n2 = (middle * r2).astype(bf16)
    n2t[...] = n2.T
    og2 = ogb[...].reshape(256, 768)
    ogt[...] = og2.T
    gb[...] = n2
    acc[...] = jnp.zeros_like(acc)
    outp[...] = jnp.zeros_like(outp)

    def quarter(y, carry):
        w_gate = ffn_panel(wf, 0, y)
        w_up = ffn_panel(wf, 1, y)
        w_down = ffn_panel(wf, 2, y)
        gate = dot(gb[...], w_gate)
        up = dot(gb[...], w_up)
        grad_hidden = dot(ogb[...].reshape(256, 768), w_down)
        sig = jax.nn.sigmoid(gate)
        act = gate * sig
        hidden = (act * up).astype(bf16)
        d_gate = (grad_hidden * up * (sig * (1.0 + gate * (1.0 - sig)))).astype(bf16)
        d_up = (grad_hidden * act).astype(bf16)
        outp[...] += dot_nt(hidden, w_down)
        acc[...] += dot_nt(d_gate, w_gate) + dot_nt(d_up, w_up)
        store_ffn_panel(g, 0, y, dot(n2t[...], d_gate).astype(bf16))
        store_ffn_panel(g, 1, y, dot(n2t[...], d_up).astype(bf16))
        store_ffn_panel(g, 2, y, dot(ogt[...], hidden).astype(bf16))
        return carry

    lax.fori_loop(0, 4, quarter, 0)
    s_acc = swap(acc, accr)
    s_out = net.take(2)
    net.send(outp.at[pl.ds(pl.multiple_of((1 - c) * 128, 128), 128), :], outr, s_out, s_out + 1, partner)
    net.arrive(accr, s_acc)
    middle = mid[...]
    r2 = inverse_rms(middle)
    a = acc[...] + accr[...]
    scaled = middle * r2
    gmid = ogb[...].reshape(256, 768).astype(f32) + r2 * (
        a - scaled * jnp.mean(a * scaled, axis=-1, keepdims=True)
    )
    por[...] = gmid
    grad_middle[...] = por[pl.ds(pl.multiple_of(c * 128, 128), 128), :]
    branch = gmid.astype(bf16)
    gb[...] = branch
    for ch in range(2):
        for y2 in range(2):
            dwo[ch, pl.ds(y2 * 192, 192), :] = dot_tn(mix[y2], branch[:, ch * 384 : (ch + 1) * 384]).astype(bf16)
    s_dw = swap(dwo.at[1 - c], dwr)
    for y2 in range(2):
        r = pl.ds(y2 * 192, 192)
        v = dot_nt(branch[:, :384], wo[0, c, r, :]) + dot_nt(branch[:, 384:], wo[1, c, r, :])
        for s in range(2):
            gm[y2, s] = v[s * 128 : (s + 1) * 128, :].astype(bf16)
    net.arrive(outr, s_out + 1)
    own = pl.ds(pl.multiple_of(c * 128, 128), 128)
    outputs[...] = (mid[own, :] + (outp[own, :] + outr[...])).astype(bf16)
    net.arrive(dwr, s_dw)
    for p in range(3):
        for yy in range(4):
            for xx in range(4):
                for zl in range(2):
                    r = (xx * 2 + zl) * 48 + p * 16
                    own_place, their_place = (ffn_index(p, yy, xx, h * 2 + zl) for h in (c, 1 - c))
                    if yy < 3:
                        put_rows(g, own_place, 3, dwo[c, pl.ds(r, 16), pl.ds(yy * 128, 128)])
                        put_rows(g, their_place, 3, dwr[pl.ds(r, 16), pl.ds(yy * 128, 128)])
                    else:
                        put_rows(g, own_place, 3, jnp.zeros((16, 128), bf16))
                        put_rows(g, their_place, 3, jnp.zeros((16, 128), bf16))
    net.drain()


def third_body(
    gm, g, watt, xn, tb, kv, q, lse, x, grad_middle,
    input_grad, grads,
    go, kpos, dkv, dkv_s, dkv_r, dq_t, dp_kv, dp_q, dw, dw_r, dw_sum, plane, a_s, a_r, tall, stage, pieces, back,
    got3, got2, got1, on3, on2, on1, lev2, lev1, lev0, send_sem, recv_sem,
):
    at = here()
    c, y, zl = at["c"], at["y"], low_z(at)
    net = Net(at, send_sem, recv_sem)
    peers = group_of(at)
    partner = device(at, c=1 - c)
    signal_all(peers)
    for cc in range(2):
        for yy in range(4):
            kpos[pl.ds(cc * 512 + yy * 128, 128), :] = every_lane_position(tb[cc, yy])
    dkv[...] = jnp.zeros_like(dkv)
    wait_all(peers)

    s_g = net.take(4)
    s_gr = net.take(4)
    for y2 in range(2):
        for s in range(2):
            mine = jnp.logical_and(c * 2 + y2 == y, jnp.logical_and(zl == s, zl == c))
            net.send_or_keep(
                gm.at[y2, s], go.at[y], s_g + y2 * 2 + s, s_gr + y, device(at, y=c * 2 + y2, zl=s, c=zl), mine
            )
    levels, got, on = (g, lev2, lev1, lev0), (got3, got2, got1), (on3, on2, on1)
    jobs = [Scatter(net, levels, got, on, job) for job in range(2)]
    for j in jobs:
        j.start(2)
    for yy in range(4):
        net.arrive(go.at[yy], s_gr + yy)

    for h in range(3):
        backward_head(h, c, q, kv, tb, kpos, lse, go, dkv, dq_t)
        if h == 0:
            jobs[0].forward(2)
            jobs[1].forward(2)
    dkv_s[...] = dkv[1 - c].astype(bf16)
    s_k = net.take(1)
    net.send(dkv_s, dkv_r, s_k, s_k, partner)
    dq = dq_t[...].T * 0.125
    for yy in range(4):
        cosine, sine = tables(tb[c, yy])
        r = pl.ds(yy * 128, 128)
        d = dq[yy * 128 : (yy + 1) * 128, :]
        dp_q[r, :128] = turn(d[:, :128], cosine, -sine).astype(bf16)
        dp_q[r, 128:] = turn(d[:, 128:], cosine, -sine).astype(bf16)
    jobs[0].finish(2)
    jobs[0].start(1)
    net.arrive(dkv_r, s_k)
    for yy in range(4):
        cosine, sine = tables(tb[c, yy])
        r = pl.ds(yy * 128, 128)
        d = dkv[c, r, :] + dkv_r[r, :].astype(f32)
        dp_kv[r, :128] = turn(d[:, :128], cosine, -sine).astype(bf16)
        dp_kv[r, 128:256] = turn_first_half(d[:, 128:256], cosine, -sine).astype(bf16)
        dp_kv[r, 256:] = d[:, 256:].astype(bf16)
    tokens = xn[...].reshape(512, 768)
    dw[0] = dot_tn(tokens, dp_kv[...]).astype(bf16).reshape(16, 48, 384)
    dw[1, :, :, :256] = dot_tn(tokens, dp_q[...]).astype(bf16).reshape(16, 48, 256)
    dw[1, :, :, 256:] = jnp.zeros((16, 48, 128), bf16)
    s_w = net.take(1)
    net.send(dw.at[1 - c], dw_r, s_w, s_w, partner)
    jobs[1].finish(2)
    jobs[1].start(1)
    a_kv = dot_nt(dp_kv[...], watt[0].reshape(768, 384))
    a_q = dot_nt(dp_q[...], watt[1, :, :, :256].reshape(768, 256))
    a_s[...] = (a_kv + a_q).astype(bf16).reshape(4, 128, 768)
    net.arrive(dw_r, s_w)
    dw_sum[...] = (dw[c].astype(f32) + dw_r[...].astype(f32)).astype(bf16)
    s_p, s_pr = net.take(16), net.take(16)
    rb = row_block(at)
    others = []
    for k in range(4):
        for j in range(4):
            if k == 0 and j == 0:
                continue
            others.append((k * 4 + j, dict(moved_zlow(at, j), x=(at["x"] + k) % 4)))
    for i, place in others:
        net.send(dw_sum.at[row_block(place)], plane.at[rb], s_p + i, s_pr + rb, device(place))
    s_a, s_ar = net.take(4), net.take(4)
    for yy in range(4):
        mine = jnp.logical_and(y == yy, zl == c)
        net.send_or_keep(a_s.at[yy], a_r.at[y], s_a + yy, s_ar + y, device(at, y=yy, zl=c, c=zl), mine)
    for j in jobs:
        j.forward(1)
    for j in jobs:
        j.finish(1)
        j.start(0)
    for yy in range(4):
        net.arrive(a_r.at[yy], s_ar + yy)
    v = x[...].astype(f32)
    r1 = inverse_rms(v)
    scaled = v * r1
    a = (a_r[0].astype(f32) + a_r[1].astype(f32)) + (a_r[2].astype(f32) + a_r[3].astype(f32))
    input_grad[...] = grad_middle[...] + r1 * (a - scaled * jnp.mean(a * scaled, axis=-1, keepdims=True))
    for j in jobs:
        j.forward(0)
    total = dw_sum[rb].astype(f32)
    for _, place in others:
        r = row_block(place)
        net.arrive(plane.at[r], s_pr + r)
        total = total + plane[r].astype(f32)
    for cb in range(3):
        tall[cb] = total[:, cb * 128 : (cb + 1) * 128]
    for j in jobs:
        j.finish(0)
    for cb in range(3):
        for m in range(3):
            for own, job, first, count in ROWS[m]:
                tall[3 + m * 3 + cb, pl.ds(own, count), :] = lev0[job, cb, pl.ds(first, count), :].astype(f32)
        tall[12, pl.ds(cb * 16, 16), :] = lev0[1, cb, pl.ds(64, 16), :].astype(f32)
    for s in range(8):
        for unit in range(13):
            stage[s, pl.ds(unit * 6, 6), :] = tall[unit, pl.ds(s * 6, 6), :]
        stage[s, pl.ds(78, 2), :] = jnp.zeros((2, 128), f32)
    pieces[...] = stage[...].astype(bf16)
    s_b, s_br = net.take(8), net.take(8)
    slot = c * 4 + y
    for s in range(8):
        mine = jnp.logical_and(y * 2 + zl == s, zl == c)
        net.send_or_keep(
            pieces.at[s], back.at[slot], s_b + s, s_br + slot, device(at, y=s // 2, zl=s % 2, c=zl), mine
        )
    for s in range(8):
        net.arrive(back.at[s], s_br + s)
    grads[...] = back[...].astype(f32)
    net.drain()


def backward_head(h, c, q, kv, tb, kpos, lse, go, dkv, dq_t):
    k, v = head_parts(h, c, kv)
    for half in range(2):
        rows = pl.ds(half * 256, 256)
        q_part = q[rows, h * 64 : (h + 1) * 64]
        g_part = go[pl.ds(half * 2, 2), :, h * 64 : (h + 1) * 64].reshape(256, 64)
        s = masked_scores(k, q_part, kpos, query_positions(tb, c, half))
        p = jnp.exp(s - lse[pl.ds(h, 1), rows])
        dp = dot_nt(v, g_part)
        centre = jnp.sum(p * dp, axis=0, keepdims=True)
        ds = (p * (dp - centre)).astype(bf16)
        dv = dot(p.astype(bf16), g_part)
        dk = dot(ds, q_part)
        dq_t[pl.ds(h * 64, 64), rows] = dot_tn(k, ds)
        for cc in range(2):
            dkv[cc, :, h * 64 : (h + 1) * 64] += dk[cc * 512 : (cc + 1) * 512]
            dkv[cc, :, 192 + h * 64 : 192 + (h + 1) * 64] += dv[cc * 512 : (cc + 1) * 512]


def adam_step(master, gradient, moment_one, moment_two, rate_value, decay_value):
    moment_one = BETA_FIRST * moment_one + (1.0 - BETA_FIRST) * gradient
    moment_two = BETA_SECOND * moment_two + (1.0 - BETA_SECOND) * gradient * gradient
    first_hat = moment_one / (1.0 - BETA_FIRST**STEP)
    second_hat = moment_two / (1.0 - BETA_SECOND**STEP)
    updated = master - rate_value * (
        first_hat / (jnp.sqrt(second_hat) + ADAM_EPS) + decay_value * master
    )
    return (moment_one, moment_two, updated)


def position_table(positions):
    half = HD // 2
    frequency = ROPE_BASE ** (-2.0 * jnp.arange(half, dtype=f32) / HD)
    place = positions.reshape(128, 1).astype(f32)
    angles = place * frequency[None, :]
    return jnp.concatenate([jnp.cos(angles), jnp.sin(angles), jnp.broadcast_to(place, (128, 64))], axis=1)


def body(
    inputs, positions, output_grad,
    qkv_weight, qkv_first, qkv_second, out_weight, out_first, out_second,
    gate_up_weight, gate_up_first, gate_up_second, down_weight, down_first, down_second,
    norm_gains, gains_first, gains_second,
):
    x = inputs.reshape(128, D)
    og = output_grad.reshape(128, D)
    table = position_table(positions)
    wf_shape = (2, 3, 4, 4, 4, JOB_ROWS, 128)
    wf, watt, wo, xn, tb, kv, q, lse, mixed = call(
        first_body, 0,
        [
            (wf_shape, bf16), ((2, 16, 48, 384), bf16), ((2, 2, 384, 384), bf16), ((4, 128, 768), bf16),
            ((2, 4, 128, 128), f32), ((2, 512, 384), bf16), ((512, 256), bf16), ((8, 512), f32),
            ((2, 2, 128, 192), bf16),
        ],
        [
            ((8, 80, 128), f32), ((8, 80, 128), bf16), ((8, 80, 128), bf16), ((8, 80, 128), f32),
            ((13, 48, 128), f32), ((4, 128, 768), bf16), ((1024, 128), f32), ((192, 512), f32),
            ((4, 128, 192), bf16),
        ],
        qkv_weight, out_weight, gate_up_weight, down_weight.T, norm_gains, x, table,
    )
    outputs, grad_middle, gm, g = call(
        second_body, 1,
        [((128, 768), bf16), ((128, 768), f32), ((2, 2, 128, 192), bf16), (wf_shape, bf16)],
        [
            ((2, 128, 768), bf16), ((2, 128, 768), bf16), ((256, 768), f32), ((256, 768), f32), ((256, 768), f32),
            ((768, 256), bf16), ((768, 256), bf16), ((256, 768), f32), ((256, 768), f32),
            ((256, 768), f32), ((128, 768), f32), ((256, 768), bf16), ((2, 384, 384), bf16), ((384, 384), bf16),
        ],
        mixed, wo, wf, x, og,
    )
    input_grad, grads = call(
        third_body, 2,
        [((128, 768), f32), ((8, 80, 128), f32)],
        [
            ((4, 128, 192), bf16), ((1024, 128), f32), ((2, 512, 384), f32), ((512, 384), bf16), ((512, 384), bf16),
            ((256, 512), f32), ((512, 384), bf16), ((512, 256), bf16), ((2, 16, 48, 384), bf16), ((16, 48, 384), bf16),
            ((16, 48, 384), bf16), ((16, 48, 384), bf16), ((4, 128, 768), bf16), ((4, 128, 768), bf16),
            ((13, 48, 128), f32), ((8, 80, 128), f32), ((8, 80, 128), bf16), ((8, 80, 128), bf16),
            *[((2, 3, 3) + (4,) * k + (JOB_ROWS, 128), bf16) for k in (2, 1, 0)],
            *[((2, 3) + (4,) * k + (JOB_ROWS, 128), bf16) for k in (2, 1, 0)],
            *[((2, 3) + (4,) * k + (JOB_ROWS, 128), bf16) for k in (2, 1, 0)],
        ],
        gm, g, watt, xn, tb, kv, q, lse, x, grad_middle,
    )
    units = grads[:, :78].reshape(2, 4, 13, 6, 128)

    def wide(first):
        v = units[:, :, first : first + 3]
        return v.transpose(3, 0, 1, 2, 4)

    att = wide(0).reshape(6, 2, 4, 384)
    d_k, d_v = att[:, 0, :, :192].reshape(6, 768), att[:, 0, :, 192:].reshape(6, 768)
    d_q = att[:, 1, :, :192].reshape(6, 768)
    d_qkv = jnp.concatenate([d_q, d_k, d_v], axis=1)
    d_gate_up = jnp.concatenate([wide(3).reshape(6, 3072), wide(6).reshape(6, 3072)], axis=1)
    d_down = wide(9).reshape(6, 3072).T
    d_out = units[:, :3, 12].transpose(2, 0, 1, 3).reshape(6, 768)

    def low(v):
        return v.astype(bf16).astype(f32)

    gains_low = low(norm_gains)
    d_gains = jnp.stack(
        [jnp.sum(low(qkv_weight) * d_qkv, axis=1), jnp.sum(low(gate_up_weight) * d_gate_up, axis=1)]
    )
    d_qkv = d_qkv * gains_low[0][:, None]
    d_gate_up = d_gate_up * gains_low[1][:, None]
    qkv_new = adam_step(qkv_weight, d_qkv, qkv_first, qkv_second, D ** (-0.5), WEIGHT_DECAY)
    out_new = adam_step(
        out_weight, d_out, out_first, out_second, (H * HD * 32 // LEN) ** (-0.5), WEIGHT_DECAY
    )
    gate_up_new = adam_step(
        gate_up_weight, d_gate_up, gate_up_first, gate_up_second, D ** (-0.5), WEIGHT_DECAY
    )
    down_new = adam_step(down_weight, d_down, down_first, down_second, FF ** (-0.5), WEIGHT_DECAY)
    gains_new = adam_step(norm_gains, d_gains, gains_first, gains_second, GAIN_RATE, 0.0)
    return (
        outputs.reshape(1, 128, D), input_grad.reshape(1, 128, D),
        *qkv_new, *out_new, *gate_up_new, *down_new, *gains_new,
    )


def solution(mesh):
    token = P("dp", "ctx", None)
    rows, columns = P(("dp", "ctx"), None), P(None, ("dp", "ctx"))
    return jax.shard_map(
        body,
        mesh=mesh,
        in_specs=(token, P("dp", "ctx"), token) + (rows,) * 9 + (columns,) * 6,
        out_specs=(token, token) + (rows,) * 9 + (columns,) * 6,
        check_vma=False,
    )
```

```python
import functools

import jax
import jax.numpy as jnp
from jax import lax
from jax.experimental import pallas as pl
from jax.experimental.pallas import tpu as pltpu
from jax.sharding import PartitionSpec as P

D = 768
H = 12
HD = 64
FF = 3072
LEN = 1024
STEP = 10

NORM_EPS = 1e-05
ROPE_BASE = 10000.0
BETA_FIRST = 0.9
BETA_SECOND = 0.95
ADAM_EPS = 1e-08
WEIGHT_DECAY = 0.1
GAIN_RATE = 1.2
MASKED = -1e30

MESH = pl.DeviceIdType.MESH
bf16, f32 = jnp.bfloat16, jnp.float32

ORDERS = (("x", "y", "z"), ("y", "z", "x"), ("z", "x", "y"))
JOB_ROWS = 80


def here():
    dp, ctx = lax.axis_index("dp"), lax.axis_index("ctx")
    return dict(x=(dp // 2) % 4, y=ctx // 2, z=(dp // 8) * 2 + ctx % 2, c=dp % 2)


def low_z(at):
    return at["z"] % 2


def device(at, zl=None, **moved):
    at = dict(at, **moved)
    if zl is not None:
        at["z"] = (at["z"] // 2) * 2 + zl
    return ((at["z"] // 2) * 8 + at["x"] * 2 + at["c"], at["y"] * 2 + at["z"] % 2)


def moved(at, axis, step):
    return dict(at, **{axis: (at[axis] + step + 4) % 4})


def row_block(at):
    return (at["z"] // 2) * 8 + at["x"] * 2 + at["z"] % 2


def group_of(at):
    out = []
    me = at["c"] * 8 + at["y"] * 2 + low_z(at)
    for k in range(1, 16):
        other = (me + k) % 16
        out.append(device(at, c=other // 8, y=(other // 2) % 4, zl=other % 2))
    for k in range(4):
        for j in range(4):
            if k == 0 and j in (0, 1):
                continue
            out.append(device(moved_zlow(at, j), x=(at["x"] + k) % 4))
    return out


def moved_zlow(at, j):
    zh, zl = at["z"] // 2, at["z"] % 2
    zh = (zh + j // 2) % 2
    zl = (zl + j % 2) % 2
    return dict(at, z=zh * 2 + zl)


def signal_all(peers):
    barrier = pltpu.get_barrier_semaphore()
    for p in peers:
        pl.semaphore_signal(barrier, inc=1, device_id=p, device_id_type=MESH)


def wait_all(peers):
    pl.semaphore_wait(pltpu.get_barrier_semaphore(), len(peers))


class Net:
    def __init__(self, at, send_sem, recv_sem):
        self.at, self.send_sem, self.recv_sem = at, send_sem, recv_sem
        self.used = 0
        self.sent = []

    def take(self, count):
        base = self.used
        self.used += count
        return base

    def copy(self, src, dst, s, r, to):
        return pltpu.make_async_remote_copy(
            src_ref=src, dst_ref=dst, send_sem=self.send_sem.at[s], recv_sem=self.recv_sem.at[r],
            device_id=to, device_id_type=MESH,
        )

    def send(self, src, dst, s, r, to):
        c = self.copy(src, dst, s, r, to)
        c.start()
        self.sent.append((c, None))

    def send_or_keep(self, src, dst, s, r, to, mine):
        c = self.copy(src, dst, s, r, to)
        away = jnp.logical_not(mine)

        @pl.when(away)
        def _():
            c.start()

        @pl.when(mine)
        def _():
            pltpu.make_async_copy(src, dst, self.recv_sem.at[r]).start()

        self.sent.append((c, away))

    def arrive(self, dst, r):
        pltpu.make_async_copy(dst, dst, self.recv_sem.at[r]).wait()

    def drain(self):
        for c, away in self.sent:
            if away is None:
                c.wait_send()
            else:
                pl.when(away)(c.wait_send)
        self.sent = []


class Gather:
    def __init__(self, net, ref, job):
        self.net, self.at, self.ref, self.job = net, net.at, ref, job
        self.base = net.take(27)

    def view(self, part, at, phase):
        a1, a2, a3 = ORDERS[part]
        return self.ref.at[(self.job, part, at[a3], at[a2], at[a1])[: 5 - phase]]

    def sem(self, part, phase, kind):
        return self.base + (part * 3 + phase) * 3 + kind

    def send(self, part, phase, kind, at, axis, step):
        v, i = self.view(part, at, phase), self.sem(part, phase, kind)
        self.net.send(v, v, i, i, device(moved(self.at, axis, step)))

    def arrive(self, part, phase, kind, at):
        self.net.arrive(self.view(part, at, phase), self.sem(part, phase, kind))

    def start(self, phase):
        for part in range(3):
            axis = ORDERS[part][phase]
            self.send(part, phase, 0, self.at, axis, 1)
            self.send(part, phase, 1, self.at, axis, 3)

    def forward(self, phase):
        d = 1 - 2 * self.at["c"]
        for part in range(3):
            axis = ORDERS[part][phase]
            self.arrive(part, phase, 0, moved(self.at, axis, 3))
            self.arrive(part, phase, 1, moved(self.at, axis, 1))
            self.send(part, phase, 2, moved(self.at, axis, -d), axis, d)

    def finish(self, phase):
        for part in range(3):
            self.arrive(part, phase, 2, moved(self.at, ORDERS[part][phase], 2))


class Scatter:
    def __init__(self, net, levels, got, turned, job):
        self.net, self.at, self.job = net, net.at, job
        self.levels, self.got, self.turned = levels, got, turned
        self.base = net.take(27)

    def sem(self, part, phase, kind):
        return self.base + (part * 3 + phase) * 3 + kind

    def level(self, part, phase, i):
        return self.levels[2 - phase].at[self.job, part, i]

    def slot(self, part, phase, kind):
        return self.got[2 - phase].at[self.job, part, kind]

    def pass_on(self, part, phase):
        return self.turned[2 - phase].at[self.job, part]

    def go(self, src, part, phase, kind, axis, step):
        i = self.sem(part, phase, kind)
        self.net.send(src, self.slot(part, phase, kind), i, i, device(moved(self.at, axis, step)))

    def come(self, part, phase, kind):
        self.net.arrive(self.slot(part, phase, kind), self.sem(part, phase, kind))

    def add(self, to, refs, phase):
        blocks = 4**phase

        def one(b, carry):
            index = ()
            for k in reversed(range(phase)):
                index += ((b // 4**k) % 4,)
            total = refs[0][index].astype(f32)
            for r in refs[1:]:
                total = total + r[index].astype(f32)
            to[index] = total.astype(to.dtype)
            return carry

        if blocks == 1:
            one(0, 0)
        else:
            lax.fori_loop(0, blocks, one, 0)

    def start(self, phase):
        d = 1 - 2 * self.at["c"]
        for part in range(3):
            axis = ORDERS[part][phase]
            me = self.at[axis]
            self.go(self.level(part, phase, (me + 2) % 4), part, phase, 2, axis, 4 - d)
            self.go(self.level(part, phase, (me + d + 4) % 4), part, phase, 0, axis, d)

    def forward(self, phase):
        d = 1 - 2 * self.at["c"]
        for part in range(3):
            axis = ORDERS[part][phase]
            me = self.at[axis]
            self.come(part, phase, 2)
            to = self.pass_on(part, phase)
            self.add(to, [self.level(part, phase, (me - d + 4) % 4), self.slot(part, phase, 2)], phase)
            self.go(to, part, phase, 1, axis, 4 - d)

    def finish(self, phase):
        for part in range(3):
            axis = ORDERS[part][phase]
            me = self.at[axis]
            self.come(part, phase, 0)
            self.come(part, phase, 1)
            to = self.levels[3 - phase].at[self.job, part]
            self.add(
                to,
                [self.level(part, phase, me), self.slot(part, phase, 0), self.slot(part, phase, 1)],
                phase,
            )


def dot(a, b):
    return jnp.dot(a, b, preferred_element_type=f32)


def dot_nt(a, b):
    return lax.dot_general(a, b, (((1,), (1,)), ((), ())), preferred_element_type=f32)


def dot_tn(a, b):
    return lax.dot_general(a, b, (((0,), (0,)), ((), ())), preferred_element_type=f32)


def inverse_rms(v):
    return lax.rsqrt(jnp.mean(v * v, axis=-1, keepdims=True) + NORM_EPS)


def tables(place, freq):
    angle = place * freq
    lane = lax.broadcasted_iota(jnp.int32, place.shape, 1)
    sine = jnp.sin(angle)
    return jnp.cos(angle), jnp.where(lane % 64 < 32, -sine, sine)


def turn(v, cosine, sine):
    lane = lax.broadcasted_iota(jnp.int32, v.shape, 1)
    swapped = jnp.where(lane % 64 < 32, pltpu.roll(v, 96, 1), pltpu.roll(v, 32, 1))
    return v * cosine + swapped * sine


def turn_first_half(v, cosine, sine):
    lane = lax.broadcasted_iota(jnp.int32, v.shape, 1)
    return jnp.where(lane < 64, turn(v, cosine, sine), v)


def ffn_index(part, y, x, z):
    place = dict(x=x, y=y, z=z)
    a1, a2, a3 = ORDERS[part]
    return (part, place[a3], place[a2], place[a1])


WEIGHT_ROWS = (
    ((0, 0, 16, 48),),
    ((0, 0, 64, 16), (16, 1, 0, 32)),
    ((0, 1, 32, 48),),
    ((0, 0, 0, 16),),
)
GRAD_ROWS = (
    ((0, 0, 0, 48),),
    ((0, 0, 48, 32), (32, 1, 0, 16)),
    ((0, 1, 16, 48),),
    ((0, 1, 64, 16),),
)


def put_rows(ref, place, rows, value):
    for own, job, first, count in rows:
        ref[(job,) + place + (pl.ds(first, count), slice(None))] = value[own : own + count, :]


def get_rows(ref, place, rows):
    return [ref[(job,) + place + (pl.ds(first, count), slice(None))] for _, job, first, count in rows]


def ffn_panel(wf, matrix, y):
    return jnp.concatenate(
        [
            jnp.concatenate(
                [
                    rows
                    for zh in range(2) for x in range(4) for zl in range(2)
                    for rows in get_rows(wf, ffn_index(p, y, x, zh * 2 + zl), WEIGHT_ROWS[matrix])
                ],
                axis=0,
            )
            for p in range(3)
        ],
        axis=1,
    )


def store_ffn_panel(g, matrix, y, value):
    for p in range(3):
        for zh in range(2):
            for x in range(4):
                for zl in range(2):
                    r = (zh * 8 + x * 2 + zl) * 48
                    put_rows(
                        g, ffn_index(p, y, x, zh * 2 + zl), GRAD_ROWS[matrix], value[r : r + 48, p * 128 : (p + 1) * 128]
                    )


def head_parts(h, kv):
    k = jnp.concatenate([kv[0, :, h * 64 : (h + 1) * 64], kv[1, :, h * 64 : (h + 1) * 64]], axis=0)
    o = 192 + h * 64
    v = jnp.concatenate([kv[0, :, o : o + 64], kv[1, :, o : o + 64]], axis=0)
    return k, v


def query_positions(qpos, half):
    return jnp.concatenate([qpos[half * 2], qpos[half * 2 + 1]], axis=1)[0:1, :]


def masked_scores(k, q_part, kpos, q_row):
    s = dot_nt(k, q_part)
    kp = kpos[...].reshape(1024, 128)
    allowed = jnp.concatenate([kp, kp], axis=1) <= q_row
    return jnp.where(allowed, s, MASKED)


def forward_head(h, q, kv, qpos, kpos, lse, mixed_t):
    k, v = head_parts(h, kv)
    for half in range(2):
        q_part = q[pl.ds(half * 256, 256), h * 64 : (h + 1) * 64]
        s = masked_scores(k, q_part, kpos, query_positions(qpos, half))
        highest = jnp.max(s, axis=0, keepdims=True)
        e = jnp.exp(s - highest)
        total = jnp.sum(e, axis=0, keepdims=True)
        p = (e * (1.0 / total)).astype(bf16)
        mixed_t[pl.ds(h * 64, 64), pl.ds(half * 256, 256)] = dot_tn(v, p)
        lse[pl.ds(h, 1), pl.ds(half * 256, 256)] = highest + jnp.log(total)


def backward_head(h, q, kv, qpos, kpos, lse, go, dkv, dq_t):
    k, v = head_parts(h, kv)
    for half in range(2):
        rows = pl.ds(half * 256, 256)
        q_part = q[rows, h * 64 : (h + 1) * 64]
        g_part = go[pl.ds(half * 2, 2), :, h * 64 : (h + 1) * 64].reshape(256, 64)
        s = masked_scores(k, q_part, kpos, query_positions(qpos, half))
        p = jnp.exp(s - lse[pl.ds(h, 1), rows])
        dp = dot_nt(v, g_part)
        centre = jnp.sum(p * dp, axis=0, keepdims=True)
        ds = (p * (dp - centre)).astype(bf16)
        dv = dot(p.astype(bf16), g_part)
        dk = dot(ds, q_part)
        dq_t[pl.ds(h * 64, 64), rows] = dot_tn(k, ds)
        for cc in range(2):
            dkv[cc, :, h * 64 : (h + 1) * 64] += dk[cc * 512 : (cc + 1) * 512]
            dkv[cc, :, 192 + h * 64 : 192 + (h + 1) * 64] += dv[cc * 512 : (cc + 1) * 512]


def plane_others(at):
    out = []
    for k in range(4):
        for j in range(4):
            if k or j:
                out.append((k * 4 + j, dict(moved_zlow(at, j), x=(at["x"] + k) % 4)))
    return out


def cut_for_group(qkv, out, gu, dt, gains, positions, stage):
    eye = lax.broadcasted_iota(jnp.int32, (6, 6), 0) == lax.broadcasted_iota(jnp.int32, (6, 6), 1)
    g_low = gains[...].astype(bf16).astype(f32)
    g_one = jnp.sum(jnp.where(eye, g_low[0:1, :], 0.0), axis=1, keepdims=True)
    g_two = jnp.sum(jnp.where(eye, g_low[1:2, :], 0.0), axis=1, keepdims=True)
    place = positions[...]
    place = jnp.concatenate([(place // 64).astype(f32), (place % 64).astype(f32)], axis=0)

    def put(slot, unit, v):
        stage[slot, pl.ds(unit * 6, 6), :] = v

    zero = jnp.zeros((6, 64), f32)
    for yy in range(4):
        o = yy * 192
        q_y = qkv[:, o : o + 192].astype(bf16).astype(f32) * g_one
        k_y = qkv[:, 768 + o : 768 + o + 192].astype(bf16).astype(f32) * g_one
        v_y = qkv[:, 1536 + o : 1536 + o + 192].astype(bf16).astype(f32) * g_one
        put(yy, 0, k_y[:, :128])
        put(yy, 1, jnp.concatenate([k_y[:, 128:], v_y[:, :64]], axis=1))
        put(yy, 2, v_y[:, 64:])
        put(4 + yy, 0, q_y[:, :128])
        put(4 + yy, 1, jnp.concatenate([q_y[:, 128:], zero], axis=1))
        put(4 + yy, 2, jnp.zeros((6, 128), f32))
        for cc in range(2):
            slot = cc * 4 + yy
            for cb in range(3):
                f = cc * 1536 + yy * 384 + cb * 128
                put(slot, 3 + cb, gu[:, f : f + 128].astype(bf16).astype(f32) * g_two)
                put(slot, 6 + cb, gu[:, 3072 + f : 3072 + f + 128].astype(bf16).astype(f32) * g_two)
                put(slot, 9 + cb, dt[:, f : f + 128])
            if yy < 3:
                put(slot, 12, out[:, cc * 384 + yy * 128 : cc * 384 + (yy + 1) * 128])
            else:
                put(slot, 12, jnp.zeros((6, 128), f32))
            stage[slot, pl.ds(78, 2), :] = place


def layer_body(
    qkv, out, gu, dt, gains, x, og, positions, freq,
    outputs, input_grad, grads,
    stage, pieces, recv, wide, tall, watt, wf, wo, x_in, xg, xn, xnt, cosine, sine, kpos, qpos, kv, q, lse,
    mixed_t, mixed_s, mixed,
    xb, ogb, po, por, mid, n2, n2t, ogt, acc, accr, outp, outr, branch, dwo, dwr, gm, g,
    go, dkv, dkv_s, dkv_r, dq_t, dp, dw, dw_r, dw_sum, plane, a_s, a_got, a_on, a_sum, a_own, back_s, back_p, back,
    got3, got2, got1, on3, on2, on1, lev2, lev1, lev0, send_sem, recv_sem,
):
    at = here()
    c, y, zl = at["c"], at["y"], low_z(at)
    d = 1 - 2 * c
    net = Net(at, send_sem, recv_sem)
    peers = group_of(at)
    partner = device(at, c=1 - c)
    column = [device(at, y=(y + k) % 4) for k in range(4)]
    rb = row_block(at)
    own_rows = pl.ds(pl.multiple_of(c * 128, 128), 128)
    their_rows = pl.ds(pl.multiple_of((1 - c) * 128, 128), 128)

    def swap(src, dst):
        i = net.take(1)
        net.send(src, dst, i, i, partner)
        return i

    signal_all(peers)
    cut_for_group(qkv, out, gu, dt, gains, positions, stage)
    pieces[...] = stage[...].astype(bf16)
    xb[c] = x[...]
    ogb[c] = og[...]
    wait_all(peers)

    a_r = net.take(8)
    source = y * 2 + zl
    for cc in range(2):
        for yy in range(4):
            mine = jnp.logical_and(zl == c, jnp.logical_and(y == yy, c == cc))
            net.send_or_keep(
                pieces.at[cc * 4 + yy], recv.at[source], a_r + cc * 4 + yy, a_r + source,
                device(at, y=yy, zl=c, c=cc), mine,
            )
    i_x = net.take(1)
    net.send_or_keep(x, x_in, i_x, i_x, device(at, zl=c, c=zl), zl == c)
    i_xb = swap(xb.at[c], xb.at[c])
    i_ob = swap(ogb.at[c], ogb.at[c])

    for s in range(8):
        net.arrive(recv.at[s], a_r + s)
    wide[...] = recv[...].astype(f32)
    for unit in range(13):
        for s in range(8):
            tall[unit, pl.ds(s * 6, 6), :] = wide[s, pl.ds(unit * 6, 6), :]
    for cb in range(3):
        watt[c, rb, :, pl.ds(cb * 128, 128)] = tall[cb].astype(bf16)
    others = plane_others(at)
    w_s, w_r = net.take(16), net.take(16)
    for i, place in others:
        net.send(watt.at[c, rb], watt.at[c, rb], w_s + i, w_r + rb, device(place))
    for cb in range(3):
        block = ffn_index(cb, y, at["x"], at["z"])
        for m in range(3):
            put_rows(wf, block, WEIGHT_ROWS[m], tall[3 + m * 3 + cb].astype(bf16))
        put_rows(wf, block, WEIGHT_ROWS[3], tall[12, pl.ds(cb * 16, 16), :].astype(bf16))
    jobs = [Gather(net, wf, job) for job in range(2)]
    for j in jobs:
        j.start(0)
    net.arrive(x_in, i_x)
    xg[y] = x_in[...]
    i_y = net.take(3)
    net.send(xg.at[y], xg.at[y], i_y, i_y, column[1])
    net.send(xg.at[y], xg.at[y], i_y + 1, i_y + 1, column[3])

    for s in range(8):
        row = wide[s, pl.ds(78, 1), :] * 64.0 + wide[s, pl.ds(79, 1), :]
        rows = jnp.broadcast_to(row, (128, 128))
        kpos[s % 2, s // 2] = rows.T
        qpos[s % 2, s // 2] = rows[:8]
    for yy in range(4):
        cosine[yy], sine[yy] = tables(kpos[c, yy], freq[0:1, :])

    for j in jobs:
        j.forward(0)
    net.arrive(xg.at[(y + 3) % 4], i_y)
    net.arrive(xg.at[(y + 1) % 4], i_y + 1)
    behind = (y - d + 4) % 4
    net.send(xg.at[behind], xg.at[behind], i_y + 2, i_y + 2, device(moved(at, "y", d)))
    for j in jobs:
        j.finish(0)
        j.start(1)

    def normalize(v):
        v = v.astype(f32)
        return (v * inverse_rms(v)).astype(bf16)

    for k in (0, 1, 3):
        yy = (y + k) % 4
        xn[yy] = normalize(xg[yy])
    for _, place in others:
        r = row_block(place)
        net.arrive(watt.at[c, r], w_r + r)
    e_w = net.take(2)
    net.send(watt.at[c], watt.at[c], e_w, e_w + c, partner)
    opposite = (y + 2) % 4
    net.arrive(xg.at[opposite], i_y + 2)
    xn[opposite] = normalize(xg[opposite])
    net.arrive(watt.at[1 - c], e_w + 1 - c)

    w_kv = watt[0].reshape(768, 384)
    w_q = watt[1, :, :, :256].reshape(768, 256)
    for yy in range(4):
        r = pl.ds(yy * 128, 128)
        kv_y = dot(xn[yy], w_kv)
        kv[c, r, :128] = turn(kv_y[:, :128], cosine[yy], sine[yy]).astype(bf16)
        kv[c, r, 128:256] = turn_first_half(kv_y[:, 128:256], cosine[yy], sine[yy]).astype(bf16)
        kv[c, r, 256:] = kv_y[:, 256:].astype(bf16)
    e_k = swap(kv.at[c], kv.at[c])
    for yy in range(4):
        r = pl.ds(yy * 128, 128)
        q_y = dot(xn[yy], w_q)
        q[r, :128] = (turn(q_y[:, :128], cosine[yy], sine[yy]).astype(bf16) * 0.125).astype(bf16)
        q[r, 128:] = (turn(q_y[:, 128:], cosine[yy], sine[yy]).astype(bf16) * 0.125).astype(bf16)
    for j in jobs:
        j.forward(1)
    net.arrive(kv.at[1 - c], e_k)
    own_qpos = qpos.at[c]
    for h in range(3):
        forward_head(h, q, kv, own_qpos, kpos, lse, mixed_t)
        if h == 0:
            for j in jobs:
                j.finish(1)
                j.start(2)
    mix = mixed_t[...].T.astype(bf16)
    for yy in range(4):
        mixed_s[yy] = mix[yy * 128 : (yy + 1) * 128, :]
    m_s = net.take(4)
    for yy in range(4):
        mine = jnp.logical_and(y == yy, jnp.logical_and(zl == c, y // 2 == c))
        net.send_or_keep(
            mixed_s.at[yy], mixed.at[zl, y % 2], m_s + yy, m_s + zl * 2 + y % 2,
            device(at, y=yy, zl=c, c=y // 2), mine,
        )
    xnt[...] = xn[...].reshape(512, 768).T
    net.arrive(ogb.at[1 - c], i_ob)
    net.arrive(xb.at[1 - c], i_xb)
    ogt[...] = ogb[...].reshape(256, 768).T
    jobs[0].forward(2)
    jobs[1].forward(2)
    for s in range(2):
        for y2 in range(2):
            net.arrive(mixed.at[s, y2], m_s + s * 2 + y2)
    jobs[0].finish(2)
    for p in range(3):
        for yy in range(3):
            for z in range(4):
                for xx in range(4):
                    r = (xx * 2 + z % 2) * 48 + p * 16
                    wo[c, z // 2, pl.ds(r, 16), pl.ds(yy * 128, 128)] = get_rows(
                        wf, ffn_index(p, yy, xx, z), WEIGHT_ROWS[3]
                    )[0]
    e_o = net.take(2)
    net.send(wo.at[c], wo.at[c], e_o, e_o + c, partner)
    net.arrive(wo.at[1 - c], e_o + 1 - c)

    mix = [mixed[:, y2].reshape(256, 192) for y2 in range(2)]
    for ch in range(2):
        po[:, pl.ds(ch * 384, 384)] = dot(mix[0], wo[ch, c, :192, :]) + dot(mix[1], wo[ch, c, 192:, :])
    s_po = swap(po, por)
    acc[...] = jnp.zeros_like(acc)
    outp[...] = jnp.zeros_like(outp)
    net.arrive(por, s_po)
    middle = xb[...].reshape(256, 768).astype(f32) + (po[...] + por[...])
    mid[...] = middle
    n2[...] = (middle * inverse_rms(middle)).astype(bf16)
    n2t[...] = n2[...].T
    jobs[1].finish(2)

    def quarter(yy, carry):
        w_gate = ffn_panel(wf, 0, yy)
        w_up = ffn_panel(wf, 1, yy)
        w_down = ffn_panel(wf, 2, yy)
        gate = dot(n2[...], w_gate)
        up = dot(n2[...], w_up)
        grad_hidden = dot(ogb[...].reshape(256, 768), w_down)
        sig = jax.nn.sigmoid(gate)
        act = gate * sig
        hidden = (act * up).astype(bf16)
        d_gate = (grad_hidden * up * (sig * (1.0 + gate * (1.0 - sig)))).astype(bf16)
        d_up = (grad_hidden * act).astype(bf16)
        outp[...] += dot_nt(hidden, w_down)
        acc[...] += dot_nt(d_gate, w_gate) + dot_nt(d_up, w_up)
        store_ffn_panel(g, 0, yy, dot(n2t[...], d_gate).astype(bf16))
        store_ffn_panel(g, 1, yy, dot(n2t[...], d_up).astype(bf16))
        store_ffn_panel(g, 2, yy, dot(ogt[...], hidden).astype(bf16))
        return carry

    lax.fori_loop(0, 4, quarter, 0)
    s_acc = swap(acc, accr)
    levels, got, on = (g, lev2, lev1, lev0), (got3, got2, got1), (on3, on2, on1)
    jobs = [Scatter(net, levels, got, on, job) for job in range(2)]
    jobs[0].start(2)
    s_out = swap(outp.at[their_rows, :], outr)
    dkv[...] = jnp.zeros_like(dkv)
    dq_t[pl.ds(192, 64), :] = jnp.zeros((64, 512), f32)
    net.arrive(accr, s_acc)
    middle = mid[...]
    r2 = inverse_rms(middle)
    a = acc[...] + accr[...]
    scaled = middle * r2
    grad_middle = ogb[...].reshape(256, 768).astype(f32) + r2 * (
        a - scaled * jnp.mean(a * scaled, axis=-1, keepdims=True)
    )
    por[...] = grad_middle
    branch[...] = grad_middle.astype(bf16)
    for y2 in range(2):
        r = pl.ds(y2 * 192, 192)
        v = dot_nt(branch[:, :384], wo[0, c, r, :]) + dot_nt(branch[:, 384:], wo[1, c, r, :])
        for s in range(2):
            gm[y2, s] = v[s * 128 : (s + 1) * 128, :].astype(bf16)
    s_g, s_gr = net.take(4), net.take(4)
    for y2 in range(2):
        for s in range(2):
            mine = jnp.logical_and(c * 2 + y2 == y, jnp.logical_and(zl == s, zl == c))
            net.send_or_keep(
                gm.at[y2, s], go.at[y], s_g + y2 * 2 + s, s_gr + y, device(at, y=c * 2 + y2, zl=s, c=zl), mine
            )
    for ch in range(2):
        for y2 in range(2):
            dwo[ch, pl.ds(y2 * 192, 192), :] = dot_tn(mix[y2], branch[:, ch * 384 : (ch + 1) * 384]).astype(bf16)
    s_dw = swap(dwo.at[1 - c], dwr)
    net.arrive(outr, s_out)
    outputs[...] = (mid[own_rows, :] + (outp[own_rows, :] + outr[...])).astype(bf16)
    net.arrive(dwr, s_dw)
    for p in range(3):
        for yy in range(4):
            for xx in range(4):
                for low in range(2):
                    r = (xx * 2 + low) * 48 + p * 16
                    own_place, their_place = (ffn_index(p, yy, xx, h * 2 + low) for h in (c, 1 - c))
                    if yy < 3:
                        put_rows(g, own_place, GRAD_ROWS[3], dwo[c, pl.ds(r, 16), pl.ds(yy * 128, 128)])
                        put_rows(g, their_place, GRAD_ROWS[3], dwr[pl.ds(r, 16), pl.ds(yy * 128, 128)])
                    else:
                        put_rows(g, own_place, GRAD_ROWS[3], jnp.zeros((16, 128), bf16))
                        put_rows(g, their_place, GRAD_ROWS[3], jnp.zeros((16, 128), bf16))
    jobs[1].start(2)

    for yy in range(4):
        net.arrive(go.at[yy], s_gr + yy)
    for h in range(3):
        backward_head(h, q, kv, own_qpos, kpos, lse, go, dkv, dq_t)
        if h == 0:
            jobs[0].forward(2)
        if h == 1:
            jobs[0].finish(2)
            jobs[0].start(1)
            jobs[1].forward(2)
    dkv_s[...] = dkv[1 - c].astype(bf16)
    s_k = swap(dkv_s, dkv_r)
    dq = dq_t[...].T * 0.125
    for yy in range(4):
        r = pl.ds(yy * 128, 128)
        v = dq[yy * 128 : (yy + 1) * 128, :]
        dp[r, 384:512] = turn(v[:, :128], cosine[yy], -sine[yy]).astype(bf16)
        dp[r, 512:] = turn(v[:, 128:], cosine[yy], -sine[yy]).astype(bf16)
    net.arrive(dkv_r, s_k)
    for yy in range(4):
        r = pl.ds(yy * 128, 128)
        v = dkv[c, r, :] + dkv_r[r, :].astype(f32)
        dp[r, :128] = turn(v[:, :128], cosine[yy], -sine[yy]).astype(bf16)
        dp[r, 128:256] = turn_first_half(v[:, 128:256], cosine[yy], -sine[yy]).astype(bf16)
        dp[r, 256:384] = v[:, 256:].astype(bf16)
    dw[0] = dot(xnt[...], dp[:, :384]).astype(bf16).reshape(16, 48, 384)
    dw[1, :, :, :256] = dot(xnt[...], dp[:, 384:]).astype(bf16).reshape(16, 48, 256)
    dw[1, :, :, 256:] = jnp.zeros((16, 48, 128), bf16)
    s_w = swap(dw.at[1 - c], dw_r)
    a_kv = dot_nt(dp[:, :384], watt[0].reshape(768, 384))
    a_q = dot_nt(dp[:, 384:], watt[1, :, :, :256].reshape(768, 256))
    a_s[...] = (a_kv + a_q).astype(bf16).reshape(4, 128, 768)
    i_a = net.take(3)
    net.send(a_s.at[opposite], a_got.at[2], i_a + 2, i_a + 2, device(moved(at, "y", 4 - d)))
    ahead = (y + d + 4) % 4
    net.send(a_s.at[ahead], a_got.at[0], i_a, i_a, device(moved(at, "y", d)))
    net.arrive(dw_r, s_w)
    dw_sum[...] = (dw[c].astype(f32) + dw_r[...].astype(f32)).astype(bf16)
    s_p, s_pr = net.take(16), net.take(16)
    for i, place in others:
        net.send(dw_sum.at[row_block(place)], plane.at[rb], s_p + i, s_pr + rb, device(place))
    jobs[1].finish(2)
    jobs[1].start(1)
    net.arrive(a_got.at[2], i_a + 2)
    a_on[...] = (a_s[behind].astype(f32) + a_got[2].astype(f32)).astype(bf16)
    net.send(a_on, a_got.at[1], i_a + 1, i_a + 1, device(moved(at, "y", 4 - d)))
    for j in jobs:
        j.forward(1)
    net.arrive(a_got.at[0], i_a)
    net.arrive(a_got.at[1], i_a + 1)
    a_sum[...] = (a_s[y].astype(f32) + a_got[0].astype(f32) + a_got[1].astype(f32)).astype(bf16)
    i_z = net.take(1)
    net.send_or_keep(a_sum, a_own, i_z, i_z, device(at, zl=c, c=zl), zl == c)
    for j in jobs:
        j.finish(1)
        j.start(0)
    total = dw_sum[rb].astype(f32)
    for _, place in others:
        r = row_block(place)
        net.arrive(plane.at[r], s_pr + r)
        total = total + plane[r].astype(f32)
    for cb in range(3):
        tall[cb] = total[:, cb * 128 : (cb + 1) * 128]
    for j in jobs:
        j.forward(0)
    net.arrive(a_own, i_z)
    v = x[...].astype(f32)
    r1 = inverse_rms(v)
    scaled = v * r1
    a = a_own[...].astype(f32)
    input_grad[...] = por[own_rows, :] + r1 * (a - scaled * jnp.mean(a * scaled, axis=-1, keepdims=True))
    for j in jobs:
        j.finish(0)
    for cb in range(3):
        for m in range(3):
            for own, job, first, count in GRAD_ROWS[m]:
                tall[3 + m * 3 + cb, pl.ds(own, count), :] = lev0[job, cb, pl.ds(first, count), :].astype(f32)
        tall[12, pl.ds(cb * 16, 16), :] = lev0[1, cb, pl.ds(64, 16), :].astype(f32)
    for s in range(8):
        for unit in range(13):
            back_s[s, pl.ds(unit * 6, 6), :] = tall[unit, pl.ds(s * 6, 6), :]
        back_s[s, pl.ds(78, 2), :] = jnp.zeros((2, 128), f32)
    back_p[...] = back_s[...].astype(bf16)
    s_b, s_br = net.take(8), net.take(8)
    slot = c * 4 + y
    for s in range(8):
        mine = jnp.logical_and(y * 2 + zl == s, zl == c)
        net.send_or_keep(
            back_p.at[s], back.at[slot], s_b + s, s_br + slot, device(at, y=s // 2, zl=s % 2, c=zl), mine
        )
    for s in range(8):
        net.arrive(back.at[s], s_br + s)
    grads[...] = back[...].astype(f32)
    net.drain()


VM = pl.BlockSpec(memory_space=pltpu.VMEM)
SEMS = 320


def layer(*args):
    wf_shape = (2, 3, 4, 4, 4, JOB_ROWS, 128)
    f, h = f32, bf16
    scratch = [
        ((8, 80, 128), f), ((8, 80, 128), h), ((8, 80, 128), h), ((8, 80, 128), f), ((13, 48, 128), f),
        ((2, 16, 48, 384), h), (wf_shape, h), ((2, 2, 384, 384), h),
        ((128, 768), h), ((4, 128, 768), h), ((4, 128, 768), h), ((768, 512), h), ((4, 128, 128), f),
        ((4, 128, 128), f), ((2, 4, 128, 128), f), ((2, 4, 8, 128), f), ((2, 512, 384), h), ((512, 256), h),
        ((8, 512), f),
        ((192, 512), f), ((4, 128, 192), h), ((2, 2, 128, 192), h),
        ((2, 128, 768), h), ((2, 128, 768), h), ((256, 768), f), ((256, 768), f), ((256, 768), f),
        ((256, 768), h), ((768, 256), h), ((768, 256), h), ((256, 768), f), ((256, 768), f), ((256, 768), f),
        ((128, 768), f), ((256, 768), h), ((2, 384, 384), h), ((384, 384), h), ((2, 2, 128, 192), h), (wf_shape, h),
        ((4, 128, 192), h), ((2, 512, 384), f), ((512, 384), h), ((512, 384), h), ((256, 512), f), ((512, 640), h),
        ((2, 16, 48, 384), h), ((16, 48, 384), h), ((16, 48, 384), h), ((16, 48, 384), h),
        ((4, 128, 768), h), ((3, 128, 768), h), ((128, 768), h), ((128, 768), h), ((128, 768), h),
        ((8, 80, 128), f), ((8, 80, 128), h), ((8, 80, 128), h),
        *[((2, 3, 3) + (4,) * k + (JOB_ROWS, 128), h) for k in (2, 1, 0)],
        *[((2, 3) + (4,) * k + (JOB_ROWS, 128), h) for k in (2, 1, 0)],
        *[((2, 3) + (4,) * k + (JOB_ROWS, 128), h) for k in (2, 1, 0)],
    ]
    return pl.pallas_call(
        layer_body,
        out_shape=(
            jax.ShapeDtypeStruct((128, 768), bf16),
            jax.ShapeDtypeStruct((128, 768), f32),
            jax.ShapeDtypeStruct((8, 80, 128), f32),
        ),
        in_specs=[VM] * len(args),
        out_specs=(VM,) * 3,
        scratch_shapes=[pltpu.VMEM(s, t) for s, t in scratch] + [pltpu.SemaphoreType.DMA((SEMS,))] * 2,
        compiler_params=pltpu.CompilerParams(collective_id=0, has_side_effects=True, vmem_limit_bytes=60 << 20),
    )(*args)


def adam_step(master, gradient, moment_one, moment_two, rate_value, decay_value):
    moment_one = BETA_FIRST * moment_one + (1.0 - BETA_FIRST) * gradient
    moment_two = BETA_SECOND * moment_two + (1.0 - BETA_SECOND) * gradient * gradient
    first_hat = moment_one / (1.0 - BETA_FIRST**STEP)
    second_hat = moment_two / (1.0 - BETA_SECOND**STEP)
    updated = master - rate_value * (
        first_hat / (jnp.sqrt(second_hat) + ADAM_EPS) + decay_value * master
    )
    return (moment_one, moment_two, updated)


def owner_body(
    grads, outputs, input_grad,
    qkv, qkv_m, qkv_s, out, out_m, out_s, gu, gu_m, gu_s, dt, dt_m, dt_s, gains, gains_m, gains_s,
    outputs_o, input_grad_o,
    qkv_mo, qkv_so, qkv_o, out_mo, out_so, out_o, gu_mo, gu_so, gu_o, dt_mo, dt_so, dt_o,
    gains_mo, gains_so, gains_o,
):
    outputs_o[...] = outputs[...]
    input_grad_o[...] = input_grad[...]

    def unit(slot, u):
        return grads[slot, pl.ds(u * 6, 6), :]

    eye = lax.broadcasted_iota(jnp.int32, (6, 6), 0) == lax.broadcasted_iota(jnp.int32, (6, 6), 1)
    g_low = gains[...].astype(bf16).astype(f32)
    g_one = jnp.sum(jnp.where(eye, g_low[0:1, :], 0.0), axis=1, keepdims=True)
    g_two = jnp.sum(jnp.where(eye, g_low[1:2, :], 0.0), axis=1, keepdims=True)

    def update(refs, new, columns, gradient, rate, decay):
        w, m, s = refs
        values = adam_step(w[:, columns], gradient, m[:, columns], s[:, columns], rate, decay)
        for to, v in zip(new, values):
            to[:, columns] = v

    def low_times(w, columns, gradient):
        return jnp.sum(w[:, columns].astype(bf16).astype(f32) * gradient, axis=1, keepdims=True)

    def join(a, b):
        return jnp.concatenate([a, b], axis=1)

    rate = D ** (-0.5)
    sum_one = jnp.zeros((6, 1), f32)
    for pair in range(2):
        e, o = 2 * pair, 2 * pair + 1
        u = {(s, k): unit(s, k) for s in (e, o, 4 + e, 4 + o) for k in range(3)}
        tiles = {
            0: (u[4 + e, 0], join(u[4 + e, 1][:, :64], u[4 + o, 0][:, :64]), join(u[4 + o, 0][:, 64:], u[4 + o, 1][:, :64])),
            768: (u[e, 0], join(u[e, 1][:, :64], u[o, 0][:, :64]), join(u[o, 0][:, 64:], u[o, 1][:, :64])),
            1536: (join(u[e, 1][:, 64:], u[e, 2][:, :64]), join(u[e, 2][:, 64:], u[o, 1][:, 64:]), u[o, 2]),
        }
        for first, three in tiles.items():
            for k, t in enumerate(three):
                columns = pl.ds(first + pair * 384 + k * 128, 128)
                sum_one = sum_one + low_times(qkv, columns, t)
                update((qkv, qkv_m, qkv_s), (qkv_mo, qkv_so, qkv_o), columns, t * g_one, rate, WEIGHT_DECAY)
    sum_two = jnp.zeros((6, 1), f32)
    for slot in range(8):
        for cb in range(3):
            f = slot * 384 + cb * 128
            for half in range(2):
                columns = pl.ds(half * 3072 + f, 128)
                t = unit(slot, 3 + half * 3 + cb)
                sum_two = sum_two + low_times(gu, columns, t)
                update((gu, gu_m, gu_s), (gu_mo, gu_so, gu_o), columns, t * g_two, rate, WEIGHT_DECAY)
            update(
                (dt, dt_m, dt_s), (dt_mo, dt_so, dt_o), pl.ds(f, 128), unit(slot, 9 + cb), FF ** (-0.5), WEIGHT_DECAY
            )
        if slot % 4 < 3:
            update(
                (out, out_m, out_s), (out_mo, out_so, out_o), pl.ds((slot // 4) * 384 + (slot % 4) * 128, 128),
                unit(slot, 12), (H * HD * 32 // LEN) ** (-0.5), WEIGHT_DECAY,
            )
    rows = [jnp.sum(jnp.where(eye, v, 0.0), axis=0, keepdims=True) for v in (sum_one, sum_two)]
    values = adam_step(gains[...], jnp.concatenate(rows, axis=0), gains_m[...], gains_s[...], GAIN_RATE, 0.0)
    for to, v in zip((gains_mo, gains_so, gains_o), values):
        to[...] = v


def owners_step(*args):
    shapes = [(args[1].shape, bf16), (args[2].shape, f32)]
    for first in range(3, 18, 3):
        shapes += [(args[first].shape, f32)] * 3
    return pl.pallas_call(
        owner_body,
        out_shape=tuple(jax.ShapeDtypeStruct(s, t) for s, t in shapes),
        in_specs=[VM] * len(args),
        out_specs=(VM,) * len(shapes),
    )(*args)


def body(
    inputs, positions, output_grad,
    qkv_weight, qkv_first, qkv_second, out_weight, out_first, out_second,
    gate_up_weight, gate_up_first, gate_up_second, down_weight, down_first, down_second,
    norm_gains, gains_first, gains_second,
):
    frequency = ROPE_BASE ** (-2.0 * (jnp.arange(128) % 32).astype(f32) / HD)
    outputs, input_grad, grads = layer(
        qkv_weight, out_weight, gate_up_weight, down_weight.T, norm_gains,
        inputs.reshape(128, D), output_grad.reshape(128, D), positions,
        jnp.broadcast_to(frequency[None], (8, 128)),
    )
    new = owners_step(
        grads, outputs, input_grad,
        qkv_weight, qkv_first, qkv_second, out_weight, out_first, out_second,
        gate_up_weight, gate_up_first, gate_up_second, down_weight.T, down_first.T, down_second.T,
        norm_gains, gains_first, gains_second,
    )
    return (
        new[0].reshape(1, 128, D), new[1].reshape(1, 128, D), *new[2:11],
        *(v.T for v in new[11:14]), *new[14:],
    )


def solution(mesh):
    token = P("dp", "ctx", None)
    rows, columns = P(("dp", "ctx"), None), P(None, ("dp", "ctx"))
    return jax.shard_map(
        body,
        mesh=mesh,
        in_specs=(token, P("dp", "ctx"), token) + (rows,) * 9 + (columns,) * 6,
        out_specs=(token, token) + (rows,) * 9 + (columns,) * 6,
        check_vma=False,
    )
```

```python
import math

import jax
import jax.numpy as jnp
from jax import lax
from jax.experimental import pallas as pl
from jax.experimental.pallas import tpu as pltpu
from jax.sharding import PartitionSpec as P

D = 768
H = 12
HD = 64
FF = 3072
LEN = 1024
STEP = 10

NORM_EPS = 1e-05
ROPE_BASE = 10000.0
BETA_FIRST = 0.9
BETA_SECOND = 0.95
ADAM_EPS = 1e-08
WEIGHT_DECAY = 0.1
GAIN_RATE = 1.2
MASKED = -1e30

MESH = pl.DeviceIdType.MESH
bf16, f32 = jnp.bfloat16, jnp.float32

ORDERS = (("x", "y", "z"), ("y", "z", "x"), ("z", "x", "y"))
WEIGHT_JOBS = (64, 48, 48)
GRAD_JOBS = (48, 48, 64)


def here():
    dp, ctx = lax.axis_index("dp"), lax.axis_index("ctx")
    return dict(x=(dp // 2) % 4, y=ctx // 2, z=(dp // 8) * 2 + ctx % 2, c=dp % 2)


def low_z(at):
    return at["z"] % 2


def device(at, zl=None, **moved):
    at = dict(at, **moved)
    if zl is not None:
        at["z"] = (at["z"] // 2) * 2 + zl
    return ((at["z"] // 2) * 8 + at["x"] * 2 + at["c"], at["y"] * 2 + at["z"] % 2)


def moved(at, axis, step):
    return dict(at, **{axis: (at[axis] + step + 4) % 4})


def row_block(at):
    return (at["z"] // 2) * 8 + at["x"] * 2 + at["z"] % 2


def group_of(at):
    out = []
    me = at["c"] * 8 + at["y"] * 2 + low_z(at)
    for k in range(1, 16):
        other = (me + k) % 16
        out.append(device(at, c=other // 8, y=(other // 2) % 4, zl=other % 2))
    for k in range(4):
        for j in range(4):
            if k == 0 and j in (0, 1):
                continue
            out.append(device(moved_zlow(at, j), x=(at["x"] + k) % 4))
    return out


def moved_zlow(at, j):
    zh, zl = at["z"] // 2, at["z"] % 2
    zh = (zh + j // 2) % 2
    zl = (zl + j % 2) % 2
    return dict(at, z=zh * 2 + zl)


def signal_all(peers):
    barrier = pltpu.get_barrier_semaphore()
    for p in peers:
        pl.semaphore_signal(barrier, inc=1, device_id=p, device_id_type=MESH)


def wait_all(peers):
    pl.semaphore_wait(pltpu.get_barrier_semaphore(), len(peers))


class Net:
    def __init__(self, at, send_sem, recv_sem):
        self.at, self.send_sem, self.recv_sem = at, send_sem, recv_sem
        self.used = 0
        self.sent = []

    def take(self, count):
        base = self.used
        self.used += count
        return base

    def copy(self, src, dst, s, r, to):
        return pltpu.make_async_remote_copy(
            src_ref=src, dst_ref=dst, send_sem=self.send_sem.at[s], recv_sem=self.recv_sem.at[r],
            device_id=to, device_id_type=MESH,
        )

    def send(self, src, dst, s, r, to):
        c = self.copy(src, dst, s, r, to)
        c.start()
        self.sent.append((c, None))

    def send_or_keep(self, src, dst, s, r, to, mine):
        c = self.copy(src, dst, s, r, to)
        away = jnp.logical_not(mine)

        @pl.when(away)
        def _():
            c.start()

        @pl.when(mine)
        def _():
            pltpu.make_async_copy(src, dst, self.recv_sem.at[r]).start()

        self.sent.append((c, away))

    def arrive(self, dst, r):
        pltpu.make_async_copy(dst, dst, self.recv_sem.at[r]).wait()

    def drain(self):
        for c, away in self.sent:
            if away is None:
                c.wait_send()
            else:
                pl.when(away)(c.wait_send)
        self.sent = []


class Gather:
    def __init__(self, net, ref):
        self.net, self.at, self.ref = net, net.at, ref
        self.base = net.take(27)

    def view(self, part, at, phase):
        a1, a2, a3 = ORDERS[part]
        return self.ref.at[(part, at[a3], at[a2], at[a1])[: 4 - phase]]

    def sem(self, part, phase, kind):
        return self.base + (part * 3 + phase) * 3 + kind

    def send(self, part, phase, kind, at, axis, step):
        v, i = self.view(part, at, phase), self.sem(part, phase, kind)
        self.net.send(v, v, i, i, device(moved(self.at, axis, step)))

    def arrive(self, part, phase, kind, at):
        self.net.arrive(self.view(part, at, phase), self.sem(part, phase, kind))

    def start(self, phase):
        for part in range(3):
            axis = ORDERS[part][phase]
            self.send(part, phase, 0, self.at, axis, 1)
            self.send(part, phase, 1, self.at, axis, 3)
            if phase < 2:
                self.send(part, phase, 2, self.at, axis, 2)

    def forward(self):
        d = 1 - 2 * self.at["c"]
        for part in range(3):
            axis = ORDERS[part][2]
            self.arrive(part, 2, 0, moved(self.at, axis, 3))
            self.arrive(part, 2, 1, moved(self.at, axis, 1))
            self.send(part, 2, 2, moved(self.at, axis, -d), axis, d)

    def finish(self, phase):
        for part in range(3):
            axis = ORDERS[part][phase]
            if phase < 2:
                self.arrive(part, phase, 0, moved(self.at, axis, 3))
                self.arrive(part, phase, 1, moved(self.at, axis, 1))
            self.arrive(part, phase, 2, moved(self.at, axis, 2))


class Scatter:
    def __init__(self, net, levels, got, turned):
        self.net, self.at = net, net.at
        self.levels, self.got, self.turned = levels, got, turned
        self.base = net.take(27)

    def sem(self, part, phase, kind):
        return self.base + (part * 3 + phase) * 3 + kind

    def level(self, part, phase, i):
        return self.levels[2 - phase].at[part, i]

    def slot(self, part, phase, kind):
        return self.got[2 - phase].at[part, kind]

    def go(self, src, part, phase, kind, axis, step):
        i = self.sem(part, phase, kind)
        self.net.send(src, self.slot(part, phase, kind), i, i, device(moved(self.at, axis, step)))

    def come(self, part, phase, kind):
        self.net.arrive(self.slot(part, phase, kind), self.sem(part, phase, kind))

    def add(self, to, refs, phase):
        blocks = 4**phase

        def one(b, carry):
            index = ()
            for k in reversed(range(phase)):
                index += ((b // 4**k) % 4,)
            total = refs[0][index].astype(f32)
            for r in refs[1:]:
                total = total + r[index].astype(f32)
            to[index] = total.astype(to.dtype)
            return carry

        if blocks == 1:
            one(0, 0)
        else:
            lax.fori_loop(0, blocks, one, 0)

    def start(self, phase):
        d = 1 - 2 * self.at["c"]
        for part in range(3):
            axis = ORDERS[part][phase]
            me = self.at[axis]
            if phase < 2:
                for kind, step in enumerate((1, 3, 2)):
                    self.go(self.level(part, phase, (me + step) % 4), part, phase, kind, axis, step)
            else:
                self.go(self.level(part, phase, (me + 2) % 4), part, phase, 2, axis, 4 - d)
                self.go(self.level(part, phase, (me + d + 4) % 4), part, phase, 0, axis, d)

    def forward(self):
        d = 1 - 2 * self.at["c"]
        for part in range(3):
            axis = ORDERS[part][2]
            me = self.at[axis]
            self.come(part, 2, 2)
            to = self.turned.at[part]
            self.add(to, [self.level(part, 2, (me - d + 4) % 4), self.slot(part, 2, 2)], 2)
            self.go(to, part, 2, 1, axis, 4 - d)

    def finish(self, phase):
        for part in range(3):
            me = self.at[ORDERS[part][phase]]
            kinds = (0, 1, 2) if phase < 2 else (0, 1)
            for kind in kinds:
                self.come(part, phase, kind)
            to = self.levels[3 - phase].at[part]
            self.add(to, [self.level(part, phase, me)] + [self.slot(part, phase, k) for k in kinds], phase)


def dot(a, b):
    return jnp.dot(a, b, preferred_element_type=f32)


def dot_nt(a, b):
    return lax.dot_general(a, b, (((1,), (1,)), ((), ())), preferred_element_type=f32)


def dot_tn(a, b):
    return lax.dot_general(a, b, (((0,), (0,)), ((), ())), preferred_element_type=f32)


def inverse_rms(v):
    return lax.rsqrt(jnp.mean(v * v, axis=-1, keepdims=True) + NORM_EPS)


def tables(place, freq):
    angle = place * freq
    lane = lax.broadcasted_iota(jnp.int32, place.shape, 1)
    sine = jnp.sin(angle)
    return jnp.cos(angle), jnp.where(lane % 64 < 32, -sine, sine)


def turn(v, cosine, sine):
    lane = lax.broadcasted_iota(jnp.int32, v.shape, 1)
    swapped = jnp.where(lane % 64 < 32, pltpu.roll(v, 96, 1), pltpu.roll(v, 32, 1))
    return v * cosine + swapped * sine


def turn_first_half(v, cosine, sine):
    lane = lax.broadcasted_iota(jnp.int32, v.shape, 1)
    return jnp.where(lane < 64, turn(v, cosine, sine), v)


def ffn_index(part, y, x, z):
    place = dict(x=x, y=y, z=z)
    a1, a2, a3 = ORDERS[part]
    return (part, place[a3], place[a2], place[a1])


WEIGHT_ROWS = ((0, 16, 48), (1, 0, 48), (2, 0, 48), (0, 0, 16))
GRAD_ROWS = ((1, 0, 48), (2, 0, 48), (0, 0, 48), (2, 48, 16))


def put_rows(refs, place, rows, value):
    job, first, count = rows
    refs[job][place + (pl.ds(first, count), slice(None))] = value


def get_rows(refs, place, rows):
    job, first, count = rows
    return refs[job][place + (pl.ds(first, count), slice(None))]


def ffn_panel(wf, matrix, y):
    return jnp.concatenate(
        [
            jnp.concatenate(
                [
                    get_rows(wf, ffn_index(p, y, x, zh * 2 + zl), WEIGHT_ROWS[matrix])
                    for zh in range(2) for x in range(4) for zl in range(2)
                ],
                axis=0,
            )
            for p in range(3)
        ],
        axis=1,
    )


def store_ffn_panel(g, matrix, y, value):
    for p in range(3):
        for zh in range(2):
            for x in range(4):
                for zl in range(2):
                    r = (zh * 8 + x * 2 + zl) * 48
                    put_rows(
                        g, ffn_index(p, y, x, zh * 2 + zl), GRAD_ROWS[matrix], value[r : r + 48, p * 128 : (p + 1) * 128]
                    )


def head_parts(h, kv):
    k = jnp.concatenate([kv[0, :, h * 64 : (h + 1) * 64], kv[1, :, h * 64 : (h + 1) * 64]], axis=0)
    o = 192 + h * 64
    v = jnp.concatenate([kv[0, :, o : o + 64], kv[1, :, o : o + 64]], axis=0)
    return k, v


def query_positions(qpos, half):
    return jnp.concatenate([qpos[half * 2], qpos[half * 2 + 1]], axis=1)[0:1, :]


def masked_scores(k, q_part, kpos, q_row):
    s = dot_nt(k, q_part)
    kp = kpos[...].reshape(1024, 128)
    allowed = jnp.concatenate([kp, kp], axis=1) <= q_row
    return jnp.where(allowed, s, MASKED)


def forward_head(h, q, kv, qpos, kpos, lse, mixed_t):
    k, v = head_parts(h, kv)
    for half in range(2):
        q_part = q[pl.ds(half * 256, 256), h * 64 : (h + 1) * 64]
        s = masked_scores(k, q_part, kpos, query_positions(qpos, half))
        highest = jnp.max(s, axis=0, keepdims=True)
        e = jnp.exp(s - highest)
        total = jnp.sum(e, axis=0, keepdims=True)
        p = (e * (1.0 / total)).astype(bf16)
        mixed_t[pl.ds(h * 64, 64), pl.ds(half * 256, 256)] = dot_tn(v, p)
        lse[pl.ds(h, 1), pl.ds(half * 256, 256)] = highest + jnp.log(total)


def backward_head(h, q, kv, qpos, kpos, lse, go, dkv, dq_t):
    k, v = head_parts(h, kv)
    for half in range(2):
        rows = pl.ds(half * 256, 256)
        q_part = q[rows, h * 64 : (h + 1) * 64]
        g_part = go[pl.ds(half * 2, 2), :, h * 64 : (h + 1) * 64].reshape(256, 64)
        s = masked_scores(k, q_part, kpos, query_positions(qpos, half))
        p = jnp.exp(s - lse[pl.ds(h, 1), rows])
        dp = dot_nt(v, g_part)
        centre = jnp.sum(p * dp, axis=0, keepdims=True)
        ds = (p * (dp - centre)).astype(bf16)
        dv = dot(p.astype(bf16), g_part)
        dk = dot(ds, q_part)
        dq_t[pl.ds(h * 64, 64), rows] = dot_tn(k, ds)
        for cc in range(2):
            dkv[cc, :, h * 64 : (h + 1) * 64] += dk[cc * 512 : (cc + 1) * 512]
            dkv[cc, :, 192 + h * 64 : 192 + (h + 1) * 64] += dv[cc * 512 : (cc + 1) * 512]


def plane_others(at):
    out = []
    for k in range(4):
        for j in range(4):
            if k or j:
                out.append((k * 4 + j, dict(moved_zlow(at, j), x=(at["x"] + k) % 4)))
    return out


def as_column(eye, row):
    return jnp.sum(jnp.where(eye, row, 0.0), axis=1, keepdims=True)


def low_gains(gains):
    eye = lax.broadcasted_iota(jnp.int32, (6, 6), 0) == lax.broadcasted_iota(jnp.int32, (6, 6), 1)
    g_low = gains[...].astype(bf16).astype(f32)
    return as_column(eye, g_low[0:1, :]), as_column(eye, g_low[1:2, :])


def cut_attention(qkv, g_one, positions, stage):
    place = positions[...]
    place = jnp.concatenate([(place // 64).astype(f32), (place % 64).astype(f32)], axis=0)
    zero = jnp.zeros((6, 64), f32)
    for yy in range(4):
        o = yy * 192
        q_y = qkv[:, o : o + 192].astype(bf16).astype(f32) * g_one
        k_y = qkv[:, 768 + o : 768 + o + 192].astype(bf16).astype(f32) * g_one
        v_y = qkv[:, 1536 + o : 1536 + o + 192].astype(bf16).astype(f32) * g_one
        stage[yy, pl.ds(0, 6), :] = k_y[:, :128]
        stage[yy, pl.ds(6, 6), :] = jnp.concatenate([k_y[:, 128:], v_y[:, :64]], axis=1)
        stage[yy, pl.ds(12, 6), :] = v_y[:, 64:]
        stage[4 + yy, pl.ds(0, 6), :] = q_y[:, :128]
        stage[4 + yy, pl.ds(6, 6), :] = jnp.concatenate([q_y[:, 128:], zero], axis=1)
        stage[4 + yy, pl.ds(12, 6), :] = jnp.zeros((6, 128), f32)
    for slot in range(8):
        stage[slot, pl.ds(18, 2), :] = place
        stage[slot, pl.ds(20, 12), :] = jnp.zeros((12, 128), f32)


def cut_rest(out, gu, dt, g_two, stage):
    def put(slot, unit, v):
        stage[slot, pl.ds(unit * 6, 6), :] = v

    for slot in range(8):
        for cb in range(3):
            f = slot * 384 + cb * 128
            put(slot, cb, gu[:, f : f + 128].astype(bf16).astype(f32) * g_two)
            put(slot, 3 + cb, gu[:, 3072 + f : 3072 + f + 128].astype(bf16).astype(f32) * g_two)
            put(slot, 6 + cb, dt[:, f : f + 128])
        cc, yy = slot // 4, slot % 4
        if yy < 3:
            put(slot, 9, out[:, cc * 384 + yy * 128 : cc * 384 + (yy + 1) * 128])
        else:
            put(slot, 9, jnp.zeros((6, 128), f32))
        stage[slot, pl.ds(60, 4), :] = jnp.zeros((4, 128), f32)


def layer_body(
    qkv_h, out_h, gu_h, dt_h, gains_h, x_h, og_h, positions_h,
    outputs, input_grad, grads,
    qkv, out, gu, dt, gains, positions,
    stage_a, pieces_a, recv_a, wide_a, stage_f, pieces_f, recv_f, wide_f, tall,
    watt, wf0, wf1, wf2, wo, xg, xn, xnt, cosine, sine, kpos, qpos, kv, q, lse,
    mixed_t, mixed_s, mixed,
    xb, ogb, po, por, mid, n2, n2t, ogt, act, slope, hid, acc, accr, outp, outr, branch, dwo, dwr, gm, g0, g1, g2,
    go, dkv, dkv_s, dkv_r, dq_t, dp, dw, dw_r, dw_sum, plane, a_s, a_got, a_sum, a_own, back_s, back_p, back,
    *rest,
):
    per_job, (send_sem, recv_sem, load_sem) = rest[:-3], rest[-3:]
    at = here()
    c, y, zl = at["c"], at["y"], low_z(at)
    d = 1 - 2 * c
    net = Net(at, send_sem, recv_sem)
    peers = group_of(at)
    partner = device(at, c=1 - c)
    rb = row_block(at)
    own_rows = pl.ds(pl.multiple_of(c * 128, 128), 128)
    their_rows = pl.ds(pl.multiple_of((1 - c) * 128, 128), 128)

    def swap(src, dst):
        i = net.take(1)
        net.send(src, dst, i, i, partner)
        return i

    loads = [
        pltpu.make_async_copy(src, dst, load_sem.at[i])
        for i, (src, dst) in enumerate(
            (
                (qkv_h, qkv), (gains_h, gains), (positions_h, positions), (x_h, xb.at[c]),
                (gu_h, gu), (dt_h, dt), (out_h, out), (og_h, ogb.at[c]),
            )
        )
    ]
    for copy in loads:
        copy.start()
    signal_all(peers)
    for copy in loads[:3]:
        copy.wait()
    g_one, g_two = low_gains(gains)
    cut_attention(qkv, g_one, positions, stage_a)
    pieces_a[...] = stage_a[...].astype(bf16)
    loads[3].wait()
    wait_all(peers)

    source = y * 2 + zl

    def to_group(pieces, recv):
        i = net.take(8)
        for cc in range(2):
            for yy in range(4):
                mine = jnp.logical_and(zl == c, jnp.logical_and(y == yy, c == cc))
                net.send_or_keep(
                    pieces.at[cc * 4 + yy], recv.at[source], i + cc * 4 + yy, i + source,
                    device(at, y=yy, zl=c, c=cc), mine,
                )
        return i

    r_a = to_group(pieces_a, recv_a)
    i_x = net.take(1)
    net.send_or_keep(xb.at[c], xg.at[y], i_x, i_x, device(at, zl=c, c=zl), zl == c)
    i_xb = swap(xb.at[c], xb.at[c])
    for copy in loads[4:]:
        copy.wait()
    cut_rest(out, gu, dt, g_two, stage_f)
    pieces_f[...] = stage_f[...].astype(bf16)
    r_f = to_group(pieces_f, recv_f)
    i_ob = swap(ogb.at[c], ogb.at[c])

    for s in range(8):
        net.arrive(recv_a.at[s], r_a + s)
    wide_a[...] = recv_a[...].astype(f32)
    for unit in range(3):
        for s in range(8):
            tall[unit, pl.ds(s * 6, 6), :] = wide_a[s, pl.ds(unit * 6, 6), :]
    for cb in range(3):
        watt[c, rb, :, pl.ds(cb * 128, 128)] = tall[cb].astype(bf16)
    others = plane_others(at)
    w_s, w_r = net.take(16), net.take(16)
    for i, place in others:
        net.send(watt.at[c, rb], watt.at[c, rb], w_s + i, w_r + rb, device(place))
    net.arrive(xg.at[y], i_x)
    i_y = net.take(3)
    for kind, step in enumerate((1, 3, 2)):
        net.send(xg.at[y], xg.at[y], i_y + kind, i_y + kind, device(moved(at, "y", step)))

    for s in range(8):
        net.arrive(recv_f.at[s], r_f + s)
    wide_f[...] = recv_f[...].astype(f32)
    for unit in range(10):
        for s in range(8):
            tall[3 + unit, pl.ds(s * 6, 6), :] = wide_f[s, pl.ds(unit * 6, 6), :]
    wf = (wf0, wf1, wf2)
    for cb in range(3):
        block = ffn_index(cb, y, at["x"], at["z"])
        for m in range(3):
            put_rows(wf, block, WEIGHT_ROWS[m], tall[3 + m * 3 + cb].astype(bf16))
        put_rows(wf, block, WEIGHT_ROWS[3], tall[12, pl.ds(cb * 16, 16), :].astype(bf16))
    jobs = [Gather(net, ref) for ref in wf]
    for j in jobs:
        j.start(0)

    for s in range(8):
        row = wide_a[s, pl.ds(18, 1), :] * 64.0 + wide_a[s, pl.ds(19, 1), :]
        rows = jnp.broadcast_to(row, (128, 128))
        kpos[s % 2, s // 2] = rows.T
        qpos[s % 2, s // 2] = rows[:8]
    lane = lax.broadcasted_iota(jnp.int32, (1, 128), 1) % 32
    freq = jnp.exp(lane.astype(f32) * (-2.0 * math.log(ROPE_BASE) / HD))
    for yy in range(4):
        cosine[yy], sine[yy] = tables(kpos[c, yy], freq)
    for j in jobs:
        j.finish(0)
        j.start(1)

    def normalize(yy):
        v = xg[yy].astype(f32)
        xn[yy] = (v * inverse_rms(v)).astype(bf16)

    normalize(y)
    for kind, step in enumerate((3, 1, 2)):
        yy = (y + step) % 4
        net.arrive(xg.at[yy], i_y + kind)
        normalize(yy)
    for _, place in others:
        r = row_block(place)
        net.arrive(watt.at[c, r], w_r + r)
    e_w = net.take(2)
    net.send(watt.at[c], watt.at[c], e_w, e_w + c, partner)
    for j in jobs:
        j.finish(1)
        j.start(2)
    net.arrive(watt.at[1 - c], e_w + 1 - c)

    w_kv = watt[0].reshape(768, 384)
    w_q = watt[1, :, :, :256].reshape(768, 256)
    for yy in range(4):
        r = pl.ds(yy * 128, 128)
        kv_y = dot(xn[yy], w_kv)
        kv[c, r, :128] = turn(kv_y[:, :128], cosine[yy], sine[yy]).astype(bf16)
        kv[c, r, 128:256] = turn_first_half(kv_y[:, 128:256], cosine[yy], sine[yy]).astype(bf16)
        kv[c, r, 256:] = kv_y[:, 256:].astype(bf16)
    e_k = swap(kv.at[c], kv.at[c])
    for yy in range(4):
        r = pl.ds(yy * 128, 128)
        q_y = dot(xn[yy], w_q)
        q[r, :128] = (turn(q_y[:, :128], cosine[yy], sine[yy]).astype(bf16) * 0.125).astype(bf16)
        q[r, 128:] = (turn(q_y[:, 128:], cosine[yy], sine[yy]).astype(bf16) * 0.125).astype(bf16)
    net.arrive(kv.at[1 - c], e_k)
    own_qpos = qpos.at[c]
    for h in range(3):
        forward_head(h, q, kv, own_qpos, kpos, lse, mixed_t)
        if h == 1:
            jobs[0].forward()
    mix = mixed_t[...].T.astype(bf16)
    for yy in range(4):
        mixed_s[yy] = mix[yy * 128 : (yy + 1) * 128, :]
    m_s = net.take(4)
    for yy in range(4):
        mine = jnp.logical_and(y == yy, jnp.logical_and(zl == c, y // 2 == c))
        net.send_or_keep(
            mixed_s.at[yy], mixed.at[zl, y % 2], m_s + yy, m_s + zl * 2 + y % 2,
            device(at, y=yy, zl=c, c=y // 2), mine,
        )
    xnt[...] = xn[...].reshape(512, 768).T
    net.arrive(ogb.at[1 - c], i_ob)
    net.arrive(xb.at[1 - c], i_xb)
    ogt[...] = ogb[...].reshape(256, 768).T
    jobs[1].forward()
    jobs[0].finish(2)
    for p in range(3):
        for yy in range(3):
            for z in range(4):
                for xx in range(4):
                    r = (xx * 2 + z % 2) * 48 + p * 16
                    wo[c, z // 2, pl.ds(r, 16), pl.ds(yy * 128, 128)] = get_rows(
                        wf, ffn_index(p, yy, xx, z), WEIGHT_ROWS[3]
                    )
    e_o = net.take(2)
    net.send(wo.at[c], wo.at[c], e_o, e_o + c, partner)
    for s in range(2):
        for y2 in range(2):
            net.arrive(mixed.at[s, y2], m_s + s * 2 + y2)
    jobs[2].forward()
    net.arrive(wo.at[1 - c], e_o + 1 - c)

    mix = [mixed[:, y2].reshape(256, 192) for y2 in range(2)]
    for ch in range(2):
        po[:, pl.ds(ch * 384, 384)] = dot(mix[0], wo[ch, c, :192, :]) + dot(mix[1], wo[ch, c, 192:, :])
    s_po = swap(po, por)
    acc[...] = jnp.zeros_like(acc)
    jobs[1].finish(2)
    net.arrive(por, s_po)
    middle = xb[...].reshape(256, 768).astype(f32) + (po[...] + por[...])
    mid[...] = middle
    n2[...] = (middle * inverse_rms(middle)).astype(bf16)
    n2t[...] = n2[...].T

    grad = (g0, g1, g2)

    def forward_quarter(yy, carry):
        gate = dot(n2[...], ffn_panel(wf, 0, yy))
        up = dot(n2[...], ffn_panel(wf, 1, yy))
        sig = jax.nn.sigmoid(gate)
        a = gate * sig
        act[yy] = a
        slope[yy] = up * (sig * (1.0 + gate * (1.0 - sig)))
        hid[yy] = (a * up).astype(bf16)
        store_ffn_panel(grad, 2, yy, dot(ogt[...], hid[yy]).astype(bf16))
        return carry

    def backward_quarter(yy, carry):
        w_gate = ffn_panel(wf, 0, yy)
        w_up = ffn_panel(wf, 1, yy)
        grad_hidden = dot(ogb[...].reshape(256, 768), ffn_panel(wf, 2, yy))
        d_gate = (grad_hidden * slope[yy]).astype(bf16)
        d_up = (grad_hidden * act[yy]).astype(bf16)
        acc[...] += dot_nt(d_gate, w_gate) + dot_nt(d_up, w_up)
        store_ffn_panel(grad, 0, yy, dot(n2t[...], d_gate).astype(bf16))
        store_ffn_panel(grad, 1, yy, dot(n2t[...], d_up).astype(bf16))
        return carry

    def output_quarter(yy, carry):
        outp[...] += dot_nt(hid[yy], ffn_panel(wf, 2, yy))
        return carry

    gathers = jobs
    jobs = []
    for k in range(3):
        own = per_job[7 * k : 7 * k + 7]
        jobs.append(Scatter(net, (grad[k],) + own[:3], own[3:6], own[6]))
    lax.fori_loop(0, 4, forward_quarter, 0)
    jobs[0].start(2)
    gathers[2].finish(2)
    lax.fori_loop(0, 4, backward_quarter, 0)
    s_acc = swap(acc, accr)
    jobs[1].start(2)
    outp[...] = jnp.zeros_like(outp)
    lax.fori_loop(0, 4, output_quarter, 0)
    s_out = swap(outp.at[their_rows, :], outr)
    dkv[...] = jnp.zeros_like(dkv)
    dq_t[pl.ds(192, 64), :] = jnp.zeros((64, 512), f32)
    net.arrive(accr, s_acc)
    middle = mid[...]
    r2 = inverse_rms(middle)
    a = acc[...] + accr[...]
    scaled = middle * r2
    grad_middle = ogb[...].reshape(256, 768).astype(f32) + r2 * (
        a - scaled * jnp.mean(a * scaled, axis=-1, keepdims=True)
    )
    por[...] = grad_middle
    branch[...] = grad_middle.astype(bf16)
    for y2 in range(2):
        r = pl.ds(y2 * 192, 192)
        v = dot_nt(branch[:, :384], wo[0, c, r, :]) + dot_nt(branch[:, 384:], wo[1, c, r, :])
        for s in range(2):
            gm[y2, s] = v[s * 128 : (s + 1) * 128, :].astype(bf16)
    s_g, s_gr = net.take(4), net.take(4)
    for y2 in range(2):
        for s in range(2):
            mine = jnp.logical_and(c * 2 + y2 == y, jnp.logical_and(zl == s, zl == c))
            net.send_or_keep(
                gm.at[y2, s], go.at[y], s_g + y2 * 2 + s, s_gr + y, device(at, y=c * 2 + y2, zl=s, c=zl), mine
            )
    for ch in range(2):
        for y2 in range(2):
            dwo[ch, pl.ds(y2 * 192, 192), :] = dot_tn(mix[y2], branch[:, ch * 384 : (ch + 1) * 384]).astype(bf16)
    s_dw = swap(dwo.at[1 - c], dwr)
    net.arrive(outr, s_out)
    outputs[...] = (mid[own_rows, :] + (outp[own_rows, :] + outr[...])).astype(bf16)
    net.arrive(dwr, s_dw)
    for p in range(3):
        for yy in range(4):
            for xx in range(4):
                for low in range(2):
                    r = (xx * 2 + low) * 48 + p * 16
                    own_place, their_place = (ffn_index(p, yy, xx, h * 2 + low) for h in (c, 1 - c))
                    if yy < 3:
                        put_rows(grad, own_place, GRAD_ROWS[3], dwo[c, pl.ds(r, 16), pl.ds(yy * 128, 128)])
                        put_rows(grad, their_place, GRAD_ROWS[3], dwr[pl.ds(r, 16), pl.ds(yy * 128, 128)])
                    else:
                        put_rows(grad, own_place, GRAD_ROWS[3], jnp.zeros((16, 128), bf16))
                        put_rows(grad, their_place, GRAD_ROWS[3], jnp.zeros((16, 128), bf16))
    jobs[2].start(2)

    jobs[0].forward()
    for yy in range(4):
        net.arrive(go.at[yy], s_gr + yy)
    for h in range(3):
        backward_head(h, q, kv, own_qpos, kpos, lse, go, dkv, dq_t)
        if h == 0:
            jobs[1].forward()
        if h == 1:
            jobs[0].finish(2)
            jobs[0].start(1)
    dkv_s[...] = dkv[1 - c].astype(bf16)
    s_k = swap(dkv_s, dkv_r)
    dq = dq_t[...].T * 0.125
    for yy in range(4):
        r = pl.ds(yy * 128, 128)
        v = dq[yy * 128 : (yy + 1) * 128, :]
        dp[r, 384:512] = turn(v[:, :128], cosine[yy], -sine[yy]).astype(bf16)
        dp[r, 512:] = turn(v[:, 128:], cosine[yy], -sine[yy]).astype(bf16)
    jobs[2].forward()
    net.arrive(dkv_r, s_k)
    for yy in range(4):
        r = pl.ds(yy * 128, 128)
        v = dkv[c, r, :] + dkv_r[r, :].astype(f32)
        dp[r, :128] = turn(v[:, :128], cosine[yy], -sine[yy]).astype(bf16)
        dp[r, 128:256] = turn_first_half(v[:, 128:256], cosine[yy], -sine[yy]).astype(bf16)
        dp[r, 256:384] = v[:, 256:].astype(bf16)
    dw[0] = dot(xnt[...], dp[:, :384]).astype(bf16).reshape(16, 48, 384)
    dw[1, :, :, :256] = dot(xnt[...], dp[:, 384:]).astype(bf16).reshape(16, 48, 256)
    dw[1, :, :, 256:] = jnp.zeros((16, 48, 128), bf16)
    s_w = swap(dw.at[1 - c], dw_r)
    jobs[1].finish(2)
    jobs[1].start(1)
    net.arrive(dw_r, s_w)
    dw_sum[...] = (dw[c].astype(f32) + dw_r[...].astype(f32)).astype(bf16)
    s_p, s_pr = net.take(16), net.take(16)
    for i, place in others:
        net.send(dw_sum.at[row_block(place)], plane.at[rb], s_p + i, s_pr + rb, device(place))
    a_kv = dot_nt(dp[:, :384], watt[0].reshape(768, 384))
    a_q = dot_nt(dp[:, 384:], watt[1, :, :, :256].reshape(768, 256))
    a_s[...] = (a_kv + a_q).astype(bf16).reshape(4, 128, 768)
    i_a = net.take(3)
    for kind, step in enumerate((1, 3, 2)):
        net.send(a_s.at[(y + step) % 4], a_got.at[kind], i_a + kind, i_a + kind, device(moved(at, "y", step)))
    jobs[0].finish(1)
    jobs[0].start(0)
    jobs[2].finish(2)
    jobs[2].start(1)
    for kind in range(3):
        net.arrive(a_got.at[kind], i_a + kind)
    a = a_s[y].astype(f32) + a_got[0].astype(f32) + a_got[1].astype(f32) + a_got[2].astype(f32)
    a_sum[...] = a.astype(bf16)
    i_z = net.take(1)
    net.send_or_keep(a_sum, a_own, i_z, i_z, device(at, zl=c, c=zl), zl == c)
    jobs[1].finish(1)
    jobs[1].start(0)
    total = dw_sum[rb].astype(f32)
    for _, place in others:
        r = row_block(place)
        net.arrive(plane.at[r], s_pr + r)
        total = total + plane[r].astype(f32)
    for cb in range(3):
        tall[cb] = total[:, cb * 128 : (cb + 1) * 128]
    jobs[2].finish(1)
    jobs[2].start(0)
    net.arrive(a_own, i_z)
    v = xb[c].astype(f32)
    r1 = inverse_rms(v)
    scaled = v * r1
    a = a_own[...].astype(f32)
    input_grad[...] = por[own_rows, :] + r1 * (a - scaled * jnp.mean(a * scaled, axis=-1, keepdims=True))
    for j in jobs:
        j.finish(0)
    lowest = [j.levels[3] for j in jobs]
    for cb in range(3):
        for m in range(3):
            tall[3 + m * 3 + cb] = get_rows(lowest, (cb,), GRAD_ROWS[m]).astype(f32)
        tall[12, pl.ds(cb * 16, 16), :] = get_rows(lowest, (cb,), GRAD_ROWS[3]).astype(f32)
    for s in range(8):
        for unit in range(13):
            back_s[s, pl.ds(unit * 6, 6), :] = tall[unit, pl.ds(s * 6, 6), :]
        back_s[s, pl.ds(78, 2), :] = jnp.zeros((2, 128), f32)
    back_p[...] = back_s[...].astype(bf16)
    s_b, s_br = net.take(8), net.take(8)
    slot = c * 4 + y
    for s in range(8):
        mine = jnp.logical_and(y * 2 + zl == s, zl == c)
        net.send_or_keep(
            back_p.at[s], back.at[slot], s_b + s, s_br + slot, device(at, y=s // 2, zl=s % 2, c=zl), mine
        )
    for s in range(8):
        net.arrive(back.at[s], s_br + s)
    grads[...] = back[...].astype(f32)
    net.drain()


VM = pl.BlockSpec(memory_space=pltpu.VMEM)
SEMS = 340


def layer(*args):
    f, h = f32, bf16

    def blocks(lead, rows):
        return (lead + (rows, 128), h)

    scratch = [
        *[(a.shape, a.dtype) for a in args[:5]], (args[7].shape, args[7].dtype),
        ((8, 32, 128), f), ((8, 32, 128), h), ((8, 32, 128), h), ((8, 32, 128), f),
        ((8, 64, 128), f), ((8, 64, 128), h), ((8, 64, 128), h), ((8, 64, 128), f), ((13, 48, 128), f),
        ((2, 16, 48, 384), h), *[blocks((3, 4, 4, 4), r) for r in WEIGHT_JOBS], ((2, 2, 384, 384), h),
        ((4, 128, 768), h), ((4, 128, 768), h), ((768, 512), h), ((4, 128, 128), f),
        ((4, 128, 128), f), ((2, 4, 128, 128), f), ((2, 4, 8, 128), f), ((2, 512, 384), h), ((512, 256), h),
        ((8, 512), f),
        ((192, 512), f), ((4, 128, 192), h), ((2, 2, 128, 192), h),
        ((2, 128, 768), h), ((2, 128, 768), h), ((256, 768), f), ((256, 768), f), ((256, 768), f),
        ((256, 768), h), ((768, 256), h), ((768, 256), h), ((4, 256, 384), f), ((4, 256, 384), f), ((4, 256, 384), h),
        ((256, 768), f), ((256, 768), f), ((256, 768), f), ((128, 768), f), ((256, 768), h), ((2, 384, 384), h),
        ((384, 384), h), ((2, 2, 128, 192), h), *[blocks((3, 4, 4, 4), r) for r in GRAD_JOBS],
        ((4, 128, 192), h), ((2, 512, 384), f), ((512, 384), h), ((512, 384), h), ((256, 512), f), ((512, 640), h),
        ((2, 16, 48, 384), h), ((16, 48, 384), h), ((16, 48, 384), h), ((16, 48, 384), h),
        ((4, 128, 768), h), ((3, 128, 768), h), ((128, 768), h), ((128, 768), h),
        ((8, 80, 128), f), ((8, 80, 128), h), ((8, 80, 128), h),
    ]
    for r in GRAD_JOBS:
        scratch += [blocks((3,) + (4,) * k, r) for k in (2, 1, 0)]
        scratch += [blocks((3, 3) + (4,) * k, r) for k in (2, 1, 0)]
        scratch += [blocks((3, 4, 4), r)]
    return pl.pallas_call(
        layer_body,
        out_shape=(
            jax.ShapeDtypeStruct((128, 768), bf16),
            jax.ShapeDtypeStruct((128, 768), f32),
            jax.ShapeDtypeStruct((8, 80, 128), f32),
        ),
        in_specs=[pl.BlockSpec(memory_space=pl.ANY)] * len(args),
        out_specs=(VM,) * 3,
        scratch_shapes=[pltpu.VMEM(s, t) for s, t in scratch]
        + [pltpu.SemaphoreType.DMA((SEMS,))] * 2
        + [pltpu.SemaphoreType.DMA((8,))],
        compiler_params=pltpu.CompilerParams(collective_id=0, has_side_effects=True, vmem_limit_bytes=60 << 20),
    )(*args)


def adam_step(master, gradient, moment_one, moment_two, rate_value, decay_value):
    moment_one = BETA_FIRST * moment_one + (1.0 - BETA_FIRST) * gradient
    moment_two = BETA_SECOND * moment_two + (1.0 - BETA_SECOND) * gradient * gradient
    first_hat = moment_one / (1.0 - BETA_FIRST**STEP)
    second_hat = moment_two / (1.0 - BETA_SECOND**STEP)
    updated = master - rate_value * (
        first_hat / (jnp.sqrt(second_hat) + ADAM_EPS) + decay_value * master
    )
    return (moment_one, moment_two, updated)


def owner_body(
    grads, outputs, input_grad,
    qkv, qkv_m, qkv_s, out, out_m, out_s, gu, gu_m, gu_s, dt, dt_m, dt_s, gains, gains_m, gains_s,
    outputs_o, input_grad_o,
    qkv_mo, qkv_so, qkv_o, out_mo, out_so, out_o, gu_mo, gu_so, gu_o, dt_mo, dt_so, dt_o,
    gains_mo, gains_so, gains_o,
):
    outputs_o[...] = outputs[...]
    input_grad_o[...] = input_grad[...]

    def unit(slot, u):
        return grads[slot, pl.ds(u * 6, 6), :]

    eye = lax.broadcasted_iota(jnp.int32, (6, 6), 0) == lax.broadcasted_iota(jnp.int32, (6, 6), 1)
    g_low = gains[...].astype(bf16).astype(f32)
    g_one = jnp.sum(jnp.where(eye, g_low[0:1, :], 0.0), axis=1, keepdims=True)
    g_two = jnp.sum(jnp.where(eye, g_low[1:2, :], 0.0), axis=1, keepdims=True)

    def update(refs, new, columns, gradient, rate, decay):
        w, m, s = refs
        values = adam_step(w[:, columns], gradient, m[:, columns], s[:, columns], rate, decay)
        for to, v in zip(new, values):
            to[:, columns] = v

    def low_times(w, columns, gradient):
        return jnp.sum(w[:, columns].astype(bf16).astype(f32) * gradient, axis=1, keepdims=True)

    def join(a, b):
        return jnp.concatenate([a, b], axis=1)

    rate = D ** (-0.5)
    sum_one = jnp.zeros((6, 1), f32)
    for pair in range(2):
        e, o = 2 * pair, 2 * pair + 1
        u = {(s, k): unit(s, k) for s in (e, o, 4 + e, 4 + o) for k in range(3)}
        tiles = {
            0: (u[4 + e, 0], join(u[4 + e, 1][:, :64], u[4 + o, 0][:, :64]), join(u[4 + o, 0][:, 64:], u[4 + o, 1][:, :64])),
            768: (u[e, 0], join(u[e, 1][:, :64], u[o, 0][:, :64]), join(u[o, 0][:, 64:], u[o, 1][:, :64])),
            1536: (join(u[e, 1][:, 64:], u[e, 2][:, :64]), join(u[e, 2][:, 64:], u[o, 1][:, 64:]), u[o, 2]),
        }
        for first, three in tiles.items():
            for k, t in enumerate(three):
                columns = pl.ds(first + pair * 384 + k * 128, 128)
                sum_one = sum_one + low_times(qkv, columns, t)
                update((qkv, qkv_m, qkv_s), (qkv_mo, qkv_so, qkv_o), columns, t * g_one, rate, WEIGHT_DECAY)
    sum_two = jnp.zeros((6, 1), f32)
    for slot in range(8):
        for cb in range(3):
            f = slot * 384 + cb * 128
            for half in range(2):
                columns = pl.ds(half * 3072 + f, 128)
                t = unit(slot, 3 + half * 3 + cb)
                sum_two = sum_two + low_times(gu, columns, t)
                update((gu, gu_m, gu_s), (gu_mo, gu_so, gu_o), columns, t * g_two, rate, WEIGHT_DECAY)
            update(
                (dt, dt_m, dt_s), (dt_mo, dt_so, dt_o), pl.ds(f, 128), unit(slot, 9 + cb), FF ** (-0.5), WEIGHT_DECAY
            )
        if slot % 4 < 3:
            update(
                (out, out_m, out_s), (out_mo, out_so, out_o), pl.ds((slot // 4) * 384 + (slot % 4) * 128, 128),
                unit(slot, 12), (H * HD * 32 // LEN) ** (-0.5), WEIGHT_DECAY,
            )
    rows = [jnp.sum(jnp.where(eye, v, 0.0), axis=0, keepdims=True) for v in (sum_one, sum_two)]
    values = adam_step(gains[...], jnp.concatenate(rows, axis=0), gains_m[...], gains_s[...], GAIN_RATE, 0.0)
    for to, v in zip((gains_mo, gains_so, gains_o), values):
        to[...] = v


def owners_step(*args):
    shapes = [(args[1].shape, bf16), (args[2].shape, f32)]
    for first in range(3, 18, 3):
        shapes += [(args[first].shape, f32)] * 3
    return pl.pallas_call(
        owner_body,
        out_shape=tuple(jax.ShapeDtypeStruct(s, t) for s, t in shapes),
        in_specs=[VM] * len(args),
        out_specs=(VM,) * len(shapes),
    )(*args)


def body(
    inputs, positions, output_grad,
    qkv_weight, qkv_first, qkv_second, out_weight, out_first, out_second,
    gate_up_weight, gate_up_first, gate_up_second, down_weight, down_first, down_second,
    norm_gains, gains_first, gains_second,
):
    outputs, input_grad, grads = layer(
        qkv_weight, out_weight, gate_up_weight, down_weight.T, norm_gains,
        inputs.reshape(128, D), output_grad.reshape(128, D), positions,
    )
    new = owners_step(
        grads, outputs, input_grad,
        qkv_weight, qkv_first, qkv_second, out_weight, out_first, out_second,
        gate_up_weight, gate_up_first, gate_up_second, down_weight.T, down_first.T, down_second.T,
        norm_gains, gains_first, gains_second,
    )
    return (
        new[0].reshape(1, 128, D), new[1].reshape(1, 128, D), *new[2:11],
        *(v.T for v in new[11:14]), *new[14:],
    )


def solution(mesh):
    token = P("dp", "ctx", None)
    rows, columns = P(("dp", "ctx"), None), P(None, ("dp", "ctx"))
    return jax.shard_map(
        body,
        mesh=mesh,
        in_specs=(token, P("dp", "ctx"), token) + (rows,) * 9 + (columns,) * 6,
        out_specs=(token, token) + (rows,) * 9 + (columns,) * 6,
        check_vma=False,
    )
```

```python
import math

import jax
import jax.numpy as jnp
from jax import lax
from jax.experimental import pallas as pl
from jax.experimental.pallas import tpu as pltpu
from jax.sharding import PartitionSpec as P

D = 768
H = 12
HD = 64
FF = 3072
LEN = 1024
STEP = 10

NORM_EPS = 1e-05
ROPE_BASE = 10000.0
BETA_FIRST = 0.9
BETA_SECOND = 0.95
ADAM_EPS = 1e-08
WEIGHT_DECAY = 0.1
GAIN_RATE = 1.2
MASKED = -1e30

MESH = pl.DeviceIdType.MESH
bf16, f32 = jnp.bfloat16, jnp.float32

ORDERS = (("x", "y", "z"), ("y", "z", "x"), ("z", "x", "y"))
WEIGHT_JOBS = (16, 48, 48, 48)
GRAD_JOBS = (48, 48, 64)
WEIGHT_ORDERS = (ORDERS,) * 4
GRAD_ORDERS = (ORDERS,) * 3


def here():
    dp, ctx = lax.axis_index("dp"), lax.axis_index("ctx")
    return dict(x=(dp // 2) % 4, y=ctx // 2, z=(dp // 8) * 2 + ctx % 2, c=dp % 2)


def low_z(at):
    return at["z"] % 2


def device(at, zl=None, **moved):
    at = dict(at, **moved)
    if zl is not None:
        at["z"] = (at["z"] // 2) * 2 + zl
    return ((at["z"] // 2) * 8 + at["x"] * 2 + at["c"], at["y"] * 2 + at["z"] % 2)


def moved(at, axis, step):
    return dict(at, **{axis: (at[axis] + step + 4) % 4})


def row_block(at):
    return (at["z"] // 2) * 8 + at["x"] * 2 + at["z"] % 2


def group_of(at):
    out = []
    me = at["c"] * 8 + at["y"] * 2 + low_z(at)
    for k in range(1, 16):
        other = (me + k) % 16
        out.append(device(at, c=other // 8, y=(other // 2) % 4, zl=other % 2))
    for k in range(1, 4):
        out.append(device(at, x=(at["x"] + k) % 4))
    other_half = dict(at, z=(at["z"] + 2) % 4)
    for low in range(2):
        out.append(device(other_half, zl=low))
    return out


def signal_all(peers):
    barrier = pltpu.get_barrier_semaphore()
    for p in peers:
        pl.semaphore_signal(barrier, inc=1, device_id=p, device_id_type=MESH)


def wait_all(peers):
    pl.semaphore_wait(pltpu.get_barrier_semaphore(), len(peers))


class Net:
    def __init__(self, at, send_sem, recv_sem):
        self.at, self.send_sem, self.recv_sem = at, send_sem, recv_sem
        self.used = 0
        self.ends = []

    def take(self):
        self.used += 1
        return self.used - 1

    def send(self, src, dst, i, to, r=None):
        pltpu.make_async_remote_copy(
            src_ref=src, dst_ref=dst, send_sem=self.send_sem.at[i], recv_sem=self.recv_sem.at[i if r is None else r],
            device_id=to, device_id_type=MESH,
        ).start()

    def send_or_keep(self, src, dst, i, to, mine):
        pl.when(jnp.logical_not(mine))(lambda: self.send(src, dst, i, to))
        pl.when(mine)(lambda: pltpu.make_async_copy(src, dst, self.recv_sem.at[i]).start())

    def left(self, view, i):
        self.ends.append((None, view, i))

    def left_if(self, condition, view, i):
        self.ends.append((condition, view, i))

    def arrive(self, view, i):
        pltpu.make_async_copy(view, view, self.recv_sem.at[i]).wait()

    def drain(self):
        for condition, view, i in self.ends:
            wait = pltpu.make_async_copy(view, view, self.send_sem.at[i]).wait
            if condition is None:
                wait()
            else:
                pl.when(condition)(wait)


class Gather:
    def __init__(self, net, ref, orders):
        self.net, self.at, self.ref, self.orders = net, net.at, ref, orders
        self.sems = [net.take() for _ in range(4)]
        views = (ref.at[0, 0:3, 0:3, 0], ref.at[0, 0:3, 0:3], ref.at[0:2, 0:3], ref.at[0, 0:3])
        self.views = views
        for view, i in zip(views, self.sems):
            net.left(view, i)

    def view(self, part, at, phase):
        a1, a2, a3 = self.orders[part]
        return self.ref.at[(part, at[a3], at[a2], at[a1])[: 4 - phase]]

    def send(self, part, phase, at, axis, step, i):
        v = self.view(part, at, phase)
        self.net.send(v, v, i, device(moved(self.at, axis, step)))

    def start(self, phase):
        for step in (2, 1, 3) if phase < 2 else (1, 3):
            for part in range(3):
                self.send(part, phase, self.at, self.orders[part][phase], step, self.sems[phase])

    def forward(self):
        d = 1 - 2 * self.at["c"]
        self.net.arrive(self.views[2], self.sems[2])
        for part in range(3):
            axis = self.orders[part][2]
            self.send(part, 2, moved(self.at, axis, -d), axis, d, self.sems[3])

    def finish(self, phase):
        k = phase if phase < 2 else 3
        self.net.arrive(self.views[k], self.sems[k])


class Scatter:
    def __init__(self, net, levels, got, turned, orders):
        self.net, self.at, self.orders = net, net.at, orders
        self.levels, self.got, self.turned = levels, got, turned
        self.sems = [net.take() for _ in range(4)]
        self.views = (got[2], got[1], got[0].at[0:2], got[0].at[2])
        for view, i in zip(self.views, self.sems):
            net.left(view, i)

    def level(self, part, phase, i):
        return self.levels[2 - phase].at[part, i]

    def slot(self, part, phase, kind):
        return self.got[2 - phase].at[kind, part]

    def go(self, src, part, phase, kind, axis, step, s, r):
        self.net.send(src, self.slot(part, phase, kind), s, device(moved(self.at, axis, step)), r)

    def add(self, to, refs, phase):
        def one(index):
            total = refs[0][index].astype(f32)
            for r in refs[1:]:
                total = total + r[index].astype(f32)
            to[index] = total.astype(to.dtype)

        if phase == 2:
            pl.loop(0, 4)(lambda b: one((b,)))
        else:
            one(...)

    def start(self, phase, parts=range(3)):
        d = 1 - 2 * self.at["c"]
        i = self.sems[phase]
        for part in parts:
            axis = self.orders[part][phase]
            me = self.at[axis]
            if phase < 2:
                for kind, step in enumerate((2, 1, 3)):
                    self.go(self.level(part, phase, (me + step) % 4), part, phase, kind, axis, step, i, i)
            else:
                self.go(self.level(part, phase, (me + 2) % 4), part, phase, 2, axis, 4 - d, i, self.sems[3])
                self.go(self.level(part, phase, (me + d + 4) % 4), part, phase, 0, axis, d, i, i)

    def forward(self):
        d = 1 - 2 * self.at["c"]
        self.net.arrive(self.views[3], self.sems[3])
        for part in range(3):
            axis = self.orders[part][2]
            me = self.at[axis]
            to = self.turned.at[part]
            self.add(to, [self.level(part, 2, (me - d + 4) % 4), self.slot(part, 2, 2)], 2)
            self.go(to, part, 2, 1, axis, 4 - d, self.sems[3], self.sems[2])

    def finish(self, phase):
        self.net.arrive(self.views[phase], self.sems[phase])
        for part in range(3):
            me = self.at[self.orders[part][phase]]
            kinds = (0, 1, 2) if phase < 2 else (0, 1)
            to = self.levels[3 - phase].at[part]
            self.add(to, [self.level(part, phase, me)] + [self.slot(part, phase, k) for k in kinds], phase)


def dot(a, b):
    return jnp.dot(a, b, preferred_element_type=f32)


def dot_nt(a, b):
    return lax.dot_general(a, b, (((1,), (1,)), ((), ())), preferred_element_type=f32)


def dot_tn(a, b):
    return lax.dot_general(a, b, (((0,), (0,)), ((), ())), preferred_element_type=f32)


def inverse_rms(v):
    return lax.rsqrt(jnp.mean(v * v, axis=-1, keepdims=True) + NORM_EPS)


def tables(place, freq):
    angle = place * freq
    lane = lax.broadcasted_iota(jnp.int32, place.shape, 1)
    sine = jnp.sin(angle)
    return jnp.cos(angle), jnp.where(lane % 64 < 32, -sine, sine)


def turn(v, cosine, sine):
    lane = lax.broadcasted_iota(jnp.int32, v.shape, 1)
    swapped = jnp.where(lane % 64 < 32, pltpu.roll(v, 96, 1), pltpu.roll(v, 32, 1))
    return v * cosine + swapped * sine


def turn_first_half(v, cosine, sine):
    lane = lax.broadcasted_iota(jnp.int32, v.shape, 1)
    return jnp.where(lane < 64, turn(v, cosine, sine), v)


def ffn_index(orders, part, y, x, z):
    place = dict(x=x, y=y, z=z)
    a1, a2, a3 = orders[part]
    return (part, place[a3], place[a2], place[a1])


WEIGHT_ROWS = ((1, 0, 48), (2, 0, 48), (3, 0, 48), (0, 0, 16))
GRAD_ROWS = ((1, 0, 48), (2, 0, 48), (0, 0, 48), (2, 48, 16))


def put_weight(refs, matrix, place, value):
    job, first, count = WEIGHT_ROWS[matrix]
    refs[job][ffn_index(WEIGHT_ORDERS[job], *place) + (pl.ds(first, count), slice(None))] = value


def get_weight(refs, matrix, place):
    job, first, count = WEIGHT_ROWS[matrix]
    return refs[job][ffn_index(WEIGHT_ORDERS[job], *place) + (pl.ds(first, count), slice(None))]


def put_grad(refs, matrix, place, value):
    job, first, count = GRAD_ROWS[matrix]
    refs[job][ffn_index(GRAD_ORDERS[job], *place) + (pl.ds(first, count), slice(None))] = value


def get_sum(refs, matrix, part):
    job, first, count = GRAD_ROWS[matrix]
    return refs[job][part, pl.ds(first, count), :].astype(f32)


def rows_of(pick):
    return jnp.concatenate([pick(x, zh * 2 + zl) for zh in range(2) for x in range(4) for zl in range(2)], axis=0)


def row_blocks(value):
    for zh in range(2):
        for x in range(4):
            for zl in range(2):
                r = (zh * 8 + x * 2 + zl) * 48
                yield x, zh * 2 + zl, value[r : r + 48, :]


def ffn_panel(wf, matrix, p):
    return jnp.concatenate(
        [rows_of(lambda x, z: get_weight(wf, matrix, (p, y, x, z))) for y in range(4)], axis=1
    )


def store_ffn_panel(g, matrix, p, value):
    for x, z, rows in row_blocks(value):
        for y in range(4):
            put_grad(g, matrix, (p, y, x, z), rows[:, y * 128 : (y + 1) * 128])


def attention_panel(wide, narrow, which):
    return rows_of(lambda x, z: jnp.concatenate([wide[which, x, z], narrow[which, z, x]], axis=1))


def head_parts(h, kv):
    k = jnp.concatenate([kv[0, :, h * 64 : (h + 1) * 64], kv[1, :, h * 64 : (h + 1) * 64]], axis=0)
    o = 192 + h * 64
    v = jnp.concatenate([kv[0, :, o : o + 64], kv[1, :, o : o + 64]], axis=0)
    return k, v


def query_positions(qpos, half):
    return jnp.concatenate([qpos[half * 2], qpos[half * 2 + 1]], axis=1)[0:1, :]


def masked_scores(k, q_part, kpos, q_row):
    s = dot_nt(k, q_part)
    kp = kpos[...].reshape(1024, 128)
    allowed = jnp.concatenate([kp, kp], axis=1) <= q_row
    return jnp.where(allowed, s, MASKED)


def forward_head(h, q, kv, qpos, kpos, lse, mixed_t):
    k, v = head_parts(h, kv)
    for half in range(2):
        q_part = q[pl.ds(half * 256, 256), h * 64 : (h + 1) * 64]
        s = masked_scores(k, q_part, kpos, query_positions(qpos, half))
        highest = jnp.max(s, axis=0, keepdims=True)
        e = jnp.exp(s - highest)
        total = jnp.sum(e, axis=0, keepdims=True)
        p = (e * (1.0 / total)).astype(bf16)
        mixed_t[pl.ds(h * 64, 64), pl.ds(half * 256, 256)] = dot_tn(v, p)
        lse[pl.ds(h, 1), pl.ds(half * 256, 256)] = highest + jnp.log(total)


def backward_head(h, q, kv, qpos, kpos, lse, go, dkv, dq_t):
    k, v = head_parts(h, kv)
    for half in range(2):
        rows = pl.ds(half * 256, 256)
        q_part = q[rows, h * 64 : (h + 1) * 64]
        g_part = go[pl.ds(half * 2, 2), :, h * 64 : (h + 1) * 64].reshape(256, 64)
        s = masked_scores(k, q_part, kpos, query_positions(qpos, half))
        p = jnp.exp(s - lse[pl.ds(h, 1), rows])
        dp = dot_nt(v, g_part)
        centre = jnp.sum(p * dp, axis=0, keepdims=True)
        ds = (p * (dp - centre)).astype(bf16)
        dv = dot(p.astype(bf16), g_part)
        dk = dot(ds, q_part)
        dq_t[pl.ds(h * 64, 64), rows] = dot_tn(k, ds)
        for cc in range(2):
            dkv[cc, :, h * 64 : (h + 1) * 64] += dk[cc * 512 : (cc + 1) * 512]
            dkv[cc, :, 192 + h * 64 : 192 + (h + 1) * 64] += dv[cc * 512 : (cc + 1) * 512]


def as_column(eye, row):
    return jnp.sum(jnp.where(eye, row, 0.0), axis=1, keepdims=True)


def low_gains(gains):
    eye = lax.broadcasted_iota(jnp.int32, (6, 6), 0) == lax.broadcasted_iota(jnp.int32, (6, 6), 1)
    g_low = gains[...].astype(bf16).astype(f32)
    return as_column(eye, g_low[0:1, :]), as_column(eye, g_low[1:2, :])


def cut_attention(qkv, g_one, positions, stage):
    place = positions[...]
    place = jnp.concatenate([(place // 64).astype(f32), (place % 64).astype(f32)], axis=0)
    zero = jnp.zeros((6, 64), f32)
    for yy in range(4):
        o = yy * 192
        q_y = qkv[:, o : o + 192].astype(bf16).astype(f32) * g_one
        k_y = qkv[:, 768 + o : 768 + o + 192].astype(bf16).astype(f32) * g_one
        v_y = qkv[:, 1536 + o : 1536 + o + 192].astype(bf16).astype(f32) * g_one
        stage[yy, pl.ds(0, 6), :] = k_y[:, :128]
        stage[yy, pl.ds(6, 6), :] = jnp.concatenate([k_y[:, 128:], v_y[:, :64]], axis=1)
        stage[yy, pl.ds(12, 6), :] = v_y[:, 64:]
        stage[4 + yy, pl.ds(0, 6), :] = q_y[:, :128]
        stage[4 + yy, pl.ds(6, 6), :] = jnp.concatenate([q_y[:, 128:], zero], axis=1)
        stage[4 + yy, pl.ds(12, 6), :] = jnp.zeros((6, 128), f32)
    for slot in range(8):
        stage[slot, pl.ds(18, 2), :] = place
        stage[slot, pl.ds(20, 12), :] = jnp.zeros((12, 128), f32)


def cut_rest(out, gu, dt, g_two, stage):
    def put(slot, unit, v):
        stage[slot, pl.ds(unit * 6, 6), :] = v

    for slot in range(8):
        for cb in range(3):
            f = slot * 384 + cb * 128
            put(slot, cb, gu[:, f : f + 128].astype(bf16).astype(f32) * g_two)
            put(slot, 3 + cb, gu[:, 3072 + f : 3072 + f + 128].astype(bf16).astype(f32) * g_two)
            put(slot, 6 + cb, dt[:, f : f + 128])
        cc, yy = slot // 4, slot % 4
        if yy < 3:
            put(slot, 9, out[:, cc * 384 + yy * 128 : cc * 384 + (yy + 1) * 128])
        else:
            put(slot, 9, jnp.zeros((6, 128), f32))
        stage[slot, pl.ds(60, 4), :] = jnp.zeros((4, 128), f32)


def layer_body(
    qkv_h, out_h, gu_h, dt_h, gains_h, x_h, og_h, positions_h,
    outputs, input_grad, grads,
    qkv, out, gu, dt, gains, positions,
    stage_a, pieces_a, recv_a, wide_a, stage_f, pieces_f, recv_f, wide_f, tall,
    wide_w, narrow_w, wf0, wf1, wf2, wf3, wo, xg, xn, xnt, cosine, sine, kpos, qpos, kv, q, lse,
    mixed_t, mixed_s, mixed,
    xb, ogb, po, por, mid, n2, n2t, ogt, act, slope, hid, acc, accr, outp, outr, branch, dwo, dwr, gm, g0, g1, g2,
    go, dkv, dkv_s, dkv_r, dq_t, dp, wide_d, narrow_d, wide_r, narrow_r, wide_t, narrow_t,
    wide_1, narrow_1, wide_2, narrow_2, wide_0, narrow_0, a_s, a_got, a_on, a_sum, a_own, back_s, back_p, back,
    *rest,
):
    per_job, (send_sem, recv_sem, load_sem) = rest[:-3], rest[-3:]
    at = here()
    c, y, zl = at["c"], at["y"], low_z(at)
    d = 1 - 2 * c
    net = Net(at, send_sem, recv_sem)
    peers = group_of(at)
    partner = device(at, c=1 - c)
    rb = row_block(at)
    own_rows = pl.ds(pl.multiple_of(c * 128, 128), 128)
    their_rows = pl.ds(pl.multiple_of((1 - c) * 128, 128), 128)

    def swap(src, dst):
        i = net.take()
        net.send(src, dst, i, partner)
        net.left(src, i)
        return i

    def to_line(axis, pick, slot):
        i = net.take()
        for kind, step in enumerate((2, 1, 3)):
            net.send(pick(step), slot(kind), i, device(moved(at, axis, step)))
        return i

    loads = [
        pltpu.make_async_copy(src, dst, load_sem.at[i])
        for i, (src, dst) in enumerate(
            (
                (qkv_h, qkv), (gains_h, gains), (positions_h, positions), (x_h, xb.at[c]),
                (gu_h, gu), (dt_h, dt), (out_h, out), (og_h, ogb.at[c]),
            )
        )
    ]
    for copy in loads:
        copy.start()
    signal_all(peers)
    for copy in loads[:3]:
        copy.wait()
    g_one, g_two = low_gains(gains)
    cut_attention(qkv, g_one, positions, stage_a)
    pieces_a[...] = stage_a[...].astype(bf16)
    for copy in loads[3:]:
        copy.wait()
    cut_rest(out, gu, dt, g_two, stage_f)
    pieces_f[...] = stage_f[...].astype(bf16)
    wait_all(peers)

    source = y * 2 + zl

    def to_group(pieces, recv):
        i = net.take()
        for cc in range(2):
            for yy in range(4):
                mine = jnp.logical_and(zl == c, jnp.logical_and(y == yy, c == cc))
                net.send_or_keep(pieces.at[cc * 4 + yy], recv.at[source], i, device(at, y=yy, zl=c, c=cc), mine)
        net.left_if(zl == c, pieces.at[0:7], i)
        net.left_if(zl != c, pieces, i)
        return i

    r_a = to_group(pieces_a, recv_a)
    r_f = to_group(pieces_f, recv_f)
    i_x = net.take()
    net.send_or_keep(xb.at[c], xg.at[y], i_x, device(at, zl=c, c=zl), zl == c)
    net.left_if(zl != c, xb.at[c], i_x)
    i_xb = swap(xb.at[c], xb.at[c])
    i_ob = swap(ogb.at[c], ogb.at[c])

    net.arrive(recv_a, r_a)
    wide_a[...] = recv_a[...].astype(f32)
    for unit in range(3):
        for s in range(8):
            tall[unit, pl.ds(s * 6, 6), :] = wide_a[s, pl.ds(unit * 6, 6), :]
    x, z = at["x"], at["z"]
    wide_w[c, x, z] = jnp.concatenate([tall[0], tall[1]], axis=1).astype(bf16)
    narrow_w[c, z, x] = tall[2].astype(bf16)
    block = wide_w.at[c, x, z]
    i_wz = to_line("z", lambda step: block, lambda kind: block)
    net.left(wide_w.at[0, 0, 0:3], i_wz)
    thin = narrow_w.at[c, z, x]
    i_nx = to_line("x", lambda step: thin, lambda kind: thin)
    net.left(narrow_w.at[0, 0, 0:3], i_nx)
    net.arrive(xg.at[y], i_x)
    i_y, i_y2 = net.take(), net.take()
    for step in (1, 3):
        net.send(xg.at[y], xg.at[y], i_y, device(moved(at, "y", step)))
    net.left(xg.at[0:2], i_y)

    net.arrive(recv_f, r_f)
    wide_f[...] = recv_f[...].astype(f32)
    for unit in range(10):
        for s in range(8):
            tall[3 + unit, pl.ds(s * 6, 6), :] = wide_f[s, pl.ds(unit * 6, 6), :]
    wf = (wf0, wf1, wf2, wf3)
    for cb in range(3):
        place = (cb, y, x, z)
        for m in range(3):
            put_weight(wf, m, place, tall[3 + m * 3 + cb].astype(bf16))
        put_weight(wf, 3, place, tall[12, pl.ds(cb * 16, 16), :].astype(bf16))
    jobs = [Gather(net, ref, orders) for ref, orders in zip(wf, WEIGHT_ORDERS)]
    for j in jobs:
        j.start(0)
    net.arrive(wide_w.at[0, 0, 0:3], i_wz)
    row = wide_w.at[c, x]
    i_wx = to_line("x", lambda step: row, lambda kind: row)
    net.left(wide_w.at[0, 0:3], i_wx)
    net.arrive(narrow_w.at[0, 0, 0:3], i_nx)
    thin_row = narrow_w.at[c, z]
    i_nz = to_line("z", lambda step: thin_row, lambda kind: thin_row)
    net.left(narrow_w.at[0, 0:3], i_nz)

    for s in range(8):
        row = wide_a[s, pl.ds(18, 1), :] * 64.0 + wide_a[s, pl.ds(19, 1), :]
        rows = jnp.broadcast_to(row, (128, 128))
        kpos[s % 2, s // 2] = rows.T
        qpos[s % 2, s // 2] = rows[:8]
    lane = lax.broadcasted_iota(jnp.int32, (1, 128), 1) % 32
    freq = jnp.exp(lane.astype(f32) * (-2.0 * math.log(ROPE_BASE) / HD))
    for yy in range(4):
        cosine[yy], sine[yy] = tables(kpos[c, yy], freq)
    net.arrive(xg.at[0:2], i_y)
    behind = xg.at[(y - d + 4) % 4]
    net.send(behind, behind, i_y2, device(moved(at, "y", d)))
    net.left(xg.at[0], i_y2)
    for j in jobs:
        j.finish(0)
        j.start(1)

    def normalize(yy):
        v = xg[yy].astype(f32)
        xn[yy] = (v * inverse_rms(v)).astype(bf16)

    for step in (0, 1, 3):
        normalize((y + step) % 4)
    net.arrive(xg.at[0], i_y2)
    normalize((y + 2) % 4)
    jobs[0].finish(1)
    jobs[0].start(2)
    jobs[1].finish(1)
    jobs[1].start(2)
    jobs[2].finish(1)
    jobs[2].start(2)
    jobs[3].finish(1)
    jobs[3].start(2)
    net.arrive(wide_w.at[0, 0:3], i_wx)
    net.arrive(narrow_w.at[0, 0:3], i_nz)
    e_w, e_n = swap(wide_w.at[c], wide_w.at[c]), swap(narrow_w.at[c], narrow_w.at[c])
    net.arrive(wide_w.at[1 - c], e_w)
    net.arrive(narrow_w.at[1 - c], e_n)

    w_kv = attention_panel(wide_w, narrow_w, 0)
    w_q = attention_panel(wide_w, narrow_w, 1)[:, :256]
    for yy in range(4):
        r = pl.ds(yy * 128, 128)
        kv_y = dot(xn[yy], w_kv)
        kv[c, r, :128] = turn(kv_y[:, :128], cosine[yy], sine[yy]).astype(bf16)
        kv[c, r, 128:256] = turn_first_half(kv_y[:, 128:256], cosine[yy], sine[yy]).astype(bf16)
        kv[c, r, 256:] = kv_y[:, 256:].astype(bf16)
    e_k = swap(kv.at[c], kv.at[c])
    for yy in range(4):
        r = pl.ds(yy * 128, 128)
        q_y = dot(xn[yy], w_q)
        q[r, :128] = (turn(q_y[:, :128], cosine[yy], sine[yy]).astype(bf16) * 0.125).astype(bf16)
        q[r, 128:] = (turn(q_y[:, 128:], cosine[yy], sine[yy]).astype(bf16) * 0.125).astype(bf16)
    net.arrive(kv.at[1 - c], e_k)
    own_qpos = qpos.at[c]
    forward_head(0, q, kv, own_qpos, kpos, lse, mixed_t)
    forward_head(1, q, kv, own_qpos, kpos, lse, mixed_t)
    forward_head(2, q, kv, own_qpos, kpos, lse, mixed_t)
    mix = mixed_t[...].T.astype(bf16)
    for yy in range(4):
        mixed_s[yy] = mix[yy * 128 : (yy + 1) * 128, :]
    i_m = net.take()
    keeps = jnp.logical_and(zl == c, y // 2 == c)
    for yy in range(4):
        net.send_or_keep(
            mixed_s.at[yy], mixed.at[zl, y % 2], i_m, device(at, y=yy, zl=c, c=y // 2), jnp.logical_and(y == yy, keeps)
        )
    net.left_if(keeps, mixed_s.at[0:3], i_m)
    net.left_if(jnp.logical_not(keeps), mixed_s, i_m)
    xnt[...] = xn[...].reshape(512, 768).T
    net.arrive(ogb.at[1 - c], i_ob)
    net.arrive(xb.at[1 - c], i_xb)
    ogt[...] = ogb[...].reshape(256, 768).T
    jobs[0].forward()
    jobs[1].forward()
    jobs[2].forward()
    jobs[3].forward()
    jobs[0].finish(2)
    for p in range(3):
        for yy in range(3):
            for zz in range(4):
                for xx in range(4):
                    r = (xx * 2 + zz % 2) * 48 + p * 16
                    wo[c, zz // 2, pl.ds(r, 16), pl.ds(yy * 128, 128)] = get_weight(wf, 3, (p, yy, xx, zz))
    e_o = swap(wo.at[c], wo.at[c])
    net.arrive(mixed, i_m)
    net.arrive(wo.at[1 - c], e_o)

    mix = [mixed[:, y2].reshape(256, 192) for y2 in range(2)]
    for ch in range(2):
        po[:, pl.ds(ch * 384, 384)] = dot(mix[0], wo[ch, c, :192, :]) + dot(mix[1], wo[ch, c, 192:, :])
    s_po = swap(po, por)
    acc[...] = jnp.zeros_like(acc)
    net.arrive(por, s_po)
    middle = xb[...].reshape(256, 768).astype(f32) + (po[...] + por[...])
    mid[...] = middle
    n2[...] = (middle * inverse_rms(middle)).astype(bf16)
    n2t[...] = n2[...].T
    jobs[1].finish(2)
    jobs[2].finish(2)

    grad = (g0, g1, g2)

    gathers = jobs
    jobs = []
    for k in range(3):
        own = per_job[7 * k : 7 * k + 7]
        jobs.append(Scatter(net, (grad[k],) + own[:3], own[3:6], own[6], GRAD_ORDERS[k]))
    for p in range(3):
        gate = dot(n2[...], ffn_panel(wf, 0, p))
        up = dot(n2[...], ffn_panel(wf, 1, p))
        sig = jax.nn.sigmoid(gate)
        a = gate * sig
        act[p] = a
        slope[p] = up * (sig * (1.0 + gate * (1.0 - sig)))
        hid[p] = (a * up).astype(bf16)
        store_ffn_panel(grad, 2, p, dot(ogt[...], hid[p]).astype(bf16))
        jobs[0].start(2, (p,))
    gathers[3].finish(2)
    for p in range(3):
        grad_hidden = dot(ogb[...].reshape(256, 768), ffn_panel(wf, 2, p))
        d_gate = (grad_hidden * slope[p]).astype(bf16)
        d_up = (grad_hidden * act[p]).astype(bf16)
        acc[...] += dot_nt(d_gate, ffn_panel(wf, 0, p)) + dot_nt(d_up, ffn_panel(wf, 1, p))
        store_ffn_panel(grad, 0, p, dot(n2t[...], d_gate).astype(bf16))
        jobs[1].start(2, (p,))
        store_ffn_panel(grad, 1, p, dot(n2t[...], d_up).astype(bf16))
    s_acc = swap(acc, accr)
    outp[...] = jnp.zeros_like(outp)
    for p in range(3):
        outp[...] += dot_nt(hid[p], ffn_panel(wf, 2, p))
    s_out = swap(outp.at[their_rows, :], outr)
    dkv[...] = jnp.zeros_like(dkv)
    dq_t[pl.ds(192, 64), :] = jnp.zeros((64, 512), f32)
    net.arrive(accr, s_acc)
    middle = mid[...]
    r2 = inverse_rms(middle)
    a = acc[...] + accr[...]
    scaled = middle * r2
    grad_middle = ogb[...].reshape(256, 768).astype(f32) + r2 * (
        a - scaled * jnp.mean(a * scaled, axis=-1, keepdims=True)
    )
    por[...] = grad_middle
    branch[...] = grad_middle.astype(bf16)
    for y2 in range(2):
        r = pl.ds(y2 * 192, 192)
        v = dot_nt(branch[:, :384], wo[0, c, r, :]) + dot_nt(branch[:, 384:], wo[1, c, r, :])
        for s in range(2):
            gm[y2 * 2 + s] = v[s * 128 : (s + 1) * 128, :].astype(bf16)
    i_g = net.take()
    for y2 in range(2):
        for s in range(2):
            mine = jnp.logical_and(c * 2 + y2 == y, jnp.logical_and(zl == s, zl == c))
            net.send_or_keep(gm.at[y2 * 2 + s], go.at[y], i_g, device(at, y=c * 2 + y2, zl=s, c=zl), mine)
    net.left_if(keeps, gm.at[0:3], i_g)
    net.left_if(jnp.logical_not(keeps), gm, i_g)
    for ch in range(2):
        for y2 in range(2):
            dwo[ch, pl.ds(y2 * 192, 192), :] = dot_tn(mix[y2], branch[:, ch * 384 : (ch + 1) * 384]).astype(bf16)
    s_dw = swap(dwo.at[1 - c], dwr)
    net.arrive(outr, s_out)
    outputs[...] = (mid[own_rows, :] + (outp[own_rows, :] + outr[...])).astype(bf16)
    net.arrive(dwr, s_dw)
    for p in range(3):
        for yy in range(4):
            for xx in range(4):
                for low in range(2):
                    r = (xx * 2 + low) * 48 + p * 16
                    own_place, their_place = ((p, yy, xx, h * 2 + low) for h in (c, 1 - c))
                    own, their = jnp.zeros((16, 128), bf16), jnp.zeros((16, 128), bf16)
                    if yy < 3:
                        own = dwo[c, pl.ds(r, 16), pl.ds(yy * 128, 128)]
                        their = dwr[pl.ds(r, 16), pl.ds(yy * 128, 128)]
                    put_grad(grad, 3, own_place, own)
                    put_grad(grad, 3, their_place, their)
    jobs[2].start(2)

    jobs[0].forward()
    net.arrive(go, i_g)
    for h in range(3):
        backward_head(h, q, kv, own_qpos, kpos, lse, go, dkv, dq_t)
        if h == 0:
            jobs[1].forward()
        if h == 1:
            jobs[0].finish(2)
            jobs[0].start(1)
    dkv_s[...] = dkv[1 - c].astype(bf16)
    s_k = swap(dkv_s, dkv_r)
    dq = dq_t[...].T * 0.125
    for yy in range(4):
        r = pl.ds(yy * 128, 128)
        v = dq[yy * 128 : (yy + 1) * 128, :]
        dp[r, 384:512] = turn(v[:, :128], cosine[yy], -sine[yy]).astype(bf16)
        dp[r, 512:] = turn(v[:, 128:], cosine[yy], -sine[yy]).astype(bf16)
    jobs[2].forward()
    net.arrive(dkv_r, s_k)
    for yy in range(4):
        r = pl.ds(yy * 128, 128)
        v = dkv[c, r, :] + dkv_r[r, :].astype(f32)
        dp[r, :128] = turn(v[:, :128], cosine[yy], -sine[yy]).astype(bf16)
        dp[r, 128:256] = turn_first_half(v[:, 128:256], cosine[yy], -sine[yy]).astype(bf16)
        dp[r, 256:384] = v[:, 256:].astype(bf16)
    for k in range(2):
        if k == 0:
            v = dot(xnt[...], dp[:, :384]).astype(bf16)
        else:
            v = jnp.concatenate([dot(xnt[...], dp[:, 384:]).astype(bf16), jnp.zeros((768, 128), bf16)], axis=1)
        for bx, bz, rows in row_blocks(v):
            wide_d[k, bx, bz] = rows[:, :256]
            narrow_d[k, bz, bx] = rows[:, 256:]
    s_w, s_n = swap(wide_d.at[1 - c], wide_r), swap(narrow_d.at[1 - c], narrow_r)
    a_kv = dot_nt(dp[:, :384], attention_panel(wide_w, narrow_w, 0))
    a_q = dot_nt(dp[:, 384:], attention_panel(wide_w, narrow_w, 1)[:, :256])
    a_s[...] = (a_kv + a_q).astype(bf16).reshape(4, 128, 768)
    i_a, i_a2 = net.take(), net.take()
    net.send(a_s.at[(y + 2) % 4], a_got.at[2], i_a, device(moved(at, "y", 4 - d)), i_a2)
    net.send(a_s.at[(y + d + 4) % 4], a_got.at[0], i_a, device(moved(at, "y", d)))
    net.left(a_got.at[0:2], i_a)
    net.arrive(wide_r, s_w)
    net.arrive(narrow_r, s_n)
    wide_t[...] = (wide_d[c].astype(f32) + wide_r[...].astype(f32)).astype(bf16)
    narrow_t[...] = (narrow_d[c].astype(f32) + narrow_r[...].astype(f32)).astype(bf16)
    i_wx = to_line("x", lambda step: wide_t.at[(x + step) % 4], lambda kind: wide_1.at[kind])
    net.left(wide_1, i_wx)
    i_nz = to_line("z", lambda step: narrow_t.at[(z + step) % 4], lambda kind: narrow_1.at[kind])
    net.left(narrow_1, i_nz)
    jobs[1].finish(2)
    jobs[1].start(1)
    jobs[0].finish(1)
    jobs[0].start(0)

    def four(own, got):
        v = own.astype(f32)
        for kind in range(3):
            v = v + got[kind].astype(f32)
        return v

    net.arrive(a_got.at[2], i_a2)
    a_on[...] = (a_s[(y - d + 4) % 4].astype(f32) + a_got[2].astype(f32)).astype(bf16)
    net.send(a_on, a_got.at[1], i_a2, device(moved(at, "y", 4 - d)), i_a)
    net.left(a_on, i_a2)
    net.arrive(wide_1, i_wx)
    wide_2[...] = four(wide_t[x], wide_1).astype(bf16)
    i_wz = to_line("z", lambda step: wide_2.at[(z + step) % 4], lambda kind: wide_0.at[kind])
    net.left(wide_0, i_wz)
    net.arrive(narrow_1, i_nz)
    narrow_2[...] = four(narrow_t[z], narrow_1).astype(bf16)
    i_nx = to_line("x", lambda step: narrow_2.at[(x + step) % 4], lambda kind: narrow_0.at[kind])
    net.left(narrow_0, i_nx)
    jobs[2].finish(2)
    jobs[2].start(1)
    net.arrive(a_got.at[0:2], i_a)
    a_sum[...] = (a_s[y].astype(f32) + a_got[0].astype(f32) + a_got[1].astype(f32)).astype(bf16)
    i_z = net.take()
    net.send_or_keep(a_sum, a_own, i_z, device(at, zl=c, c=zl), zl == c)
    net.left_if(zl != c, a_sum, i_z)
    jobs[1].finish(1)
    jobs[1].start(0)
    net.arrive(wide_0, i_wz)
    v = four(wide_2[z], wide_0)
    tall[0], tall[1] = v[:, :128], v[:, 128:]
    net.arrive(narrow_0, i_nx)
    tall[2] = four(narrow_2[x], narrow_0)
    jobs[2].finish(1)
    jobs[2].start(0)
    net.arrive(a_own, i_z)
    v = xb[c].astype(f32)
    r1 = inverse_rms(v)
    scaled = v * r1
    a = a_own[...].astype(f32)
    input_grad[...] = por[own_rows, :] + r1 * (a - scaled * jnp.mean(a * scaled, axis=-1, keepdims=True))
    for j in jobs:
        j.finish(0)
    lowest = [j.levels[3] for j in jobs]
    for cb in range(3):
        for m in range(3):
            tall[3 + m * 3 + cb] = get_sum(lowest, m, cb)
        tall[12, pl.ds(cb * 16, 16), :] = get_sum(lowest, 3, cb)
    for s in range(8):
        for unit in range(13):
            back_s[s, pl.ds(unit * 6, 6), :] = tall[unit, pl.ds(s * 6, 6), :]
        back_s[s, pl.ds(78, 2), :] = jnp.zeros((2, 128), f32)
    back_p[...] = back_s[...].astype(bf16)
    i_b = net.take()
    slot = c * 4 + y
    for s in range(8):
        mine = jnp.logical_and(y * 2 + zl == s, zl == c)
        net.send_or_keep(back_p.at[s], back.at[slot], i_b, device(at, y=s // 2, zl=s % 2, c=zl), mine)
    net.left_if(zl == c, back_p.at[0:7], i_b)
    net.left_if(zl != c, back_p, i_b)
    net.arrive(back, i_b)
    grads[...] = back[...].astype(f32)
    net.drain()


VM = pl.BlockSpec(memory_space=pltpu.VMEM)
SEMS = 61


def layer(*args):
    f, h = f32, bf16

    def blocks(lead, rows, columns=128):
        return (lead + (rows, columns), h)

    scratch = [
        *[(a.shape, a.dtype) for a in args[:5]], (args[7].shape, args[7].dtype),
        ((8, 32, 128), f), ((8, 32, 128), h), ((8, 32, 128), h), ((8, 32, 128), f),
        ((8, 64, 128), f), ((8, 64, 128), h), ((8, 64, 128), h), ((8, 64, 128), f), ((13, 48, 128), f),
        blocks((2, 4, 4), 48, 256), blocks((2, 4, 4), 48), *[blocks((3, 4, 4, 4), r) for r in WEIGHT_JOBS], ((2, 2, 384, 384), h),
        ((4, 128, 768), h), ((4, 128, 768), h), ((768, 512), h), ((4, 128, 128), f),
        ((4, 128, 128), f), ((2, 4, 128, 128), f), ((2, 4, 8, 128), f), ((2, 512, 384), h), ((512, 256), h),
        ((8, 512), f),
        ((192, 512), f), ((4, 128, 192), h), ((2, 2, 128, 192), h),
        ((2, 128, 768), h), ((2, 128, 768), h), ((256, 768), f), ((256, 768), f), ((256, 768), f),
        ((256, 768), h), ((768, 256), h), ((768, 256), h), ((3, 256, 512), f), ((3, 256, 512), f), ((3, 256, 512), h),
        ((256, 768), f), ((256, 768), f), ((256, 768), f), ((128, 768), f), ((256, 768), h), ((2, 384, 384), h),
        ((384, 384), h), ((4, 128, 192), h), *[blocks((3, 4, 4, 4), r) for r in GRAD_JOBS],
        ((4, 128, 192), h), ((2, 512, 384), f), ((512, 384), h), ((512, 384), h), ((256, 512), f), ((512, 640), h),
        blocks((2, 4, 4), 48, 256), blocks((2, 4, 4), 48), blocks((4, 4), 48, 256), blocks((4, 4), 48),
        blocks((4, 4), 48, 256), blocks((4, 4), 48), blocks((3, 4), 48, 256), blocks((3, 4), 48),
        blocks((4,), 48, 256), blocks((4,), 48), blocks((3,), 48, 256), blocks((3,), 48),
        ((4, 128, 768), h), ((3, 128, 768), h), ((128, 768), h), ((128, 768), h), ((128, 768), h),
        ((8, 80, 128), f), ((8, 80, 128), h), ((8, 80, 128), h),
    ]
    for r in GRAD_JOBS:
        scratch += [blocks((3,) + (4,) * k, r) for k in (2, 1, 0)]
        scratch += [blocks((3, 3) + (4,) * k, r) for k in (2, 1, 0)]
        scratch += [blocks((3, 4, 4), r)]
    return pl.pallas_call(
        layer_body,
        out_shape=(
            jax.ShapeDtypeStruct((128, 768), bf16),
            jax.ShapeDtypeStruct((128, 768), f32),
            jax.ShapeDtypeStruct((8, 80, 128), f32),
        ),
        in_specs=[pl.BlockSpec(memory_space=pl.ANY)] * len(args),
        out_specs=(VM,) * 3,
        scratch_shapes=[pltpu.VMEM(s, t) for s, t in scratch]
        + [pltpu.SemaphoreType.DMA((SEMS,))] * 2
        + [pltpu.SemaphoreType.DMA((8,))],
        compiler_params=pltpu.CompilerParams(collective_id=0, has_side_effects=True, vmem_limit_bytes=60 << 20),
    )(*args)


def adam_step(master, gradient, moment_one, moment_two, rate_value, decay_value):
    moment_one = BETA_FIRST * moment_one + (1.0 - BETA_FIRST) * gradient
    moment_two = BETA_SECOND * moment_two + (1.0 - BETA_SECOND) * gradient * gradient
    first_hat = moment_one / (1.0 - BETA_FIRST**STEP)
    second_hat = moment_two / (1.0 - BETA_SECOND**STEP)
    updated = master - rate_value * (
        first_hat / (jnp.sqrt(second_hat) + ADAM_EPS) + decay_value * master
    )
    return (moment_one, moment_two, updated)


def owner_body(
    grads, outputs, input_grad,
    qkv, qkv_m, qkv_s, out, out_m, out_s, gu, gu_m, gu_s, dt, dt_m, dt_s, gains, gains_m, gains_s,
    outputs_o, input_grad_o,
    qkv_mo, qkv_so, qkv_o, out_mo, out_so, out_o, gu_mo, gu_so, gu_o, dt_mo, dt_so, dt_o,
    gains_mo, gains_so, gains_o,
):
    outputs_o[...] = outputs[...]
    input_grad_o[...] = input_grad[...]

    def unit(slot, u):
        return grads[slot, pl.ds(u * 6, 6), :]

    eye = lax.broadcasted_iota(jnp.int32, (6, 6), 0) == lax.broadcasted_iota(jnp.int32, (6, 6), 1)
    g_low = gains[...].astype(bf16).astype(f32)
    g_one = jnp.sum(jnp.where(eye, g_low[0:1, :], 0.0), axis=1, keepdims=True)
    g_two = jnp.sum(jnp.where(eye, g_low[1:2, :], 0.0), axis=1, keepdims=True)

    def update(refs, new, columns, gradient, rate, decay):
        w, m, s = refs
        values = adam_step(w[:, columns], gradient, m[:, columns], s[:, columns], rate, decay)
        for to, v in zip(new, values):
            to[:, columns] = v

    def low_times(w, columns, gradient):
        return jnp.sum(w[:, columns].astype(bf16).astype(f32) * gradient, axis=1, keepdims=True)

    def join(a, b):
        return jnp.concatenate([a, b], axis=1)

    rate = D ** (-0.5)
    sum_one = jnp.zeros((6, 1), f32)
    for pair in range(2):
        e, o = 2 * pair, 2 * pair + 1
        u = {(s, k): unit(s, k) for s in (e, o, 4 + e, 4 + o) for k in range(3)}
        tiles = {
            0: (u[4 + e, 0], join(u[4 + e, 1][:, :64], u[4 + o, 0][:, :64]), join(u[4 + o, 0][:, 64:], u[4 + o, 1][:, :64])),
            768: (u[e, 0], join(u[e, 1][:, :64], u[o, 0][:, :64]), join(u[o, 0][:, 64:], u[o, 1][:, :64])),
            1536: (join(u[e, 1][:, 64:], u[e, 2][:, :64]), join(u[e, 2][:, 64:], u[o, 1][:, 64:]), u[o, 2]),
        }
        for first, three in tiles.items():
            for k, t in enumerate(three):
                columns = pl.ds(first + pair * 384 + k * 128, 128)
                sum_one = sum_one + low_times(qkv, columns, t)
                update((qkv, qkv_m, qkv_s), (qkv_mo, qkv_so, qkv_o), columns, t * g_one, rate, WEIGHT_DECAY)
    sum_two = jnp.zeros((6, 1), f32)
    for slot in range(8):
        for cb in range(3):
            f = slot * 384 + cb * 128
            for half in range(2):
                columns = pl.ds(half * 3072 + f, 128)
                t = unit(slot, 3 + half * 3 + cb)
                sum_two = sum_two + low_times(gu, columns, t)
                update((gu, gu_m, gu_s), (gu_mo, gu_so, gu_o), columns, t * g_two, rate, WEIGHT_DECAY)
            update(
                (dt, dt_m, dt_s), (dt_mo, dt_so, dt_o), pl.ds(f, 128), unit(slot, 9 + cb), FF ** (-0.5), WEIGHT_DECAY
            )
        if slot % 4 < 3:
            update(
                (out, out_m, out_s), (out_mo, out_so, out_o), pl.ds((slot // 4) * 384 + (slot % 4) * 128, 128),
                unit(slot, 12), (H * HD * 32 // LEN) ** (-0.5), WEIGHT_DECAY,
            )
    rows = [jnp.sum(jnp.where(eye, v, 0.0), axis=0, keepdims=True) for v in (sum_one, sum_two)]
    values = adam_step(gains[...], jnp.concatenate(rows, axis=0), gains_m[...], gains_s[...], GAIN_RATE, 0.0)
    for to, v in zip((gains_mo, gains_so, gains_o), values):
        to[...] = v


def owners_step(*args):
    shapes = [(args[1].shape, bf16), (args[2].shape, f32)]
    for first in range(3, 18, 3):
        shapes += [(args[first].shape, f32)] * 3
    return pl.pallas_call(
        owner_body,
        out_shape=tuple(jax.ShapeDtypeStruct(s, t) for s, t in shapes),
        in_specs=[VM] * len(args),
        out_specs=(VM,) * len(shapes),
    )(*args)


def body(
    inputs, positions, output_grad,
    qkv_weight, qkv_first, qkv_second, out_weight, out_first, out_second,
    gate_up_weight, gate_up_first, gate_up_second, down_weight, down_first, down_second,
    norm_gains, gains_first, gains_second,
):
    outputs, input_grad, grads = layer(
        qkv_weight, out_weight, gate_up_weight, down_weight.T, norm_gains,
        inputs.reshape(128, D), output_grad.reshape(128, D), positions,
    )
    new = owners_step(
        grads, outputs, input_grad,
        qkv_weight, qkv_first, qkv_second, out_weight, out_first, out_second,
        gate_up_weight, gate_up_first, gate_up_second, down_weight.T, down_first.T, down_second.T,
        norm_gains, gains_first, gains_second,
    )
    return (
        new[0].reshape(1, 128, D), new[1].reshape(1, 128, D), *new[2:11],
        *(v.T for v in new[11:14]), *new[14:],
    )


def solution(mesh):
    token = P("dp", "ctx", None)
    rows, columns = P(("dp", "ctx"), None), P(None, ("dp", "ctx"))
    return jax.shard_map(
        body,
        mesh=mesh,
        in_specs=(token, P("dp", "ctx"), token) + (rows,) * 9 + (columns,) * 6,
        out_specs=(token, token) + (rows,) * 9 + (columns,) * 6,
        check_vma=False,
    )
```

```python
import math

import jax
import jax.numpy as jnp
from jax import lax
from jax.experimental import pallas as pl
from jax.experimental.pallas import tpu as pltpu
from jax.sharding import PartitionSpec as P

D = 768
H = 12
HD = 64
FF = 3072
LEN = 1024
STEP = 10

NORM_EPS = 1e-05
ROPE_BASE = 10000.0
BETA_FIRST = 0.9
BETA_SECOND = 0.95
ADAM_EPS = 1e-08
WEIGHT_DECAY = 0.1
GAIN_RATE = 1.2
MASKED = -1e30

MESH = pl.DeviceIdType.MESH
bf16, f32 = jnp.bfloat16, jnp.float32

ORDERS = (("x", "y", "z"), ("y", "z", "x"), ("z", "x", "y"))
WEIGHT_JOBS = (16, 48, 48, 48)
GRAD_JOBS = (48, 48, 64)
WEIGHT_ORDERS = (ORDERS,) * 4
GRAD_ORDERS = (ORDERS,) * 3


def here():
    dp, ctx = lax.axis_index("dp"), lax.axis_index("ctx")
    return dict(x=(dp // 2) % 4, y=ctx // 2, z=(dp // 8) * 2 + ctx % 2, c=dp % 2)


def low_z(at):
    return at["z"] % 2


def device(at, zl=None, **moved):
    at = dict(at, **moved)
    if zl is not None:
        at["z"] = (at["z"] // 2) * 2 + zl
    return ((at["z"] // 2) * 8 + at["x"] * 2 + at["c"], at["y"] * 2 + at["z"] % 2)


def moved(at, axis, step):
    return dict(at, **{axis: (at[axis] + step + 4) % 4})


def row_block(at):
    return (at["z"] // 2) * 8 + at["x"] * 2 + at["z"] % 2


def group_of(at):
    out = []
    me = at["c"] * 8 + at["y"] * 2 + low_z(at)
    for k in range(1, 16):
        other = (me + k) % 16
        out.append(device(at, c=other // 8, y=(other // 2) % 4, zl=other % 2))
    for k in range(1, 4):
        out.append(device(at, x=(at["x"] + k) % 4))
    other_half = dict(at, z=(at["z"] + 2) % 4)
    for low in range(2):
        out.append(device(other_half, zl=low))
    return out


def signal_all(peers):
    barrier = pltpu.get_barrier_semaphore()
    for p in peers:
        pl.semaphore_signal(barrier, inc=1, device_id=p, device_id_type=MESH)


def wait_all(peers):
    pl.semaphore_wait(pltpu.get_barrier_semaphore(), len(peers))


class Net:
    def __init__(self, at, send_sem, recv_sem):
        self.at, self.send_sem, self.recv_sem = at, send_sem, recv_sem
        self.used = 0
        self.ends = []

    def take(self):
        self.used += 1
        return self.used - 1

    def send(self, src, dst, i, to, r=None):
        pltpu.make_async_remote_copy(
            src_ref=src, dst_ref=dst, send_sem=self.send_sem.at[i], recv_sem=self.recv_sem.at[i if r is None else r],
            device_id=to, device_id_type=MESH,
        ).start()

    def send_or_keep(self, src, dst, i, to, mine):
        pl.when(jnp.logical_not(mine))(lambda: self.send(src, dst, i, to))
        pl.when(mine)(lambda: pltpu.make_async_copy(src, dst, self.recv_sem.at[i]).start())

    def left(self, view, i):
        self.ends.append((None, view, i))

    def left_if(self, condition, view, i):
        self.ends.append((condition, view, i))

    def arrive(self, view, i):
        pltpu.make_async_copy(view, view, self.recv_sem.at[i]).wait()

    def drain(self):
        for condition, view, i in self.ends:
            wait = pltpu.make_async_copy(view, view, self.send_sem.at[i]).wait
            if condition is None:
                wait()
            else:
                pl.when(condition)(wait)


class Gather:
    def __init__(self, net, ref, orders):
        self.net, self.at, self.ref, self.orders = net, net.at, ref, orders
        self.sems = [net.take() for _ in range(4)]
        views = (ref.at[0, 0:3, 0:3, 0], ref.at[0, 0:3, 0:3], ref.at[0:2, 0:3], ref.at[0, 0:3])
        self.views = views
        for view, i in zip(views, self.sems):
            net.left(view, i)

    def view(self, part, at, phase):
        a1, a2, a3 = self.orders[part]
        return self.ref.at[(part, at[a3], at[a2], at[a1])[: 4 - phase]]

    def send(self, part, phase, at, axis, step, i):
        v = self.view(part, at, phase)
        self.net.send(v, v, i, device(moved(self.at, axis, step)))

    def start(self, phase):
        for step in (2, 1, 3) if phase < 2 else (1, 3):
            for part in range(3):
                self.send(part, phase, self.at, self.orders[part][phase], step, self.sems[phase])

    def forward(self):
        d = 1 - 2 * self.at["c"]
        self.net.arrive(self.views[2], self.sems[2])
        for part in range(3):
            axis = self.orders[part][2]
            self.send(part, 2, moved(self.at, axis, -d), axis, d, self.sems[3])

    def finish(self, phase):
        k = phase if phase < 2 else 3
        self.net.arrive(self.views[k], self.sems[k])


class Scatter:
    def __init__(self, net, levels, got, turned, orders):
        self.net, self.at, self.orders = net, net.at, orders
        self.levels, self.got, self.turned = levels, got, turned
        self.sems = [net.take() for _ in range(4)]
        self.views = (got[2], got[1], got[0].at[0:2], got[0].at[2])
        for view, i in zip(self.views, self.sems):
            net.left(view, i)

    def level(self, part, phase, i):
        return self.levels[2 - phase].at[part, i]

    def slot(self, part, phase, kind):
        return self.got[2 - phase].at[kind, part]

    def go(self, src, part, phase, kind, axis, step, s, r):
        self.net.send(src, self.slot(part, phase, kind), s, device(moved(self.at, axis, step)), r)

    def add(self, to, refs, phase):
        def one(index):
            total = refs[0][index].astype(f32)
            for r in refs[1:]:
                total = total + r[index].astype(f32)
            to[index] = total.astype(to.dtype)

        if phase == 2:
            pl.loop(0, 4)(lambda b: one((b,)))
        else:
            one(...)

    def start(self, phase, parts=range(3)):
        d = 1 - 2 * self.at["c"]
        i = self.sems[phase]
        for part in parts:
            axis = self.orders[part][phase]
            me = self.at[axis]
            if phase < 2:
                for kind, step in enumerate((2, 1, 3)):
                    self.go(self.level(part, phase, (me + step) % 4), part, phase, kind, axis, step, i, i)
            else:
                self.go(self.level(part, phase, (me + 2) % 4), part, phase, 2, axis, 4 - d, i, self.sems[3])
                self.go(self.level(part, phase, (me + d + 4) % 4), part, phase, 0, axis, d, i, i)

    def forward(self):
        d = 1 - 2 * self.at["c"]
        self.net.arrive(self.views[3], self.sems[3])
        for part in range(3):
            axis = self.orders[part][2]
            me = self.at[axis]
            to = self.turned.at[part]
            self.add(to, [self.level(part, 2, (me - d + 4) % 4), self.slot(part, 2, 2)], 2)
            self.go(to, part, 2, 1, axis, 4 - d, self.sems[3], self.sems[2])

    def finish(self, phase):
        self.net.arrive(self.views[phase], self.sems[phase])
        for part in range(3):
            me = self.at[self.orders[part][phase]]
            kinds = (0, 1, 2) if phase < 2 else (0, 1)
            to = self.levels[3 - phase].at[part]
            self.add(to, [self.level(part, phase, me)] + [self.slot(part, phase, k) for k in kinds], phase)


def dot(a, b):
    return jnp.dot(a, b, preferred_element_type=f32)


def dot_nt(a, b):
    return lax.dot_general(a, b, (((1,), (1,)), ((), ())), preferred_element_type=f32)


def dot_tn(a, b):
    return lax.dot_general(a, b, (((0,), (0,)), ((), ())), preferred_element_type=f32)


def inverse_rms(v):
    return lax.rsqrt(jnp.mean(v * v, axis=-1, keepdims=True) + NORM_EPS)


def tables(place, freq):
    angle = place * freq
    lane = lax.broadcasted_iota(jnp.int32, place.shape, 1)
    sine = jnp.sin(angle)
    return jnp.cos(angle), jnp.where(lane % 64 < 32, -sine, sine)


def turn(v, cosine, sine):
    lane = lax.broadcasted_iota(jnp.int32, v.shape, 1)
    swapped = jnp.where(lane % 64 < 32, pltpu.roll(v, 96, 1), pltpu.roll(v, 32, 1))
    return v * cosine + swapped * sine


def turn_first_half(v, cosine, sine):
    lane = lax.broadcasted_iota(jnp.int32, v.shape, 1)
    return jnp.where(lane < 64, turn(v, cosine, sine), v)


def ffn_index(orders, part, y, x, z):
    place = dict(x=x, y=y, z=z)
    a1, a2, a3 = orders[part]
    return (part, place[a3], place[a2], place[a1])


WEIGHT_ROWS = ((1, 0, 48), (2, 0, 48), (3, 0, 48), (0, 0, 16))
GRAD_ROWS = ((1, 0, 48), (2, 0, 48), (0, 0, 48), (2, 48, 16))


def put_weight(refs, matrix, place, value):
    job, first, count = WEIGHT_ROWS[matrix]
    refs[job][ffn_index(WEIGHT_ORDERS[job], *place) + (pl.ds(first, count), slice(None))] = value


def get_weight(refs, matrix, place):
    job, first, count = WEIGHT_ROWS[matrix]
    return refs[job][ffn_index(WEIGHT_ORDERS[job], *place) + (pl.ds(first, count), slice(None))]


def put_grad(refs, matrix, place, value):
    job, first, count = GRAD_ROWS[matrix]
    refs[job][ffn_index(GRAD_ORDERS[job], *place) + (pl.ds(first, count), slice(None))] = value


def get_sum(refs, matrix, part):
    job, first, count = GRAD_ROWS[matrix]
    return refs[job][part, pl.ds(first, count), :].astype(f32)


def rows_of(pick):
    return jnp.concatenate([pick(x, zh * 2 + zl) for zh in range(2) for x in range(4) for zl in range(2)], axis=0)


def row_blocks(value):
    for zh in range(2):
        for x in range(4):
            for zl in range(2):
                r = (zh * 8 + x * 2 + zl) * 48
                yield x, zh * 2 + zl, value[r : r + 48, :]


def ffn_panel(wf, matrix, p):
    return jnp.concatenate(
        [rows_of(lambda x, z: get_weight(wf, matrix, (p, y, x, z))) for y in range(4)], axis=1
    )


def store_ffn_panel(g, matrix, p, value):
    for x, z, rows in row_blocks(value):
        for y in range(4):
            put_grad(g, matrix, (p, y, x, z), rows[:, y * 128 : (y + 1) * 128])


def attention_panel(wide, narrow, which):
    if which == 1:
        return rows_of(lambda x, z: wide[1, x, z])
    return rows_of(lambda x, z: jnp.concatenate([wide[0, x, z], narrow[z, x]], axis=1))


def head_parts(h, kv):
    k = jnp.concatenate([kv[0, :, h * 64 : (h + 1) * 64], kv[1, :, h * 64 : (h + 1) * 64]], axis=0)
    o = 192 + h * 64
    v = jnp.concatenate([kv[0, :, o : o + 64], kv[1, :, o : o + 64]], axis=0)
    return k, v


def query_positions(qpos, half):
    return jnp.concatenate([qpos[half * 2], qpos[half * 2 + 1]], axis=1)[0:1, :]


def masked_scores(k, q_part, kpos, q_row):
    s = dot_nt(k, q_part)
    kp = kpos[...].reshape(1024, 128)
    allowed = jnp.concatenate([kp, kp], axis=1) <= q_row
    return jnp.where(allowed, s, MASKED)


def forward_head(h, q, kv, qpos, kpos, lse, mixed_t):
    k, v = head_parts(h, kv)
    for half in range(2):
        q_part = q[pl.ds(half * 256, 256), h * 64 : (h + 1) * 64]
        s = masked_scores(k, q_part, kpos, query_positions(qpos, half))
        highest = jnp.max(s, axis=0, keepdims=True)
        e = jnp.exp(s - highest)
        total = jnp.sum(e, axis=0, keepdims=True)
        p = (e * (1.0 / total)).astype(bf16)
        mixed_t[pl.ds(h * 64, 64), pl.ds(half * 256, 256)] = dot_tn(v, p)
        lse[pl.ds(h, 1), pl.ds(half * 256, 256)] = highest + jnp.log(total)


def backward_head(h, q, kv, qpos, kpos, lse, go, dkv, dq_t):
    k, v = head_parts(h, kv)
    for half in range(2):
        rows = pl.ds(half * 256, 256)
        q_part = q[rows, h * 64 : (h + 1) * 64]
        g_part = go[pl.ds(half * 2, 2), :, h * 64 : (h + 1) * 64].reshape(256, 64)
        s = masked_scores(k, q_part, kpos, query_positions(qpos, half))
        p = jnp.exp(s - lse[pl.ds(h, 1), rows])
        dp = dot_nt(v, g_part)
        centre = jnp.sum(p * dp, axis=0, keepdims=True)
        ds = (p * (dp - centre)).astype(bf16)
        dv = dot(p.astype(bf16), g_part)
        dk = dot(ds, q_part)
        dq_t[pl.ds(h * 64, 64), rows] = dot_tn(k, ds)
        for cc in range(2):
            dkv[cc, :, h * 64 : (h + 1) * 64] += dk[cc * 512 : (cc + 1) * 512]
            dkv[cc, :, 192 + h * 64 : 192 + (h + 1) * 64] += dv[cc * 512 : (cc + 1) * 512]


def as_column(eye, row):
    return jnp.sum(jnp.where(eye, row, 0.0), axis=1, keepdims=True)


def low_gains(gains):
    eye = lax.broadcasted_iota(jnp.int32, (6, 6), 0) == lax.broadcasted_iota(jnp.int32, (6, 6), 1)
    g_low = gains[...].astype(bf16).astype(f32)
    return as_column(eye, g_low[0:1, :]), as_column(eye, g_low[1:2, :])


def cut_attention(qkv, g_one, positions, stage):
    place = positions[...]
    place = jnp.concatenate([(place // 64).astype(f32), (place % 64).astype(f32)], axis=0)
    zero = jnp.zeros((6, 64), f32)
    for yy in range(4):
        o = yy * 192
        q_y = qkv[:, o : o + 192].astype(bf16).astype(f32) * g_one
        k_y = qkv[:, 768 + o : 768 + o + 192].astype(bf16).astype(f32) * g_one
        v_y = qkv[:, 1536 + o : 1536 + o + 192].astype(bf16).astype(f32) * g_one
        stage[yy, pl.ds(0, 6), :] = k_y[:, :128]
        stage[yy, pl.ds(6, 6), :] = jnp.concatenate([k_y[:, 128:], v_y[:, :64]], axis=1)
        stage[yy, pl.ds(12, 6), :] = v_y[:, 64:]
        stage[4 + yy, pl.ds(0, 6), :] = q_y[:, :128]
        stage[4 + yy, pl.ds(6, 6), :] = jnp.concatenate([q_y[:, 128:], zero], axis=1)
        stage[4 + yy, pl.ds(12, 6), :] = jnp.zeros((6, 128), f32)
    for slot in range(8):
        stage[slot, pl.ds(18, 2), :] = place
        stage[slot, pl.ds(20, 12), :] = jnp.zeros((12, 128), f32)


def cut_rest(out, gu, dt, g_two, stage):
    def put(slot, unit, v):
        stage[slot, pl.ds(unit * 6, 6), :] = v

    for slot in range(8):
        for cb in range(3):
            f = slot * 384 + cb * 128
            put(slot, cb, gu[:, f : f + 128].astype(bf16).astype(f32) * g_two)
            put(slot, 3 + cb, gu[:, 3072 + f : 3072 + f + 128].astype(bf16).astype(f32) * g_two)
            put(slot, 6 + cb, dt[:, f : f + 128])
        cc, yy = slot // 4, slot % 4
        if yy < 3:
            put(slot, 9, out[:, cc * 384 + yy * 128 : cc * 384 + (yy + 1) * 128])
        else:
            put(slot, 9, jnp.zeros((6, 128), f32))
        stage[slot, pl.ds(60, 4), :] = jnp.zeros((4, 128), f32)


def layer_body(
    qkv_h, out_h, gu_h, dt_h, gains_h, x_h, og_h, positions_h,
    outputs, input_grad, grads,
    qkv, out, gu, dt, gains, positions,
    stage_a, pieces_a, recv_a, wide_a, stage_f, pieces_f, recv_f, wide_f, tall,
    wide_w, narrow_w, wf0, wf1, wf2, wf3, wo, xg, xn, xnt, cosine, sine, kpos, qpos, kv, q, lse,
    mixed_t, mixed_s, mixed,
    xb, ogb, po, por, mid, n2, n2t, ogt, act, slope, hid, acc, accr, outp, outr, branch, dwo, dwr, gm, g0, g1, g2,
    go, dkv, dkv_s, dkv_r, dq_t, dp, wide_d, narrow_d, wide_r, narrow_r, wide_t, narrow_t,
    wide_1, narrow_1, wide_2, narrow_2, wide_0, narrow_0, a_s, a_got, a_on, a_sum, a_own, back_s, back_p, back,
    *rest,
):
    per_job, (send_sem, recv_sem, load_sem) = rest[:-3], rest[-3:]
    at = here()
    c, y, zl = at["c"], at["y"], low_z(at)
    d = 1 - 2 * c
    net = Net(at, send_sem, recv_sem)
    peers = group_of(at)
    partner = device(at, c=1 - c)
    rb = row_block(at)
    own_rows = pl.ds(pl.multiple_of(c * 128, 128), 128)
    their_rows = pl.ds(pl.multiple_of((1 - c) * 128, 128), 128)

    def swap(src, dst):
        i = net.take()
        net.send(src, dst, i, partner)
        net.left(src, i)
        return i

    def to_line(axis, pick, slot, only=None):
        i = net.take()

        def go():
            for kind, step in enumerate((2, 1, 3)):
                net.send(pick(step), slot(kind), i, device(moved(at, axis, step)))

        if only is None:
            go()
        else:
            pl.when(only)(go)
        return i

    first = c == 0

    loads = [
        pltpu.make_async_copy(src, dst, load_sem.at[i])
        for i, (src, dst) in enumerate(
            (
                (qkv_h, qkv), (gains_h, gains), (positions_h, positions), (x_h, xb.at[c]),
                (gu_h, gu), (dt_h, dt), (out_h, out), (og_h, ogb.at[c]),
            )
        )
    ]
    for copy in loads:
        copy.start()
    signal_all(peers)
    for copy in loads[:3]:
        copy.wait()
    g_one, g_two = low_gains(gains)
    cut_attention(qkv, g_one, positions, stage_a)
    pieces_a[...] = stage_a[...].astype(bf16)
    for copy in loads[3:]:
        copy.wait()
    cut_rest(out, gu, dt, g_two, stage_f)
    pieces_f[...] = stage_f[...].astype(bf16)
    wait_all(peers)

    source = y * 2 + zl

    def to_group(pieces, recv):
        i = net.take()
        for cc in range(2):
            for yy in range(4):
                mine = jnp.logical_and(zl == c, jnp.logical_and(y == yy, c == cc))
                net.send_or_keep(pieces.at[cc * 4 + yy], recv.at[source], i, device(at, y=yy, zl=c, c=cc), mine)
        net.left_if(zl == c, pieces.at[0:7], i)
        net.left_if(zl != c, pieces, i)
        return i

    r_a = to_group(pieces_a, recv_a)
    r_f = to_group(pieces_f, recv_f)
    i_x = net.take()
    net.send_or_keep(xb.at[c], xg.at[y], i_x, device(at, zl=c, c=zl), zl == c)
    net.left_if(zl != c, xb.at[c], i_x)
    i_xb = swap(xb.at[c], xb.at[c])
    i_ob = swap(ogb.at[c], ogb.at[c])

    net.arrive(recv_a, r_a)
    wide_a[...] = recv_a[...].astype(f32)
    for unit in range(3):
        for s in range(8):
            tall[unit, pl.ds(s * 6, 6), :] = wide_a[s, pl.ds(unit * 6, 6), :]
    x, z = at["x"], at["z"]
    wide_w[c, x, z] = jnp.concatenate([tall[0], tall[1]], axis=1).astype(bf16)

    @pl.when(first)
    def _():
        narrow_w[z, x] = tall[2].astype(bf16)

    block = wide_w.at[c, x, z]
    i_wz = to_line("z", lambda step: block, lambda kind: block)
    net.left(wide_w.at[0, 0, 0:3], i_wz)
    thin = narrow_w.at[z, x]
    i_nx = to_line("x", lambda step: thin, lambda kind: thin, first)
    net.left_if(first, narrow_w.at[0, 0:3], i_nx)
    net.arrive(xg.at[y], i_x)
    i_y, i_y2 = net.take(), net.take()
    for step in (1, 3):
        net.send(xg.at[y], xg.at[y], i_y, device(moved(at, "y", step)))
    net.left(xg.at[0:2], i_y)

    net.arrive(recv_f, r_f)
    wide_f[...] = recv_f[...].astype(f32)
    for unit in range(10):
        for s in range(8):
            tall[3 + unit, pl.ds(s * 6, 6), :] = wide_f[s, pl.ds(unit * 6, 6), :]
    wf = (wf0, wf1, wf2, wf3)
    for cb in range(3):
        place = (cb, y, x, z)
        for m in range(3):
            put_weight(wf, m, place, tall[3 + m * 3 + cb].astype(bf16))
        put_weight(wf, 3, place, tall[12, pl.ds(cb * 16, 16), :].astype(bf16))
    jobs = [Gather(net, ref, orders) for ref, orders in zip(wf, WEIGHT_ORDERS)]
    for j in jobs:
        j.start(0)
    net.arrive(wide_w.at[0, 0, 0:3], i_wz)
    row = wide_w.at[c, x]
    i_wx = to_line("x", lambda step: row, lambda kind: row)
    net.left(wide_w.at[0, 0:3], i_wx)
    pl.when(first)(lambda: net.arrive(narrow_w.at[0, 0:3], i_nx))
    thin_row = narrow_w.at[z]
    i_nz = to_line("z", lambda step: thin_row, lambda kind: thin_row, first)
    net.left_if(first, narrow_w.at[0:3], i_nz)

    for s in range(8):
        row = wide_a[s, pl.ds(18, 1), :] * 64.0 + wide_a[s, pl.ds(19, 1), :]
        rows = jnp.broadcast_to(row, (128, 128))
        kpos[s % 2, s // 2] = rows.T
        qpos[s % 2, s // 2] = rows[:8]
    lane = lax.broadcasted_iota(jnp.int32, (1, 128), 1) % 32
    freq = jnp.exp(lane.astype(f32) * (-2.0 * math.log(ROPE_BASE) / HD))
    for yy in range(4):
        cosine[yy], sine[yy] = tables(kpos[c, yy], freq)
    net.arrive(xg.at[0:2], i_y)
    behind = xg.at[(y - d + 4) % 4]
    net.send(behind, behind, i_y2, device(moved(at, "y", d)))
    net.left(xg.at[0], i_y2)
    for j in jobs:
        j.finish(0)
        j.start(1)

    def normalize(yy):
        v = xg[yy].astype(f32)
        xn[yy] = (v * inverse_rms(v)).astype(bf16)

    for step in (0, 1, 3):
        normalize((y + step) % 4)
    net.arrive(xg.at[0], i_y2)
    normalize((y + 2) % 4)
    jobs[0].finish(1)
    jobs[0].start(2)
    jobs[1].finish(1)
    jobs[1].start(2)
    jobs[2].finish(1)
    jobs[2].start(2)
    jobs[3].finish(1)
    jobs[3].start(2)
    net.arrive(wide_w.at[0, 0:3], i_wx)
    e_w, e_n = swap(wide_w.at[c], wide_w.at[c]), net.take()

    @pl.when(first)
    def _():
        net.arrive(narrow_w.at[0:3], i_nz)
        net.send(narrow_w, narrow_w, e_n, partner)

    net.left_if(first, narrow_w, e_n)
    net.arrive(wide_w.at[1 - c], e_w)
    pl.when(c == 1)(lambda: net.arrive(narrow_w, e_n))

    w_kv = attention_panel(wide_w, narrow_w, 0)
    w_q = attention_panel(wide_w, narrow_w, 1)
    for yy in range(4):
        r = pl.ds(yy * 128, 128)
        kv_y = dot(xn[yy], w_kv)
        kv[c, r, :128] = turn(kv_y[:, :128], cosine[yy], sine[yy]).astype(bf16)
        kv[c, r, 128:256] = turn_first_half(kv_y[:, 128:256], cosine[yy], sine[yy]).astype(bf16)
        kv[c, r, 256:] = kv_y[:, 256:].astype(bf16)
    e_k = swap(kv.at[c], kv.at[c])
    for yy in range(4):
        r = pl.ds(yy * 128, 128)
        q_y = dot(xn[yy], w_q)
        q[r, :128] = (turn(q_y[:, :128], cosine[yy], sine[yy]).astype(bf16) * 0.125).astype(bf16)
        q[r, 128:] = (turn(q_y[:, 128:], cosine[yy], sine[yy]).astype(bf16) * 0.125).astype(bf16)
    net.arrive(kv.at[1 - c], e_k)
    own_qpos = qpos.at[c]
    forward_head(0, q, kv, own_qpos, kpos, lse, mixed_t)
    forward_head(1, q, kv, own_qpos, kpos, lse, mixed_t)
    forward_head(2, q, kv, own_qpos, kpos, lse, mixed_t)
    mix = mixed_t[...].T.astype(bf16)
    for yy in range(4):
        mixed_s[yy] = mix[yy * 128 : (yy + 1) * 128, :]
    i_m = net.take()
    keeps = jnp.logical_and(zl == c, y // 2 == c)
    for yy in range(4):
        net.send_or_keep(
            mixed_s.at[yy], mixed.at[zl, y % 2], i_m, device(at, y=yy, zl=c, c=y // 2), jnp.logical_and(y == yy, keeps)
        )
    net.left_if(keeps, mixed_s.at[0:3], i_m)
    net.left_if(jnp.logical_not(keeps), mixed_s, i_m)
    xnt[...] = xn[...].reshape(512, 768).T
    net.arrive(ogb.at[1 - c], i_ob)
    net.arrive(xb.at[1 - c], i_xb)
    ogt[...] = ogb[...].reshape(256, 768).T
    jobs[0].forward()
    jobs[1].forward()
    jobs[2].forward()
    jobs[3].forward()
    jobs[0].finish(2)
    for p in range(3):
        for yy in range(3):
            for zz in range(4):
                for xx in range(4):
                    r = (xx * 2 + zz % 2) * 48 + p * 16
                    wo[c, zz // 2, pl.ds(r, 16), pl.ds(yy * 128, 128)] = get_weight(wf, 3, (p, yy, xx, zz))
    e_o = swap(wo.at[c], wo.at[c])
    net.arrive(mixed, i_m)
    net.arrive(wo.at[1 - c], e_o)

    mix = [mixed[:, y2].reshape(256, 192) for y2 in range(2)]
    for ch in range(2):
        po[:, pl.ds(ch * 384, 384)] = dot(mix[0], wo[ch, c, :192, :]) + dot(mix[1], wo[ch, c, 192:, :])
    s_po = swap(po, por)
    acc[...] = jnp.zeros_like(acc)
    net.arrive(por, s_po)
    middle = xb[...].reshape(256, 768).astype(f32) + (po[...] + por[...])
    mid[...] = middle
    n2[...] = (middle * inverse_rms(middle)).astype(bf16)
    n2t[...] = n2[...].T
    jobs[1].finish(2)
    jobs[2].finish(2)

    grad = (g0, g1, g2)

    gathers = jobs
    jobs = []
    for k in range(3):
        own = per_job[7 * k : 7 * k + 7]
        jobs.append(Scatter(net, (grad[k],) + own[:3], own[3:6], own[6], GRAD_ORDERS[k]))
    for p in range(3):
        gate = dot(n2[...], ffn_panel(wf, 0, p))
        up = dot(n2[...], ffn_panel(wf, 1, p))
        sig = jax.nn.sigmoid(gate)
        a = gate * sig
        act[p] = a
        slope[p] = up * (sig * (1.0 + gate * (1.0 - sig)))
        hid[p] = (a * up).astype(bf16)
        store_ffn_panel(grad, 2, p, dot(ogt[...], hid[p]).astype(bf16))
        jobs[0].start(2, (p,))
    gathers[3].finish(2)
    for p in range(3):
        grad_hidden = dot(ogb[...].reshape(256, 768), ffn_panel(wf, 2, p))
        d_gate = (grad_hidden * slope[p]).astype(bf16)
        d_up = (grad_hidden * act[p]).astype(bf16)
        acc[...] += dot_nt(d_gate, ffn_panel(wf, 0, p)) + dot_nt(d_up, ffn_panel(wf, 1, p))
        store_ffn_panel(grad, 0, p, dot(n2t[...], d_gate).astype(bf16))
        jobs[1].start(2, (p,))
        store_ffn_panel(grad, 1, p, dot(n2t[...], d_up).astype(bf16))
    s_acc = swap(acc, accr)
    outp[...] = jnp.zeros_like(outp)
    for p in range(3):
        outp[...] += dot_nt(hid[p], ffn_panel(wf, 2, p))
    s_out = swap(outp.at[their_rows, :], outr)
    dkv[...] = jnp.zeros_like(dkv)
    dq_t[pl.ds(192, 64), :] = jnp.zeros((64, 512), f32)
    net.arrive(accr, s_acc)
    middle = mid[...]
    r2 = inverse_rms(middle)
    a = acc[...] + accr[...]
    scaled = middle * r2
    grad_middle = ogb[...].reshape(256, 768).astype(f32) + r2 * (
        a - scaled * jnp.mean(a * scaled, axis=-1, keepdims=True)
    )
    por[...] = grad_middle
    branch[...] = grad_middle.astype(bf16)
    for y2 in range(2):
        r = pl.ds(y2 * 192, 192)
        v = dot_nt(branch[:, :384], wo[0, c, r, :]) + dot_nt(branch[:, 384:], wo[1, c, r, :])
        for s in range(2):
            gm[y2 * 2 + s] = v[s * 128 : (s + 1) * 128, :].astype(bf16)
    i_g = net.take()
    for y2 in range(2):
        for s in range(2):
            mine = jnp.logical_and(c * 2 + y2 == y, jnp.logical_and(zl == s, zl == c))
            net.send_or_keep(gm.at[y2 * 2 + s], go.at[y], i_g, device(at, y=c * 2 + y2, zl=s, c=zl), mine)
    net.left_if(keeps, gm.at[0:3], i_g)
    net.left_if(jnp.logical_not(keeps), gm, i_g)
    for ch in range(2):
        for y2 in range(2):
            dwo[ch, pl.ds(y2 * 192, 192), :] = dot_tn(mix[y2], branch[:, ch * 384 : (ch + 1) * 384]).astype(bf16)
    s_dw = swap(dwo.at[1 - c], dwr)
    net.arrive(outr, s_out)
    outputs[...] = (mid[own_rows, :] + (outp[own_rows, :] + outr[...])).astype(bf16)
    net.arrive(dwr, s_dw)
    for p in range(3):
        for yy in range(4):
            for xx in range(4):
                for low in range(2):
                    r = (xx * 2 + low) * 48 + p * 16
                    own_place, their_place = ((p, yy, xx, h * 2 + low) for h in (c, 1 - c))
                    own, their = jnp.zeros((16, 128), bf16), jnp.zeros((16, 128), bf16)
                    if yy < 3:
                        own = dwo[c, pl.ds(r, 16), pl.ds(yy * 128, 128)]
                        their = dwr[pl.ds(r, 16), pl.ds(yy * 128, 128)]
                    put_grad(grad, 3, own_place, own)
                    put_grad(grad, 3, their_place, their)
    jobs[2].start(2)

    jobs[0].forward()
    net.arrive(go, i_g)
    for h in range(3):
        backward_head(h, q, kv, own_qpos, kpos, lse, go, dkv, dq_t)
        if h == 0:
            jobs[1].forward()
        if h == 1:
            jobs[0].finish(2)
            jobs[0].start(1)
    dkv_s[...] = dkv[1 - c].astype(bf16)
    s_k = swap(dkv_s, dkv_r)
    dq = dq_t[...].T * 0.125
    for yy in range(4):
        r = pl.ds(yy * 128, 128)
        v = dq[yy * 128 : (yy + 1) * 128, :]
        dp[r, 384:512] = turn(v[:, :128], cosine[yy], -sine[yy]).astype(bf16)
        dp[r, 512:] = turn(v[:, 128:], cosine[yy], -sine[yy]).astype(bf16)
    jobs[2].forward()
    net.arrive(dkv_r, s_k)
    for yy in range(4):
        r = pl.ds(yy * 128, 128)
        v = dkv[c, r, :] + dkv_r[r, :].astype(f32)
        dp[r, :128] = turn(v[:, :128], cosine[yy], -sine[yy]).astype(bf16)
        dp[r, 128:256] = turn_first_half(v[:, 128:256], cosine[yy], -sine[yy]).astype(bf16)
        dp[r, 256:384] = v[:, 256:].astype(bf16)
    for bx, bz, rows in row_blocks(dot(xnt[...], dp[:, :384]).astype(bf16)):
        wide_d[0, bx, bz] = rows[:, :256]
        narrow_d[bz, bx] = rows[:, 256:]
    for bx, bz, rows in row_blocks(dot(xnt[...], dp[:, 384:]).astype(bf16)):
        wide_d[1, bx, bz] = rows
    s_w, s_n = swap(wide_d.at[1 - c], wide_r), net.take()
    pl.when(c == 1)(lambda: net.send(narrow_d, narrow_r, s_n, partner))
    net.left_if(c == 1, narrow_d, s_n)
    a_kv = dot_nt(dp[:, :384], attention_panel(wide_w, narrow_w, 0))
    a_q = dot_nt(dp[:, 384:], attention_panel(wide_w, narrow_w, 1))
    a_s[...] = (a_kv + a_q).astype(bf16).reshape(4, 128, 768)
    i_a, i_a2 = net.take(), net.take()
    net.send(a_s.at[(y + 2) % 4], a_got.at[2], i_a, device(moved(at, "y", 4 - d)), i_a2)
    net.send(a_s.at[(y + d + 4) % 4], a_got.at[0], i_a, device(moved(at, "y", d)))
    net.left(a_got.at[0:2], i_a)
    net.arrive(wide_r, s_w)
    wide_t[...] = (wide_d[c].astype(f32) + wide_r[...].astype(f32)).astype(bf16)

    @pl.when(first)
    def _():
        net.arrive(narrow_r, s_n)
        narrow_t[...] = (narrow_d[...].astype(f32) + narrow_r[...].astype(f32)).astype(bf16)

    i_wx = to_line("x", lambda step: wide_t.at[(x + step) % 4], lambda kind: wide_1.at[kind])
    net.left(wide_1, i_wx)
    i_nz = to_line("z", lambda step: narrow_t.at[(z + step) % 4], lambda kind: narrow_1.at[kind], first)
    net.left_if(first, narrow_1, i_nz)
    jobs[1].finish(2)
    jobs[1].start(1)
    jobs[0].finish(1)
    jobs[0].start(0)

    def four(own, got):
        v = own.astype(f32)
        for kind in range(3):
            v = v + got[kind].astype(f32)
        return v

    net.arrive(a_got.at[2], i_a2)
    a_on[...] = (a_s[(y - d + 4) % 4].astype(f32) + a_got[2].astype(f32)).astype(bf16)
    net.send(a_on, a_got.at[1], i_a2, device(moved(at, "y", 4 - d)), i_a)
    net.left(a_on, i_a2)
    net.arrive(wide_1, i_wx)
    wide_2[...] = four(wide_t[x], wide_1).astype(bf16)
    i_wz = to_line("z", lambda step: wide_2.at[(z + step) % 4], lambda kind: wide_0.at[kind])
    net.left(wide_0, i_wz)

    @pl.when(first)
    def _():
        net.arrive(narrow_1, i_nz)
        narrow_2[...] = four(narrow_t[z], narrow_1).astype(bf16)

    i_nx = to_line("x", lambda step: narrow_2.at[(x + step) % 4], lambda kind: narrow_0.at[kind], first)
    net.left_if(first, narrow_0, i_nx)
    jobs[2].finish(2)
    jobs[2].start(1)
    net.arrive(a_got.at[0:2], i_a)
    a_sum[...] = (a_s[y].astype(f32) + a_got[0].astype(f32) + a_got[1].astype(f32)).astype(bf16)
    i_z = net.take()
    net.send_or_keep(a_sum, a_own, i_z, device(at, zl=c, c=zl), zl == c)
    net.left_if(zl != c, a_sum, i_z)
    jobs[1].finish(1)
    jobs[1].start(0)
    net.arrive(wide_0, i_wz)
    v = four(wide_2[z], wide_0)
    tall[0], tall[1] = v[:, :128], v[:, 128:]

    @pl.when(first)
    def _():
        net.arrive(narrow_0, i_nx)
        tall[2] = four(narrow_2[x], narrow_0)

    jobs[2].finish(1)
    jobs[2].start(0)
    net.arrive(a_own, i_z)
    v = xb[c].astype(f32)
    r1 = inverse_rms(v)
    scaled = v * r1
    a = a_own[...].astype(f32)
    input_grad[...] = por[own_rows, :] + r1 * (a - scaled * jnp.mean(a * scaled, axis=-1, keepdims=True))
    for j in jobs:
        j.finish(0)
    lowest = [j.levels[3] for j in jobs]
    for cb in range(3):
        for m in range(3):
            tall[3 + m * 3 + cb] = get_sum(lowest, m, cb)
        tall[12, pl.ds(cb * 16, 16), :] = get_sum(lowest, 3, cb)
    for s in range(8):
        for unit in range(13):
            back_s[s, pl.ds(unit * 6, 6), :] = tall[unit, pl.ds(s * 6, 6), :]
        back_s[s, pl.ds(78, 2), :] = jnp.zeros((2, 128), f32)
    back_p[...] = back_s[...].astype(bf16)
    i_b = net.take()
    slot = c * 4 + y
    for s in range(8):
        mine = jnp.logical_and(y * 2 + zl == s, zl == c)
        net.send_or_keep(back_p.at[s], back.at[slot], i_b, device(at, y=s // 2, zl=s % 2, c=zl), mine)
    net.left_if(zl == c, back_p.at[0:7], i_b)
    net.left_if(zl != c, back_p, i_b)
    net.arrive(back, i_b)
    grads[...] = back[...].astype(f32)
    net.drain()


VM = pl.BlockSpec(memory_space=pltpu.VMEM)
SEMS = 61


def layer(*args):
    f, h = f32, bf16

    def blocks(lead, rows, columns=128):
        return (lead + (rows, columns), h)

    scratch = [
        *[(a.shape, a.dtype) for a in args[:5]], (args[7].shape, args[7].dtype),
        ((8, 32, 128), f), ((8, 32, 128), h), ((8, 32, 128), h), ((8, 32, 128), f),
        ((8, 64, 128), f), ((8, 64, 128), h), ((8, 64, 128), h), ((8, 64, 128), f), ((13, 48, 128), f),
        blocks((2, 4, 4), 48, 256), blocks((4, 4), 48), *[blocks((3, 4, 4, 4), r) for r in WEIGHT_JOBS], ((2, 2, 384, 384), h),
        ((4, 128, 768), h), ((4, 128, 768), h), ((768, 512), h), ((4, 128, 128), f),
        ((4, 128, 128), f), ((2, 4, 128, 128), f), ((2, 4, 8, 128), f), ((2, 512, 384), h), ((512, 256), h),
        ((8, 512), f),
        ((192, 512), f), ((4, 128, 192), h), ((2, 2, 128, 192), h),
        ((2, 128, 768), h), ((2, 128, 768), h), ((256, 768), f), ((256, 768), f), ((256, 768), f),
        ((256, 768), h), ((768, 256), h), ((768, 256), h), ((3, 256, 512), f), ((3, 256, 512), f), ((3, 256, 512), h),
        ((256, 768), f), ((256, 768), f), ((256, 768), f), ((128, 768), f), ((256, 768), h), ((2, 384, 384), h),
        ((384, 384), h), ((4, 128, 192), h), *[blocks((3, 4, 4, 4), r) for r in GRAD_JOBS],
        ((4, 128, 192), h), ((2, 512, 384), f), ((512, 384), h), ((512, 384), h), ((256, 512), f), ((512, 640), h),
        blocks((2, 4, 4), 48, 256), blocks((4, 4), 48), blocks((4, 4), 48, 256), blocks((4, 4), 48),
        blocks((4, 4), 48, 256), blocks((4, 4), 48), blocks((3, 4), 48, 256), blocks((3, 4), 48),
        blocks((4,), 48, 256), blocks((4,), 48), blocks((3,), 48, 256), blocks((3,), 48),
        ((4, 128, 768), h), ((3, 128, 768), h), ((128, 768), h), ((128, 768), h), ((128, 768), h),
        ((8, 80, 128), f), ((8, 80, 128), h), ((8, 80, 128), h),
    ]
    for r in GRAD_JOBS:
        scratch += [blocks((3,) + (4,) * k, r) for k in (2, 1, 0)]
        scratch += [blocks((3, 3) + (4,) * k, r) for k in (2, 1, 0)]
        scratch += [blocks((3, 4, 4), r)]
    return pl.pallas_call(
        layer_body,
        out_shape=(
            jax.ShapeDtypeStruct((128, 768), bf16),
            jax.ShapeDtypeStruct((128, 768), f32),
            jax.ShapeDtypeStruct((8, 80, 128), f32),
        ),
        in_specs=[pl.BlockSpec(memory_space=pl.ANY)] * len(args),
        out_specs=(VM,) * 3,
        scratch_shapes=[pltpu.VMEM(s, t) for s, t in scratch]
        + [pltpu.SemaphoreType.DMA((SEMS,))] * 2
        + [pltpu.SemaphoreType.DMA((8,))],
        compiler_params=pltpu.CompilerParams(collective_id=0, has_side_effects=True, vmem_limit_bytes=60 << 20),
    )(*args)


def adam_step(master, gradient, moment_one, moment_two, rate_value, decay_value):
    moment_one = BETA_FIRST * moment_one + (1.0 - BETA_FIRST) * gradient
    moment_two = BETA_SECOND * moment_two + (1.0 - BETA_SECOND) * gradient * gradient
    first_hat = moment_one / (1.0 - BETA_FIRST**STEP)
    second_hat = moment_two / (1.0 - BETA_SECOND**STEP)
    updated = master - rate_value * (
        first_hat / (jnp.sqrt(second_hat) + ADAM_EPS) + decay_value * master
    )
    return (moment_one, moment_two, updated)


def owner_body(
    grads, outputs, input_grad,
    qkv, qkv_m, qkv_s, out, out_m, out_s, gu, gu_m, gu_s, dt, dt_m, dt_s, gains, gains_m, gains_s,
    outputs_o, input_grad_o,
    qkv_mo, qkv_so, qkv_o, out_mo, out_so, out_o, gu_mo, gu_so, gu_o, dt_mo, dt_so, dt_o,
    gains_mo, gains_so, gains_o,
):
    outputs_o[...] = outputs[...]
    input_grad_o[...] = input_grad[...]

    def unit(slot, u):
        return grads[slot, pl.ds(u * 6, 6), :]

    eye = lax.broadcasted_iota(jnp.int32, (6, 6), 0) == lax.broadcasted_iota(jnp.int32, (6, 6), 1)
    g_low = gains[...].astype(bf16).astype(f32)
    g_one = jnp.sum(jnp.where(eye, g_low[0:1, :], 0.0), axis=1, keepdims=True)
    g_two = jnp.sum(jnp.where(eye, g_low[1:2, :], 0.0), axis=1, keepdims=True)

    def update(refs, new, columns, gradient, rate, decay):
        w, m, s = refs
        values = adam_step(w[:, columns], gradient, m[:, columns], s[:, columns], rate, decay)
        for to, v in zip(new, values):
            to[:, columns] = v

    def low_times(w, columns, gradient):
        return jnp.sum(w[:, columns].astype(bf16).astype(f32) * gradient, axis=1, keepdims=True)

    def join(a, b):
        return jnp.concatenate([a, b], axis=1)

    rate = D ** (-0.5)
    sum_one = jnp.zeros((6, 1), f32)
    for pair in range(2):
        e, o = 2 * pair, 2 * pair + 1
        u = {(s, k): unit(s, k) for s in (e, o, 4 + e, 4 + o) for k in range(3)}
        tiles = {
            0: (u[4 + e, 0], join(u[4 + e, 1][:, :64], u[4 + o, 0][:, :64]), join(u[4 + o, 0][:, 64:], u[4 + o, 1][:, :64])),
            768: (u[e, 0], join(u[e, 1][:, :64], u[o, 0][:, :64]), join(u[o, 0][:, 64:], u[o, 1][:, :64])),
            1536: (join(u[e, 1][:, 64:], u[e, 2][:, :64]), join(u[e, 2][:, 64:], u[o, 1][:, 64:]), u[o, 2]),
        }
        for first, three in tiles.items():
            for k, t in enumerate(three):
                columns = pl.ds(first + pair * 384 + k * 128, 128)
                sum_one = sum_one + low_times(qkv, columns, t)
                update((qkv, qkv_m, qkv_s), (qkv_mo, qkv_so, qkv_o), columns, t * g_one, rate, WEIGHT_DECAY)
    sum_two = jnp.zeros((6, 1), f32)
    for slot in range(8):
        for cb in range(3):
            f = slot * 384 + cb * 128
            for half in range(2):
                columns = pl.ds(half * 3072 + f, 128)
                t = unit(slot, 3 + half * 3 + cb)
                sum_two = sum_two + low_times(gu, columns, t)
                update((gu, gu_m, gu_s), (gu_mo, gu_so, gu_o), columns, t * g_two, rate, WEIGHT_DECAY)
            update(
                (dt, dt_m, dt_s), (dt_mo, dt_so, dt_o), pl.ds(f, 128), unit(slot, 9 + cb), FF ** (-0.5), WEIGHT_DECAY
            )
        if slot % 4 < 3:
            update(
                (out, out_m, out_s), (out_mo, out_so, out_o), pl.ds((slot // 4) * 384 + (slot % 4) * 128, 128),
                unit(slot, 12), (H * HD * 32 // LEN) ** (-0.5), WEIGHT_DECAY,
            )
    rows = [jnp.sum(jnp.where(eye, v, 0.0), axis=0, keepdims=True) for v in (sum_one, sum_two)]
    values = adam_step(gains[...], jnp.concatenate(rows, axis=0), gains_m[...], gains_s[...], GAIN_RATE, 0.0)
    for to, v in zip((gains_mo, gains_so, gains_o), values):
        to[...] = v


def owners_step(*args):
    shapes = [(args[1].shape, bf16), (args[2].shape, f32)]
    for first in range(3, 18, 3):
        shapes += [(args[first].shape, f32)] * 3
    return pl.pallas_call(
        owner_body,
        out_shape=tuple(jax.ShapeDtypeStruct(s, t) for s, t in shapes),
        in_specs=[VM] * len(args),
        out_specs=(VM,) * len(shapes),
    )(*args)


def body(
    inputs, positions, output_grad,
    qkv_weight, qkv_first, qkv_second, out_weight, out_first, out_second,
    gate_up_weight, gate_up_first, gate_up_second, down_weight, down_first, down_second,
    norm_gains, gains_first, gains_second,
):
    outputs, input_grad, grads = layer(
        qkv_weight, out_weight, gate_up_weight, down_weight.T, norm_gains,
        inputs.reshape(128, D), output_grad.reshape(128, D), positions,
    )
    new = owners_step(
        grads, outputs, input_grad,
        qkv_weight, qkv_first, qkv_second, out_weight, out_first, out_second,
        gate_up_weight, gate_up_first, gate_up_second, down_weight.T, down_first.T, down_second.T,
        norm_gains, gains_first, gains_second,
    )
    return (
        new[0].reshape(1, 128, D), new[1].reshape(1, 128, D), *new[2:11],
        *(v.T for v in new[11:14]), *new[14:],
    )


def solution(mesh):
    token = P("dp", "ctx", None)
    rows, columns = P(("dp", "ctx"), None), P(None, ("dp", "ctx"))
    return jax.shard_map(
        body,
        mesh=mesh,
        in_specs=(token, P("dp", "ctx"), token) + (rows,) * 9 + (columns,) * 6,
        out_specs=(token, token) + (rows,) * 9 + (columns,) * 6,
        check_vma=False,
    )
```

```python
import math

import jax
import jax.numpy as jnp
from jax import lax
from jax.experimental import pallas as pl
from jax.experimental.pallas import tpu as pltpu
from jax.sharding import PartitionSpec as P

D = 768
H = 12
HD = 64
FF = 3072
LEN = 1024
STEP = 10

NORM_EPS = 1e-05
ROPE_BASE = 10000.0
BETA_FIRST = 0.9
BETA_SECOND = 0.95
ADAM_EPS = 1e-08
WEIGHT_DECAY = 0.1
GAIN_RATE = 1.2
MASKED = -1e30

MESH = pl.DeviceIdType.MESH
bf16, f32 = jnp.bfloat16, jnp.float32

ORDERS = (("x", "y", "z"), ("y", "z", "x"), ("z", "x", "y"))
WEIGHT_JOBS = (16, 48, 48, 48)
GRAD_JOBS = (48, 48, 64)
WEIGHT_ORDERS = (ORDERS,) * 4
GRAD_ORDERS = (ORDERS,) * 3


def here():
    dp, ctx = lax.axis_index("dp"), lax.axis_index("ctx")
    return dict(x=(dp // 2) % 4, y=ctx // 2, z=(dp // 8) * 2 + ctx % 2, c=dp % 2)


def low_z(at):
    return at["z"] % 2


def device(at, zl=None, **moved):
    at = dict(at, **moved)
    if zl is not None:
        at["z"] = (at["z"] // 2) * 2 + zl
    return ((at["z"] // 2) * 8 + at["x"] * 2 + at["c"], at["y"] * 2 + at["z"] % 2)


def moved(at, axis, step):
    return dict(at, **{axis: (at[axis] + step + 4) % 4})


def row_block(at):
    return (at["z"] // 2) * 8 + at["x"] * 2 + at["z"] % 2


def group_of(at):
    out = []
    me = at["c"] * 8 + at["y"] * 2 + low_z(at)
    for k in range(1, 16):
        other = (me + k) % 16
        out.append(device(at, c=other // 8, y=(other // 2) % 4, zl=other % 2))
    for k in range(1, 4):
        out.append(device(at, x=(at["x"] + k) % 4))
    other_half = dict(at, z=(at["z"] + 2) % 4)
    for low in range(2):
        out.append(device(other_half, zl=low))
    return out


def signal_all(peers):
    barrier = pltpu.get_barrier_semaphore()
    for p in peers:
        pl.semaphore_signal(barrier, inc=1, device_id=p, device_id_type=MESH)


def wait_all(peers):
    pl.semaphore_wait(pltpu.get_barrier_semaphore(), len(peers))


class Net:
    def __init__(self, at, send_sem, recv_sem):
        self.at, self.send_sem, self.recv_sem = at, send_sem, recv_sem
        self.used = 0
        self.ends = []

    def take(self):
        self.used += 1
        return self.used - 1

    def send(self, src, dst, i, to, r=None):
        pltpu.make_async_remote_copy(
            src_ref=src, dst_ref=dst, send_sem=self.send_sem.at[i], recv_sem=self.recv_sem.at[i if r is None else r],
            device_id=to, device_id_type=MESH,
        ).start()

    def send_or_keep(self, src, dst, i, to, mine):
        pl.when(jnp.logical_not(mine))(lambda: self.send(src, dst, i, to))
        pl.when(mine)(lambda: pltpu.make_async_copy(src, dst, self.recv_sem.at[i]).start())

    def left(self, view, i):
        self.ends.append((None, view, i))

    def left_if(self, condition, view, i):
        self.ends.append((condition, view, i))

    def arrive(self, view, i):
        pltpu.make_async_copy(view, view, self.recv_sem.at[i]).wait()

    def drain(self):
        for condition, view, i in self.ends:
            wait = pltpu.make_async_copy(view, view, self.send_sem.at[i]).wait
            if condition is None:
                wait()
            else:
                pl.when(condition)(wait)


class Gather:
    def __init__(self, net, ref, orders):
        self.net, self.at, self.ref, self.orders = net, net.at, ref, orders
        self.sems = [net.take() for _ in range(4)]
        views = (ref.at[0, 0:3, 0:3, 0], ref.at[0, 0:3, 0:3], ref.at[0:2, 0:3], ref.at[0, 0:3])
        self.views = views
        for view, i in zip(views, self.sems):
            net.left(view, i)

    def view(self, part, at, phase):
        a1, a2, a3 = self.orders[part]
        return self.ref.at[(part, at[a3], at[a2], at[a1])[: 4 - phase]]

    def send(self, part, phase, at, axis, step, i):
        v = self.view(part, at, phase)
        self.net.send(v, v, i, device(moved(self.at, axis, step)))

    def start(self, phase):
        for step in (2, 1, 3) if phase < 2 else (1, 3):
            for part in range(3):
                self.send(part, phase, self.at, self.orders[part][phase], step, self.sems[phase])

    def forward(self):
        d = 1 - 2 * self.at["c"]
        self.net.arrive(self.views[2], self.sems[2])
        for part in range(3):
            axis = self.orders[part][2]
            self.send(part, 2, moved(self.at, axis, -d), axis, d, self.sems[3])

    def finish(self, phase):
        k = phase if phase < 2 else 3
        self.net.arrive(self.views[k], self.sems[k])


class Scatter:
    def __init__(self, net, levels, got, turned, orders):
        self.net, self.at, self.orders = net, net.at, orders
        self.levels, self.got, self.turned = levels, got, turned
        self.sems = [net.take() for _ in range(4)]
        self.views = (got[2], got[1], got[0].at[0:2], got[0].at[2])
        for view, i in zip(self.views, self.sems):
            net.left(view, i)

    def level(self, part, phase, i):
        return self.levels[2 - phase].at[part, i]

    def slot(self, part, phase, kind):
        return self.got[2 - phase].at[kind, part]

    def go(self, src, part, phase, kind, axis, step, s, r):
        self.net.send(src, self.slot(part, phase, kind), s, device(moved(self.at, axis, step)), r)

    def add(self, to, refs, phase):
        def one(index):
            total = refs[0][index].astype(f32)
            for r in refs[1:]:
                total = total + r[index].astype(f32)
            to[index] = total.astype(to.dtype)

        if phase == 2:
            pl.loop(0, 4)(lambda b: one((b,)))
        else:
            one(...)

    def start(self, phase, parts=range(3)):
        d = 1 - 2 * self.at["c"]
        i = self.sems[phase]
        for part in parts:
            axis = self.orders[part][phase]
            me = self.at[axis]
            if phase < 2:
                for kind, step in enumerate((2, 1, 3)):
                    self.go(self.level(part, phase, (me + step) % 4), part, phase, kind, axis, step, i, i)
            else:
                self.go(self.level(part, phase, (me + 2) % 4), part, phase, 2, axis, 4 - d, i, self.sems[3])
                self.go(self.level(part, phase, (me + d + 4) % 4), part, phase, 0, axis, d, i, i)

    def forward(self):
        d = 1 - 2 * self.at["c"]
        self.net.arrive(self.views[3], self.sems[3])
        for part in range(3):
            axis = self.orders[part][2]
            me = self.at[axis]
            to = self.turned.at[part]
            self.add(to, [self.level(part, 2, (me - d + 4) % 4), self.slot(part, 2, 2)], 2)
            self.go(to, part, 2, 1, axis, 4 - d, self.sems[3], self.sems[2])

    def finish(self, phase):
        self.net.arrive(self.views[phase], self.sems[phase])
        for part in range(3):
            me = self.at[self.orders[part][phase]]
            kinds = (0, 1, 2) if phase < 2 else (0, 1)
            to = self.levels[3 - phase].at[part]
            self.add(to, [self.level(part, phase, me)] + [self.slot(part, phase, k) for k in kinds], phase)


def dot(a, b):
    return jnp.dot(a, b, preferred_element_type=f32)


def dot_nt(a, b):
    return lax.dot_general(a, b, (((1,), (1,)), ((), ())), preferred_element_type=f32)


def dot_tn(a, b):
    return lax.dot_general(a, b, (((0,), (0,)), ((), ())), preferred_element_type=f32)


def inverse_rms(v):
    return lax.rsqrt(jnp.mean(v * v, axis=-1, keepdims=True) + NORM_EPS)


def tables(place, freq):
    angle = place * freq
    lane = lax.broadcasted_iota(jnp.int32, place.shape, 1)
    sine = jnp.sin(angle)
    return jnp.cos(angle), jnp.where(lane % 64 < 32, -sine, sine)


def turn(v, cosine, sine):
    lane = lax.broadcasted_iota(jnp.int32, v.shape, 1)
    swapped = jnp.where(lane % 64 < 32, pltpu.roll(v, 96, 1), pltpu.roll(v, 32, 1))
    return v * cosine + swapped * sine


def turn_first_half(v, cosine, sine):
    lane = lax.broadcasted_iota(jnp.int32, v.shape, 1)
    return jnp.where(lane < 64, turn(v, cosine, sine), v)


def ffn_index(orders, part, y, x, z):
    place = dict(x=x, y=y, z=z)
    a1, a2, a3 = orders[part]
    return (part, place[a3], place[a2], place[a1])


WEIGHT_ROWS = ((1, 0, 48), (2, 0, 48), (3, 0, 48), (0, 0, 16))
GRAD_ROWS = ((1, 0, 48), (2, 0, 48), (0, 0, 48), (2, 48, 16))


def put_weight(refs, matrix, place, value):
    job, first, count = WEIGHT_ROWS[matrix]
    refs[job][ffn_index(WEIGHT_ORDERS[job], *place) + (pl.ds(first, count), slice(None))] = value


def get_weight(refs, matrix, place):
    job, first, count = WEIGHT_ROWS[matrix]
    return refs[job][ffn_index(WEIGHT_ORDERS[job], *place) + (pl.ds(first, count), slice(None))]


def put_grad(refs, matrix, place, value):
    job, first, count = GRAD_ROWS[matrix]
    refs[job][ffn_index(GRAD_ORDERS[job], *place) + (pl.ds(first, count), slice(None))] = value


def get_sum(refs, matrix, part):
    job, first, count = GRAD_ROWS[matrix]
    return refs[job][part, pl.ds(first, count), :].astype(f32)


def rows_of(pick):
    return jnp.concatenate([pick(x, zh * 2 + zl) for zh in range(2) for x in range(4) for zl in range(2)], axis=0)


def row_blocks(value):
    for zh in range(2):
        for x in range(4):
            for zl in range(2):
                r = (zh * 8 + x * 2 + zl) * 48
                yield x, zh * 2 + zl, value[r : r + 48, :]


def ffn_panel(wf, matrix, p):
    return jnp.concatenate(
        [rows_of(lambda x, z: get_weight(wf, matrix, (p, y, x, z))) for y in range(4)], axis=1
    )


def store_ffn_panel(g, matrix, p, value):
    for x, z, rows in row_blocks(value):
        for y in range(4):
            put_grad(g, matrix, (p, y, x, z), rows[:, y * 128 : (y + 1) * 128])


def attention_panel(wide, narrow, which):
    if which == 1:
        return rows_of(lambda x, z: wide[1, x, z])
    return rows_of(lambda x, z: jnp.concatenate([wide[0, x, z], narrow[z, x]], axis=1))


def head_parts(h, kv):
    k = jnp.concatenate([kv[0, :, h * 64 : (h + 1) * 64], kv[1, :, h * 64 : (h + 1) * 64]], axis=0)
    o = 192 + h * 64
    v = jnp.concatenate([kv[0, :, o : o + 64], kv[1, :, o : o + 64]], axis=0)
    return k, v


def query_positions(qpos, half):
    return jnp.concatenate([qpos[half * 2], qpos[half * 2 + 1]], axis=1)[0:1, :]


def masked_scores(k, q_part, kpos, q_row):
    s = dot_nt(k, q_part)
    kp = kpos[...].reshape(1024, 128)
    allowed = jnp.concatenate([kp, kp], axis=1) <= q_row
    return jnp.where(allowed, s, MASKED)


def forward_head(h, q, kv, qpos, kpos, lse, mixed_t):
    k, v = head_parts(h, kv)
    for half in range(2):
        q_part = q[pl.ds(half * 256, 256), h * 64 : (h + 1) * 64]
        s = masked_scores(k, q_part, kpos, query_positions(qpos, half))
        highest = jnp.max(s, axis=0, keepdims=True)
        e = jnp.exp(s - highest)
        total = jnp.sum(e, axis=0, keepdims=True)
        p = (e * (1.0 / total)).astype(bf16)
        mixed_t[pl.ds(h * 64, 64), pl.ds(half * 256, 256)] = dot_tn(v, p)
        lse[pl.ds(h, 1), pl.ds(half * 256, 256)] = highest + jnp.log(total)


def backward_head(h, q, kv, qpos, kpos, lse, go, dkv, dq_t):
    k, v = head_parts(h, kv)
    for half in range(2):
        rows = pl.ds(half * 256, 256)
        q_part = q[rows, h * 64 : (h + 1) * 64]
        g_part = go[pl.ds(half * 2, 2), :, h * 64 : (h + 1) * 64].reshape(256, 64)
        s = masked_scores(k, q_part, kpos, query_positions(qpos, half))
        p = jnp.exp(s - lse[pl.ds(h, 1), rows])
        dp = dot_nt(v, g_part)
        centre = jnp.sum(p * dp, axis=0, keepdims=True)
        ds = (p * (dp - centre)).astype(bf16)
        dv = dot(p.astype(bf16), g_part)
        dk = dot(ds, q_part)
        dq_t[pl.ds(h * 64, 64), rows] = dot_tn(k, ds)
        for cc in range(2):
            dkv[cc, :, h * 64 : (h + 1) * 64] += dk[cc * 512 : (cc + 1) * 512]
            dkv[cc, :, 192 + h * 64 : 192 + (h + 1) * 64] += dv[cc * 512 : (cc + 1) * 512]


def as_column(eye, row):
    return jnp.sum(jnp.where(eye, row, 0.0), axis=1, keepdims=True)


def low_gains(gains):
    eye = lax.broadcasted_iota(jnp.int32, (6, 6), 0) == lax.broadcasted_iota(jnp.int32, (6, 6), 1)
    g_low = gains[...].astype(bf16).astype(f32)
    return as_column(eye, g_low[0:1, :]), as_column(eye, g_low[1:2, :])


def cut_attention(qkv, g_one, positions, stage):
    place = positions[...]
    place = jnp.concatenate([(place // 64).astype(f32), (place % 64).astype(f32)], axis=0)
    zero = jnp.zeros((6, 64), f32)
    for yy in range(4):
        o = yy * 192
        q_y = qkv[:, o : o + 192].astype(bf16).astype(f32) * g_one
        k_y = qkv[:, 768 + o : 768 + o + 192].astype(bf16).astype(f32) * g_one
        v_y = qkv[:, 1536 + o : 1536 + o + 192].astype(bf16).astype(f32) * g_one
        stage[yy, pl.ds(0, 6), :] = k_y[:, :128]
        stage[yy, pl.ds(6, 6), :] = jnp.concatenate([k_y[:, 128:], v_y[:, :64]], axis=1)
        stage[yy, pl.ds(12, 6), :] = v_y[:, 64:]
        stage[4 + yy, pl.ds(0, 6), :] = q_y[:, :128]
        stage[4 + yy, pl.ds(6, 6), :] = jnp.concatenate([q_y[:, 128:], zero], axis=1)
        stage[4 + yy, pl.ds(12, 6), :] = jnp.zeros((6, 128), f32)
    for slot in range(8):
        stage[slot, pl.ds(18, 2), :] = place
        stage[slot, pl.ds(20, 12), :] = jnp.zeros((12, 128), f32)


def cut_rest(out, gu, dt, g_two, stage):
    def put(slot, unit, v):
        stage[slot, pl.ds(unit * 6, 6), :] = v

    for slot in range(8):
        for cb in range(3):
            f = slot * 384 + cb * 128
            put(slot, cb, gu[:, f : f + 128].astype(bf16).astype(f32) * g_two)
            put(slot, 3 + cb, gu[:, 3072 + f : 3072 + f + 128].astype(bf16).astype(f32) * g_two)
            put(slot, 6 + cb, dt[:, f : f + 128])
        cc, yy = slot // 4, slot % 4
        if yy < 3:
            put(slot, 9, out[:, cc * 384 + yy * 128 : cc * 384 + (yy + 1) * 128])
        else:
            put(slot, 9, jnp.zeros((6, 128), f32))
        stage[slot, pl.ds(60, 4), :] = jnp.zeros((4, 128), f32)


def layer_body(
    qkv_h, out_h, gu_h, dt_h, gains_h, x_h, og_h, positions_h,
    outputs, input_grad, grads,
    qkv, out, gu, dt, gains, positions,
    stage_a, pieces_a, recv_a, wide_a, stage_f, pieces_f, recv_f, wide_f, tall,
    wide_w, narrow_w, wf0, wf1, wf2, wf3, wo, xg, xn, xnt, cosine, sine, kpos, qpos, kv, q, lse,
    mixed_t, mixed_s, mixed,
    xb, ogb, po, por, mid, n2, n2t, ogt, act, slope, hid, acc, accr, outp, outr, branch, dwo, dwr, gm, g0, g1, g2,
    go, dkv, dkv_s, dkv_r, dq_t, dp, wide_d, narrow_d, wide_r, narrow_r, wide_t, narrow_t,
    wide_1, narrow_1, wide_2, narrow_2, wide_0, narrow_0, a_s, a_got, a_on, a_sum, a_own, back_s, back_p, back,
    *rest,
):
    per_job, (send_sem, recv_sem, load_sem) = rest[:-3], rest[-3:]
    at = here()
    c, y, zl = at["c"], at["y"], low_z(at)
    d = 1 - 2 * c
    net = Net(at, send_sem, recv_sem)
    peers = group_of(at)
    partner = device(at, c=1 - c)
    rb = row_block(at)
    own_rows = pl.ds(pl.multiple_of(c * 128, 128), 128)
    their_rows = pl.ds(pl.multiple_of((1 - c) * 128, 128), 128)

    def swap(src, dst):
        i = net.take()
        net.send(src, dst, i, partner)
        net.left(src, i)
        return i

    def to_line(axis, pick, slot, only=None):
        i = net.take()

        def go():
            for kind, step in enumerate((2, 1, 3)):
                net.send(pick(step), slot(kind), i, device(moved(at, axis, step)))

        if only is None:
            go()
        else:
            pl.when(only)(go)
        return i

    first = c == 0

    signal_all(peers[::-1])
    loads = [
        pltpu.make_async_copy(src, dst, load_sem.at[i])
        for i, (src, dst) in enumerate(
            (
                (qkv_h, qkv), (gains_h, gains), (positions_h, positions), (x_h, xb.at[c]),
                (gu_h, gu), (dt_h, dt), (out_h, out), (og_h, ogb.at[c]),
            )
        )
    ]
    for copy in loads:
        copy.start()
    for copy in loads[:3]:
        copy.wait()
    g_one, g_two = low_gains(gains)
    cut_attention(qkv, g_one, positions, stage_a)
    pieces_a[...] = stage_a[...].astype(bf16)
    for copy in loads[3:]:
        copy.wait()
    cut_rest(out, gu, dt, g_two, stage_f)
    pieces_f[...] = stage_f[...].astype(bf16)
    wait_all(peers)

    source = y * 2 + zl

    def to_group(pieces, recv):
        i = net.take()
        for cc in range(2):
            for yy in range(4):
                mine = jnp.logical_and(zl == c, jnp.logical_and(y == yy, c == cc))
                net.send_or_keep(pieces.at[cc * 4 + yy], recv.at[source], i, device(at, y=yy, zl=c, c=cc), mine)
        net.left_if(zl == c, pieces.at[0:7], i)
        net.left_if(zl != c, pieces, i)
        return i

    r_a = to_group(pieces_a, recv_a)
    r_f = to_group(pieces_f, recv_f)
    i_x = net.take()
    net.send_or_keep(xb.at[c], xg.at[y], i_x, device(at, zl=c, c=zl), zl == c)
    net.left_if(zl != c, xb.at[c], i_x)
    i_xb = swap(xb.at[c], xb.at[c])
    i_ob = swap(ogb.at[c], ogb.at[c])

    net.arrive(recv_a, r_a)
    wide_a[...] = recv_a[...].astype(f32)
    for unit in range(3):
        for s in range(8):
            tall[unit, pl.ds(s * 6, 6), :] = wide_a[s, pl.ds(unit * 6, 6), :]
    x, z = at["x"], at["z"]
    wide_w[c, x, z] = jnp.concatenate([tall[0], tall[1]], axis=1).astype(bf16)

    @pl.when(first)
    def _():
        narrow_w[z, x] = tall[2].astype(bf16)

    block = wide_w.at[c, x, z]
    i_wz = to_line("z", lambda step: block, lambda kind: block)
    net.left(wide_w.at[0, 0, 0:3], i_wz)
    thin = narrow_w.at[z, x]
    i_nx = to_line("x", lambda step: thin, lambda kind: thin, first)
    net.left_if(first, narrow_w.at[0, 0:3], i_nx)
    net.arrive(xg.at[y], i_x)
    i_y, i_y2 = net.take(), net.take()
    for step in (1, 3):
        net.send(xg.at[y], xg.at[y], i_y, device(moved(at, "y", step)))
    net.left(xg.at[0:2], i_y)

    net.arrive(recv_f, r_f)
    wide_f[...] = recv_f[...].astype(f32)
    for unit in range(10):
        for s in range(8):
            tall[3 + unit, pl.ds(s * 6, 6), :] = wide_f[s, pl.ds(unit * 6, 6), :]
    wf = (wf0, wf1, wf2, wf3)
    for cb in range(3):
        place = (cb, y, x, z)
        for m in range(3):
            put_weight(wf, m, place, tall[3 + m * 3 + cb].astype(bf16))
        put_weight(wf, 3, place, tall[12, pl.ds(cb * 16, 16), :].astype(bf16))
    jobs = [Gather(net, ref, orders) for ref, orders in zip(wf, WEIGHT_ORDERS)]
    for j in jobs:
        j.start(0)
    net.arrive(wide_w.at[0, 0, 0:3], i_wz)
    row = wide_w.at[c, x]
    i_wx = to_line("x", lambda step: row, lambda kind: row)
    net.left(wide_w.at[0, 0:3], i_wx)
    pl.when(first)(lambda: net.arrive(narrow_w.at[0, 0:3], i_nx))
    thin_row = narrow_w.at[z]
    i_nz = to_line("z", lambda step: thin_row, lambda kind: thin_row, first)
    net.left_if(first, narrow_w.at[0:3], i_nz)

    for s in range(8):
        row = wide_a[s, pl.ds(18, 1), :] * 64.0 + wide_a[s, pl.ds(19, 1), :]
        rows = jnp.broadcast_to(row, (128, 128))
        kpos[s % 2, s // 2] = rows.T
        qpos[s % 2, s // 2] = rows[:8]
    lane = lax.broadcasted_iota(jnp.int32, (1, 128), 1) % 32
    freq = jnp.exp(lane.astype(f32) * (-2.0 * math.log(ROPE_BASE) / HD))
    for yy in range(4):
        cosine[yy], sine[yy] = tables(kpos[c, yy], freq)
    net.arrive(xg.at[0:2], i_y)
    behind = xg.at[(y - d + 4) % 4]
    net.send(behind, behind, i_y2, device(moved(at, "y", d)))
    net.left(xg.at[0], i_y2)
    for j in jobs:
        j.finish(0)
        j.start(1)

    def normalize(yy):
        v = xg[yy].astype(f32)
        xn[yy] = (v * inverse_rms(v)).astype(bf16)

    for step in (0, 1, 3):
        normalize((y + step) % 4)
    net.arrive(xg.at[0], i_y2)
    normalize((y + 2) % 4)
    jobs[0].finish(1)
    jobs[0].start(2)
    jobs[1].finish(1)
    jobs[1].start(2)
    jobs[2].finish(1)
    jobs[2].start(2)
    jobs[3].finish(1)
    jobs[3].start(2)
    net.arrive(wide_w.at[0, 0:3], i_wx)
    e_w, e_n = swap(wide_w.at[c], wide_w.at[c]), net.take()

    @pl.when(first)
    def _():
        net.arrive(narrow_w.at[0:3], i_nz)
        net.send(narrow_w, narrow_w, e_n, partner)

    net.left_if(first, narrow_w, e_n)
    net.arrive(wide_w.at[1 - c], e_w)
    pl.when(c == 1)(lambda: net.arrive(narrow_w, e_n))

    w_kv = attention_panel(wide_w, narrow_w, 0)
    w_q = attention_panel(wide_w, narrow_w, 1)
    for yy in range(4):
        r = pl.ds(yy * 128, 128)
        kv_y = dot(xn[yy], w_kv)
        kv[c, r, :128] = turn(kv_y[:, :128], cosine[yy], sine[yy]).astype(bf16)
        kv[c, r, 128:256] = turn_first_half(kv_y[:, 128:256], cosine[yy], sine[yy]).astype(bf16)
        kv[c, r, 256:] = kv_y[:, 256:].astype(bf16)
    e_k = swap(kv.at[c], kv.at[c])
    for yy in range(4):
        r = pl.ds(yy * 128, 128)
        q_y = dot(xn[yy], w_q)
        q[r, :128] = (turn(q_y[:, :128], cosine[yy], sine[yy]).astype(bf16) * 0.125).astype(bf16)
        q[r, 128:] = (turn(q_y[:, 128:], cosine[yy], sine[yy]).astype(bf16) * 0.125).astype(bf16)
    net.arrive(kv.at[1 - c], e_k)
    own_qpos = qpos.at[c]
    forward_head(0, q, kv, own_qpos, kpos, lse, mixed_t)
    forward_head(1, q, kv, own_qpos, kpos, lse, mixed_t)
    forward_head(2, q, kv, own_qpos, kpos, lse, mixed_t)
    mix = mixed_t[...].T.astype(bf16)
    for yy in range(4):
        mixed_s[yy] = mix[yy * 128 : (yy + 1) * 128, :]
    i_m = net.take()
    keeps = jnp.logical_and(zl == c, y // 2 == c)
    for yy in range(4):
        net.send_or_keep(
            mixed_s.at[yy], mixed.at[zl, y % 2], i_m, device(at, y=yy, zl=c, c=y // 2), jnp.logical_and(y == yy, keeps)
        )
    net.left_if(keeps, mixed_s.at[0:3], i_m)
    net.left_if(jnp.logical_not(keeps), mixed_s, i_m)
    xnt[...] = xn[...].reshape(512, 768).T
    net.arrive(ogb.at[1 - c], i_ob)
    net.arrive(xb.at[1 - c], i_xb)
    ogt[...] = ogb[...].reshape(256, 768).T
    jobs[0].forward()
    jobs[1].forward()
    jobs[2].forward()
    jobs[3].forward()
    jobs[0].finish(2)
    for p in range(3):
        for yy in range(3):
            for zz in range(4):
                for xx in range(4):
                    r = (xx * 2 + zz % 2) * 48 + p * 16
                    wo[c, zz // 2, pl.ds(r, 16), pl.ds(yy * 128, 128)] = get_weight(wf, 3, (p, yy, xx, zz))
    e_o = swap(wo.at[c], wo.at[c])
    net.arrive(mixed, i_m)
    net.arrive(wo.at[1 - c], e_o)

    mix = [mixed[:, y2].reshape(256, 192) for y2 in range(2)]
    for ch in range(2):
        po[:, pl.ds(ch * 384, 384)] = dot(mix[0], wo[ch, c, :192, :]) + dot(mix[1], wo[ch, c, 192:, :])
    s_po = swap(po, por)
    acc[...] = jnp.zeros_like(acc)
    net.arrive(por, s_po)
    middle = xb[...].reshape(256, 768).astype(f32) + (po[...] + por[...])
    mid[...] = middle
    n2[...] = (middle * inverse_rms(middle)).astype(bf16)
    n2t[...] = n2[...].T
    jobs[1].finish(2)
    jobs[2].finish(2)

    grad = (g0, g1, g2)

    gathers = jobs
    jobs = []
    for k in range(3):
        own = per_job[7 * k : 7 * k + 7]
        jobs.append(Scatter(net, (grad[k],) + own[:3], own[3:6], own[6], GRAD_ORDERS[k]))
    for p in range(3):
        gate = dot(n2[...], ffn_panel(wf, 0, p))
        up = dot(n2[...], ffn_panel(wf, 1, p))
        sig = jax.nn.sigmoid(gate)
        a = gate * sig
        act[p] = a
        slope[p] = up * (sig * (1.0 + gate * (1.0 - sig)))
        hid[p] = (a * up).astype(bf16)
        store_ffn_panel(grad, 2, p, dot(ogt[...], hid[p]).astype(bf16))
        jobs[0].start(2, (p,))
    gathers[3].finish(2)
    for p in range(3):
        grad_hidden = dot(ogb[...].reshape(256, 768), ffn_panel(wf, 2, p))
        d_gate = (grad_hidden * slope[p]).astype(bf16)
        d_up = (grad_hidden * act[p]).astype(bf16)
        acc[...] += dot_nt(d_gate, ffn_panel(wf, 0, p)) + dot_nt(d_up, ffn_panel(wf, 1, p))
        store_ffn_panel(grad, 0, p, dot(n2t[...], d_gate).astype(bf16))
        jobs[1].start(2, (p,))
        store_ffn_panel(grad, 1, p, dot(n2t[...], d_up).astype(bf16))
    s_acc = swap(acc, accr)
    outp[...] = jnp.zeros_like(outp)
    for p in range(3):
        outp[...] += dot_nt(hid[p], ffn_panel(wf, 2, p))
    s_out = swap(outp.at[their_rows, :], outr)
    dkv[...] = jnp.zeros_like(dkv)
    dq_t[pl.ds(192, 64), :] = jnp.zeros((64, 512), f32)
    net.arrive(accr, s_acc)
    middle = mid[...]
    r2 = inverse_rms(middle)
    a = acc[...] + accr[...]
    scaled = middle * r2
    grad_middle = ogb[...].reshape(256, 768).astype(f32) + r2 * (
        a - scaled * jnp.mean(a * scaled, axis=-1, keepdims=True)
    )
    por[...] = grad_middle
    branch[...] = grad_middle.astype(bf16)
    for y2 in range(2):
        r = pl.ds(y2 * 192, 192)
        v = dot_nt(branch[:, :384], wo[0, c, r, :]) + dot_nt(branch[:, 384:], wo[1, c, r, :])
        for s in range(2):
            gm[y2 * 2 + s] = v[s * 128 : (s + 1) * 128, :].astype(bf16)
    i_g = net.take()
    for y2 in range(2):
        for s in range(2):
            mine = jnp.logical_and(c * 2 + y2 == y, jnp.logical_and(zl == s, zl == c))
            net.send_or_keep(gm.at[y2 * 2 + s], go.at[y], i_g, device(at, y=c * 2 + y2, zl=s, c=zl), mine)
    net.left_if(keeps, gm.at[0:3], i_g)
    net.left_if(jnp.logical_not(keeps), gm, i_g)
    for ch in range(2):
        for y2 in range(2):
            dwo[ch, pl.ds(y2 * 192, 192), :] = dot_tn(mix[y2], branch[:, ch * 384 : (ch + 1) * 384]).astype(bf16)
    s_dw = swap(dwo.at[1 - c], dwr)
    net.arrive(outr, s_out)
    outputs[...] = (mid[own_rows, :] + (outp[own_rows, :] + outr[...])).astype(bf16)
    net.arrive(dwr, s_dw)
    for p in range(3):
        for yy in range(4):
            for xx in range(4):
                for low in range(2):
                    r = (xx * 2 + low) * 48 + p * 16
                    own_place, their_place = ((p, yy, xx, h * 2 + low) for h in (c, 1 - c))
                    own, their = jnp.zeros((16, 128), bf16), jnp.zeros((16, 128), bf16)
                    if yy < 3:
                        own = dwo[c, pl.ds(r, 16), pl.ds(yy * 128, 128)]
                        their = dwr[pl.ds(r, 16), pl.ds(yy * 128, 128)]
                    put_grad(grad, 3, own_place, own)
                    put_grad(grad, 3, their_place, their)
    jobs[2].start(2)

    jobs[0].forward()
    net.arrive(go, i_g)
    for h in range(3):
        backward_head(h, q, kv, own_qpos, kpos, lse, go, dkv, dq_t)
        if h == 0:
            jobs[1].forward()
        if h == 1:
            jobs[0].finish(2)
            jobs[0].start(1)
    dkv_s[...] = dkv[1 - c].astype(bf16)
    s_k = swap(dkv_s, dkv_r)
    dq = dq_t[...].T * 0.125
    for yy in range(4):
        r = pl.ds(yy * 128, 128)
        v = dq[yy * 128 : (yy + 1) * 128, :]
        dp[r, 384:512] = turn(v[:, :128], cosine[yy], -sine[yy]).astype(bf16)
        dp[r, 512:] = turn(v[:, 128:], cosine[yy], -sine[yy]).astype(bf16)
    jobs[2].forward()
    net.arrive(dkv_r, s_k)
    for yy in range(4):
        r = pl.ds(yy * 128, 128)
        v = dkv[c, r, :] + dkv_r[r, :].astype(f32)
        dp[r, :128] = turn(v[:, :128], cosine[yy], -sine[yy]).astype(bf16)
        dp[r, 128:256] = turn_first_half(v[:, 128:256], cosine[yy], -sine[yy]).astype(bf16)
        dp[r, 256:384] = v[:, 256:].astype(bf16)
    for bx, bz, rows in row_blocks(dot(xnt[...], dp[:, :384]).astype(bf16)):
        wide_d[0, bx, bz] = rows[:, :256]
        narrow_d[bz, bx] = rows[:, 256:]
    for bx, bz, rows in row_blocks(dot(xnt[...], dp[:, 384:]).astype(bf16)):
        wide_d[1, bx, bz] = rows
    s_w, s_n = swap(wide_d.at[1 - c], wide_r), net.take()
    pl.when(c == 1)(lambda: net.send(narrow_d, narrow_r, s_n, partner))
    net.left_if(c == 1, narrow_d, s_n)
    a_kv = dot_nt(dp[:, :384], attention_panel(wide_w, narrow_w, 0))
    a_q = dot_nt(dp[:, 384:], attention_panel(wide_w, narrow_w, 1))
    a_s[...] = (a_kv + a_q).astype(bf16).reshape(4, 128, 768)
    i_a, i_a2 = net.take(), net.take()
    net.send(a_s.at[(y + 2) % 4], a_got.at[2], i_a, device(moved(at, "y", 4 - d)), i_a2)
    net.send(a_s.at[(y + d + 4) % 4], a_got.at[0], i_a, device(moved(at, "y", d)))
    net.left(a_got.at[0:2], i_a)
    net.arrive(wide_r, s_w)
    wide_t[...] = (wide_d[c].astype(f32) + wide_r[...].astype(f32)).astype(bf16)

    @pl.when(first)
    def _():
        net.arrive(narrow_r, s_n)
        narrow_t[...] = (narrow_d[...].astype(f32) + narrow_r[...].astype(f32)).astype(bf16)

    i_wx = to_line("x", lambda step: wide_t.at[(x + step) % 4], lambda kind: wide_1.at[kind])
    net.left(wide_1, i_wx)
    i_nz = to_line("z", lambda step: narrow_t.at[(z + step) % 4], lambda kind: narrow_1.at[kind], first)
    net.left_if(first, narrow_1, i_nz)
    jobs[1].finish(2)
    jobs[1].start(1)
    jobs[0].finish(1)
    jobs[0].start(0)

    def four(own, got):
        v = own.astype(f32)
        for kind in range(3):
            v = v + got[kind].astype(f32)
        return v

    net.arrive(a_got.at[2], i_a2)
    a_on[...] = (a_s[(y - d + 4) % 4].astype(f32) + a_got[2].astype(f32)).astype(bf16)
    net.send(a_on, a_got.at[1], i_a2, device(moved(at, "y", 4 - d)), i_a)
    net.left(a_on, i_a2)
    net.arrive(wide_1, i_wx)
    wide_2[...] = four(wide_t[x], wide_1).astype(bf16)
    i_wz = to_line("z", lambda step: wide_2.at[(z + step) % 4], lambda kind: wide_0.at[kind])
    net.left(wide_0, i_wz)

    @pl.when(first)
    def _():
        net.arrive(narrow_1, i_nz)
        narrow_2[...] = four(narrow_t[z], narrow_1).astype(bf16)

    i_nx = to_line("x", lambda step: narrow_2.at[(x + step) % 4], lambda kind: narrow_0.at[kind], first)
    net.left_if(first, narrow_0, i_nx)
    jobs[2].finish(2)
    jobs[2].start(1)
    net.arrive(a_got.at[0:2], i_a)
    a_sum[...] = (a_s[y].astype(f32) + a_got[0].astype(f32) + a_got[1].astype(f32)).astype(bf16)
    i_z = net.take()
    net.send_or_keep(a_sum, a_own, i_z, device(at, zl=c, c=zl), zl == c)
    net.left_if(zl != c, a_sum, i_z)
    jobs[1].finish(1)
    jobs[1].start(0)
    net.arrive(wide_0, i_wz)
    v = four(wide_2[z], wide_0)
    tall[0], tall[1] = v[:, :128], v[:, 128:]

    @pl.when(first)
    def _():
        net.arrive(narrow_0, i_nx)
        tall[2] = four(narrow_2[x], narrow_0)

    jobs[2].finish(1)
    jobs[2].start(0)
    net.arrive(a_own, i_z)
    v = xb[c].astype(f32)
    r1 = inverse_rms(v)
    scaled = v * r1
    a = a_own[...].astype(f32)
    input_grad[...] = por[own_rows, :] + r1 * (a - scaled * jnp.mean(a * scaled, axis=-1, keepdims=True))
    for j in jobs:
        j.finish(0)
    lowest = [j.levels[3] for j in jobs]
    for cb in range(3):
        for m in range(3):
            tall[3 + m * 3 + cb] = get_sum(lowest, m, cb)
        tall[12, pl.ds(cb * 16, 16), :] = get_sum(lowest, 3, cb)
    for s in range(8):
        for unit in range(13):
            back_s[s, pl.ds(unit * 6, 6), :] = tall[unit, pl.ds(s * 6, 6), :]
        back_s[s, pl.ds(78, 2), :] = jnp.zeros((2, 128), f32)
    back_p[...] = back_s[...].astype(bf16)
    i_b = net.take()
    slot = c * 4 + y
    for s in range(8):
        mine = jnp.logical_and(y * 2 + zl == s, zl == c)
        net.send_or_keep(back_p.at[s], back.at[slot], i_b, device(at, y=s // 2, zl=s % 2, c=zl), mine)
    net.left_if(zl == c, back_p.at[0:7], i_b)
    net.left_if(zl != c, back_p, i_b)
    net.arrive(back, i_b)
    grads[...] = back[...].astype(f32)
    net.drain()


VM = pl.BlockSpec(memory_space=pltpu.VMEM)
SEMS = 61


def layer(*args):
    f, h = f32, bf16

    def blocks(lead, rows, columns=128):
        return (lead + (rows, columns), h)

    scratch = [
        *[(a.shape, a.dtype) for a in args[:5]], (args[7].shape, args[7].dtype),
        ((8, 32, 128), f), ((8, 32, 128), h), ((8, 32, 128), h), ((8, 32, 128), f),
        ((8, 64, 128), f), ((8, 64, 128), h), ((8, 64, 128), h), ((8, 64, 128), f), ((13, 48, 128), f),
        blocks((2, 4, 4), 48, 256), blocks((4, 4), 48), *[blocks((3, 4, 4, 4), r) for r in WEIGHT_JOBS], ((2, 2, 384, 384), h),
        ((4, 128, 768), h), ((4, 128, 768), h), ((768, 512), h), ((4, 128, 128), f),
        ((4, 128, 128), f), ((2, 4, 128, 128), f), ((2, 4, 8, 128), f), ((2, 512, 384), h), ((512, 256), h),
        ((8, 512), f),
        ((192, 512), f), ((4, 128, 192), h), ((2, 2, 128, 192), h),
        ((2, 128, 768), h), ((2, 128, 768), h), ((256, 768), f), ((256, 768), f), ((256, 768), f),
        ((256, 768), h), ((768, 256), h), ((768, 256), h), ((3, 256, 512), f), ((3, 256, 512), f), ((3, 256, 512), h),
        ((256, 768), f), ((256, 768), f), ((256, 768), f), ((128, 768), f), ((256, 768), h), ((2, 384, 384), h),
        ((384, 384), h), ((4, 128, 192), h), *[blocks((3, 4, 4, 4), r) for r in GRAD_JOBS],
        ((4, 128, 192), h), ((2, 512, 384), f), ((512, 384), h), ((512, 384), h), ((256, 512), f), ((512, 640), h),
        blocks((2, 4, 4), 48, 256), blocks((4, 4), 48), blocks((4, 4), 48, 256), blocks((4, 4), 48),
        blocks((4, 4), 48, 256), blocks((4, 4), 48), blocks((3, 4), 48, 256), blocks((3, 4), 48),
        blocks((4,), 48, 256), blocks((4,), 48), blocks((3,), 48, 256), blocks((3,), 48),
        ((4, 128, 768), h), ((3, 128, 768), h), ((128, 768), h), ((128, 768), h), ((128, 768), h),
        ((8, 80, 128), f), ((8, 80, 128), h), ((8, 80, 128), h),
    ]
    for r in GRAD_JOBS:
        scratch += [blocks((3,) + (4,) * k, r) for k in (2, 1, 0)]
        scratch += [blocks((3, 3) + (4,) * k, r) for k in (2, 1, 0)]
        scratch += [blocks((3, 4, 4), r)]
    return pl.pallas_call(
        layer_body,
        out_shape=(
            jax.ShapeDtypeStruct((128, 768), bf16),
            jax.ShapeDtypeStruct((128, 768), f32),
            jax.ShapeDtypeStruct((8, 80, 128), f32),
        ),
        in_specs=[pl.BlockSpec(memory_space=pl.ANY)] * len(args),
        out_specs=(VM,) * 3,
        scratch_shapes=[pltpu.VMEM(s, t) for s, t in scratch]
        + [pltpu.SemaphoreType.DMA((SEMS,))] * 2
        + [pltpu.SemaphoreType.DMA((8,))],
        compiler_params=pltpu.CompilerParams(collective_id=0, has_side_effects=True, vmem_limit_bytes=60 << 20),
    )(*args)


def adam_step(master, gradient, moment_one, moment_two, rate_value, decay_value):
    moment_one = BETA_FIRST * moment_one + (1.0 - BETA_FIRST) * gradient
    moment_two = BETA_SECOND * moment_two + (1.0 - BETA_SECOND) * gradient * gradient
    first_hat = moment_one / (1.0 - BETA_FIRST**STEP)
    second_hat = moment_two / (1.0 - BETA_SECOND**STEP)
    updated = master - rate_value * (
        first_hat / (jnp.sqrt(second_hat) + ADAM_EPS) + decay_value * master
    )
    return (moment_one, moment_two, updated)


def owner_body(
    grads, outputs, input_grad,
    qkv, qkv_m, qkv_s, out, out_m, out_s, gu, gu_m, gu_s, dt, dt_m, dt_s, gains, gains_m, gains_s,
    outputs_o, input_grad_o,
    qkv_mo, qkv_so, qkv_o, out_mo, out_so, out_o, gu_mo, gu_so, gu_o, dt_mo, dt_so, dt_o,
    gains_mo, gains_so, gains_o,
):
    outputs_o[...] = outputs[...]
    input_grad_o[...] = input_grad[...]

    def unit(slot, u):
        return grads[slot, pl.ds(u * 6, 6), :]

    eye = lax.broadcasted_iota(jnp.int32, (6, 6), 0) == lax.broadcasted_iota(jnp.int32, (6, 6), 1)
    g_low = gains[...].astype(bf16).astype(f32)
    g_one = jnp.sum(jnp.where(eye, g_low[0:1, :], 0.0), axis=1, keepdims=True)
    g_two = jnp.sum(jnp.where(eye, g_low[1:2, :], 0.0), axis=1, keepdims=True)

    def update(refs, new, columns, gradient, rate, decay):
        w, m, s = refs
        values = adam_step(w[:, columns], gradient, m[:, columns], s[:, columns], rate, decay)
        for to, v in zip(new, values):
            to[:, columns] = v

    def low_times(w, columns, gradient):
        return jnp.sum(w[:, columns].astype(bf16).astype(f32) * gradient, axis=1, keepdims=True)

    def join(a, b):
        return jnp.concatenate([a, b], axis=1)

    rate = D ** (-0.5)
    sum_one = jnp.zeros((6, 1), f32)
    for pair in range(2):
        e, o = 2 * pair, 2 * pair + 1
        u = {(s, k): unit(s, k) for s in (e, o, 4 + e, 4 + o) for k in range(3)}
        tiles = {
            0: (u[4 + e, 0], join(u[4 + e, 1][:, :64], u[4 + o, 0][:, :64]), join(u[4 + o, 0][:, 64:], u[4 + o, 1][:, :64])),
            768: (u[e, 0], join(u[e, 1][:, :64], u[o, 0][:, :64]), join(u[o, 0][:, 64:], u[o, 1][:, :64])),
            1536: (join(u[e, 1][:, 64:], u[e, 2][:, :64]), join(u[e, 2][:, 64:], u[o, 1][:, 64:]), u[o, 2]),
        }
        for first, three in tiles.items():
            for k, t in enumerate(three):
                columns = pl.ds(first + pair * 384 + k * 128, 128)
                sum_one = sum_one + low_times(qkv, columns, t)
                update((qkv, qkv_m, qkv_s), (qkv_mo, qkv_so, qkv_o), columns, t * g_one, rate, WEIGHT_DECAY)
    sum_two = jnp.zeros((6, 1), f32)
    for slot in range(8):
        for cb in range(3):
            f = slot * 384 + cb * 128
            for half in range(2):
                columns = pl.ds(half * 3072 + f, 128)
                t = unit(slot, 3 + half * 3 + cb)
                sum_two = sum_two + low_times(gu, columns, t)
                update((gu, gu_m, gu_s), (gu_mo, gu_so, gu_o), columns, t * g_two, rate, WEIGHT_DECAY)
            update(
                (dt, dt_m, dt_s), (dt_mo, dt_so, dt_o), pl.ds(f, 128), unit(slot, 9 + cb), FF ** (-0.5), WEIGHT_DECAY
            )
        if slot % 4 < 3:
            update(
                (out, out_m, out_s), (out_mo, out_so, out_o), pl.ds((slot // 4) * 384 + (slot % 4) * 128, 128),
                unit(slot, 12), (H * HD * 32 // LEN) ** (-0.5), WEIGHT_DECAY,
            )
    rows = [jnp.sum(jnp.where(eye, v, 0.0), axis=0, keepdims=True) for v in (sum_one, sum_two)]
    values = adam_step(gains[...], jnp.concatenate(rows, axis=0), gains_m[...], gains_s[...], GAIN_RATE, 0.0)
    for to, v in zip((gains_mo, gains_so, gains_o), values):
        to[...] = v


def owners_step(*args):
    shapes = [(args[1].shape, bf16), (args[2].shape, f32)]
    for first in range(3, 18, 3):
        shapes += [(args[first].shape, f32)] * 3
    return pl.pallas_call(
        owner_body,
        out_shape=tuple(jax.ShapeDtypeStruct(s, t) for s, t in shapes),
        in_specs=[VM] * len(args),
        out_specs=(VM,) * len(shapes),
    )(*args)


def body(
    inputs, positions, output_grad,
    qkv_weight, qkv_first, qkv_second, out_weight, out_first, out_second,
    gate_up_weight, gate_up_first, gate_up_second, down_weight, down_first, down_second,
    norm_gains, gains_first, gains_second,
):
    outputs, input_grad, grads = layer(
        qkv_weight, out_weight, gate_up_weight, down_weight.T, norm_gains,
        inputs.reshape(128, D), output_grad.reshape(128, D), positions,
    )
    new = owners_step(
        grads, outputs, input_grad,
        qkv_weight, qkv_first, qkv_second, out_weight, out_first, out_second,
        gate_up_weight, gate_up_first, gate_up_second, down_weight.T, down_first.T, down_second.T,
        norm_gains, gains_first, gains_second,
    )
    return (
        new[0].reshape(1, 128, D), new[1].reshape(1, 128, D), *new[2:11],
        *(v.T for v in new[11:14]), *new[14:],
    )


def solution(mesh):
    token = P("dp", "ctx", None)
    rows, columns = P(("dp", "ctx"), None), P(None, ("dp", "ctx"))
    return jax.shard_map(
        body,
        mesh=mesh,
        in_specs=(token, P("dp", "ctx"), token) + (rows,) * 9 + (columns,) * 6,
        out_specs=(token, token) + (rows,) * 9 + (columns,) * 6,
        check_vma=False,
    )
```
